32 devices in a mesh: packs: 4 (over x, core), seq: 8 (over z, y).
Axes of the slice: x: 2, y: 2, z: 4, core: 2. Of those that a mesh axis runs over, the one named last changes fastest.
Arguments:
- queries: bfloat16 [4096, 8192], P(('packs', 'seq')), parts along dimension 0, may hold values from -12 to 12
- keys: bfloat16 [4096, 1024], P(('packs', 'seq')), parts along dimension 0, may hold values from -6 to 6
- values: bfloat16 [4096, 1024], P(('packs', 'seq')), parts along dimension 0, may hold values from -6 to 6
- outputs: bfloat16 [4096, 8192], P(('packs', 'seq')), parts along dimension 0, may hold values from -6 to 6
- grad_out: bfloat16 [4096, 8192], P(('packs', 'seq')), parts along dimension 0, may hold values from -4 to 4
- lse_saved: float32 [4096, 64], P(('packs', 'seq')), parts along dimension 0, may hold values from -40 to 40, as said below
- doc_lengths: int32 [32], P('packs'), parts along dimension 0, may hold values from 1 to 512, as said below
Outputs:
- grad_queries: bfloat16 [4096, 8192], P(('packs', 'seq')), parts along dimension 0
- grad_keys: bfloat16 [4096, 1024], P(('packs', 'seq')), parts along dimension 0
- grad_values: bfloat16 [4096, 1024], P(('packs', 'seq')), parts along dimension 0
The draws below stay inside these ranges and needn't reach their ends.
There are 4 independent parts, one for each index of `packs`. The reference program is written for one: setup_inputs(seed, part) draws one part's arguments, and reference() takes and returns one part's arrays. A program takes and returns all parts, laid end to end along the dimension named above; each array names one. Nothing has to cross between parts.
Inputs may be any that keep to these rules, and one draw needn't show every extreme that they name: `doc_lengths`: positive lengths summing to 1024; one document has exactly 512 tokens. lse_saved is the log-sum-exp over visible keys of the scores of queries and keys as defined in the reference program, for every row and head.
All inputs are finite; a program needn't handle non-finite values.
Results may differ from the reference program's by a relative error of at most 0.0049.
Values may be sent and summed in bfloat16 or wider, within the bound.
No kernel may reach another device: no remote copies, remote signals or barrier semaphores. Data moves between devices by JAX's collectives and lax.ppermute only.
A program may use at most 64 MiB of HBM per device.

```python
import jax
import jax.numpy as jnp
from jax import lax

HEADS = 64
KVH = 8
HDIM = 128
DOCS = 8
TOKENS = 1024
MOST = 512


def draw_doc_lengths(key, part):
    rest = TOKENS - MOST
    weights = jax.random.randint(jax.random.fold_in(key, 11), (DOCS - 1,), 1, 9).astype(jnp.int32)
    shares = weights * rest // jnp.sum(weights)
    shares = shares.at[0].add(rest - jnp.sum(shares))
    lengths = jnp.concatenate([jnp.full((1,), MOST, dtype=jnp.int32), shares.astype(jnp.int32)])
    offset = jax.random.randint(jax.random.fold_in(key, 12), (), 0, DOCS)
    return jnp.roll(lengths, offset).astype(jnp.int32)


def raw_queries(key):
    drawn = jnp.clip(jax.random.normal(jax.random.fold_in(key, 21), (TOKENS, HEADS * HDIM), jnp.float32), -6.0, 6.0)
    return drawn


def raw_keys(key):
    return jnp.clip(jax.random.normal(jax.random.fold_in(key, 23), (TOKENS, KVH * HDIM), jnp.float32), -6.0, 6.0)


def draw_queries(key, part):
    return raw_queries(key).astype(jnp.bfloat16)


def draw_keys(key, part):
    return raw_keys(key).astype(jnp.bfloat16)


def draw_lse_saved(key, part):
    total = TOKENS
    scale = 1.0 / HDIM ** 0.5
    group = HEADS // KVH
    query_heads = raw_queries(key).astype(jnp.bfloat16).astype(jnp.float32).reshape(total, HEADS, HDIM)
    key_heads = raw_keys(key).astype(jnp.bfloat16).astype(jnp.float32).reshape(total, KVH, HDIM)
    lengths = draw_doc_lengths(key, part)
    boundary = jnp.cumsum(lengths)
    position = jnp.arange(total, dtype=jnp.int32)
    segment = jnp.sum((position[:, None] >= boundary[None, :]).astype(jnp.int32), axis=1)
    visible = (position[None, :] <= position[:, None]) & (segment[None, :] == segment[:, None])

    def one_head(head):
        query_one = lax.dynamic_index_in_dim(query_heads, head, 1, keepdims=False)
        key_one = lax.dynamic_index_in_dim(key_heads, head // group, 1, keepdims=False)
        scores = jnp.dot(query_one, key_one.T, precision=lax.Precision.HIGHEST) * scale
        return jax.nn.logsumexp(jnp.where(visible, scores, -jnp.inf), axis=1)
    return lax.map(one_head, jnp.arange(HEADS, dtype=jnp.int32)).T.astype(jnp.float32)


def shard_levels(own_key, shape, pieces, low, top_value):
    factor_of, own = 1.0, jax.random.fold_in(own_key, 6)
    for dim, parts in pieces:
        draws = jnp.exp(jax.random.uniform(jax.random.fold_in(own, dim), (parts,), jnp.float32, low / len(pieces), top_value / len(pieces)))
        factor_of = factor_of * jnp.repeat(draws, shape[dim] // parts).reshape([-1 if axis == dim else 1 for axis in range(len(shape))])
    return factor_of


def gaussian(stream_key, extent, spread, bound, pieces=(), kind=jnp.bfloat16):
    entries = jax.random.normal(stream_key, extent, jnp.float32) * spread
    if len(pieces) > 0:
        entries = shard_levels(stream_key, extent, pieces, -0.22, 0.18) * entries
    return jnp.clip(entries, min=-bound, max=bound).astype(kind)


def setup_inputs(seed: int = 0, part: int = 0) -> dict:
    seeds = jax.random.split(jax.random.key(seed), 8)
    own_keys = jax.random.split(jax.random.fold_in(seeds[7], part), 8)
    return {
        "queries": draw_queries(jax.random.fold_in(jax.random.fold_in(seeds[7], part), 71), part),
        "keys": draw_keys(jax.random.fold_in(jax.random.fold_in(seeds[7], part), 71), part),
        "values": gaussian(own_keys[2], (TOKENS, KVH * HDIM), 1.0, 6.0, ((0, 8),)),
        "outputs": gaussian(own_keys[3], (TOKENS, HEADS * HDIM), 1.0, 6.0, ((0, 8),)),
        "grad_out": gaussian(own_keys[4], (TOKENS, HEADS * HDIM), 0.3, 4.0, ((0, 8),)),
        "lse_saved": draw_lse_saved(jax.random.fold_in(jax.random.fold_in(seeds[7], part), 71), part),
        "doc_lengths": draw_doc_lengths(jax.random.fold_in(jax.random.fold_in(seeds[7], part), 71), part),
    }


def segment_ids(doc_lengths, total):
    boundary = jnp.cumsum(doc_lengths)
    position = jnp.arange(total, dtype=jnp.int32)
    return jnp.sum((position[:, None] >= boundary[None, :]).astype(jnp.int32), axis=1)


def reference(queries, keys, values, outputs, grad_out, lse_saved, doc_lengths):
    total = TOKENS
    scale = 1.0 / (HDIM ** 0.5)
    group = HEADS // KVH
    segment = segment_ids(doc_lengths, total)
    position = jnp.arange(total, dtype=jnp.int32)
    visible = (position[None, :] <= position[:, None]) & (segment[None, :] == segment[:, None])
    query_heads = queries.reshape(total, HEADS, HDIM)
    gout_heads = grad_out.reshape(total, HEADS, HDIM)
    out_heads = outputs.reshape(total, HEADS, HDIM)
    key_heads = keys.reshape(total, KVH, HDIM)
    value_heads = values.reshape(total, KVH, HDIM)
    delta = jnp.sum(out_heads.astype(jnp.float32) * gout_heads.astype(jnp.float32), axis=2)

    def one_head(head):
        kv_index = head // group
        query_one = lax.dynamic_index_in_dim(query_heads, head, 1, keepdims=False)
        gout_one = lax.dynamic_index_in_dim(gout_heads, head, 1, keepdims=False)
        key_one = lax.dynamic_index_in_dim(key_heads, kv_index, 1, keepdims=False)
        value_one = lax.dynamic_index_in_dim(value_heads, kv_index, 1, keepdims=False)
        lse_one = lax.dynamic_index_in_dim(lse_saved, head, 1, keepdims=False)
        delta_one = lax.dynamic_index_in_dim(delta, head, 1, keepdims=False)
        scores = jnp.dot(query_one, key_one.T, preferred_element_type=jnp.float32) * scale
        attn_prob = jnp.where(visible, jnp.exp(scores - lse_one[:, None]), 0.0)
        grad_prob = jnp.dot(gout_one, value_one.T, preferred_element_type=jnp.float32)
        grad_score = (attn_prob * (grad_prob - delta_one[:, None])).astype(jnp.bfloat16)
        prob_half = attn_prob.astype(jnp.bfloat16)
        grad_query = (jnp.dot(grad_score, key_one, preferred_element_type=jnp.float32) * scale).astype(jnp.bfloat16)
        grad_key = jnp.dot(grad_score.T, query_one, preferred_element_type=jnp.float32) * scale
        grad_value = jnp.dot(prob_half.T, gout_one, preferred_element_type=jnp.float32)
        return grad_query, grad_key, grad_value

    grad_q_all, grad_k_all, grad_v_all = lax.map(one_head, jnp.arange(HEADS, dtype=jnp.int32))
    grad_queries = jnp.transpose(grad_q_all, (1, 0, 2)).reshape(total, HEADS * HDIM)
    grad_keys = jnp.sum(grad_k_all.reshape(KVH, group, total, HDIM), axis=1)
    grad_values = jnp.sum(grad_v_all.reshape(KVH, group, total, HDIM), axis=1)
    grad_keys = jnp.transpose(grad_keys, (1, 0, 2)).reshape(total, KVH * HDIM).astype(jnp.bfloat16)
    grad_values = jnp.transpose(grad_values, (1, 0, 2)).reshape(total, KVH * HDIM).astype(jnp.bfloat16)
    return grad_queries, grad_keys, grad_values
```

```python
import functools

import jax
import jax.numpy as jnp
from jax import lax
from jax.experimental import pallas as pl
from jax.experimental.pallas import tpu as pltpu
from jax.sharding import PartitionSpec as P

HEADS = 64
KVH = 8
HDIM = 128
GROUP = HEADS // KVH
CHUNKS = 2
LOG2E = 1.4426950408889634


def contract_last(first, second):
    return lax.dot_general(
        first, second, (((1,), (1,)), ((), ())), preferred_element_type=jnp.float32
    )


def contract_first(first, second):
    return lax.dot_general(
        first, second, (((0,), (0,)), ((), ())), preferred_element_type=jnp.float32
    )


def head_rows(block):
    return jnp.concatenate(
        [block[:, h * HDIM : (h + 1) * HDIM] for h in range(GROUP)], axis=0
    )


def delta_kernel(out_ref, gout_ref, delta_ref):
    rows = out_ref.shape[0]
    product = head_rows(out_ref[...]).astype(jnp.float32) * head_rows(gout_ref[...]).astype(
        jnp.float32
    )
    high = product.astype(jnp.bfloat16)
    low = (product - high.astype(jnp.float32)).astype(jnp.bfloat16)
    ones = jnp.ones((GROUP, HDIM), jnp.bfloat16)
    sums = contract_last(ones, high) + contract_last(ones, low)
    head = lax.broadcasted_iota(jnp.int32, (GROUP, rows), 0)
    total = jnp.zeros((GROUP, rows), jnp.float32)
    for h in range(GROUP):
        total = jnp.where(head == h, sums[:, h * rows : (h + 1) * rows], total)
    delta_ref[...] = total


def delta_rows(outputs, grad_out):
    rows = outputs.shape[0]
    return pl.pallas_call(
        delta_kernel,
        grid=(KVH,),
        in_specs=[pl.BlockSpec((rows, GROUP * HDIM), lambda g: (0, g))] * 2,
        out_specs=pl.BlockSpec((GROUP, rows), lambda g: (g, 0)),
        out_shape=jax.ShapeDtypeStruct((HEADS, rows), jnp.float32),
        cost_estimate=pl.CostEstimate(
            flops=2 * rows * HEADS * HDIM, bytes_accessed=4 * rows * HEADS * HDIM, transcendentals=0
        ),
        name="delta",
    )(outputs, grad_out)


def slot_bases(me, rows, hops):
    side = lax.rem(me, 2)
    pair = me // 2
    bases = [(me - 2 * hop) * rows for hop in range(hops + 1)]
    bases += [(2 * (pair - hop) + 1 - side) * rows for hop in range(1, hops)]
    bases.append(jnp.where(side == 1, me - 1, me - 2 * hops + 1) * rows)
    return bases


def attend_kernel(hops, docs, aliased, meta, q_ref, gout_ref, lse_ref, delta_ref, k_ref, v_ref, *refs):
    slots = 2 * hops + 1
    moved = refs[: 2 * hops + 1]
    refs = refs[2 * hops + 1 + aliased :]
    gq_ref = refs[0]
    parts = refs[1 : 1 + slots]
    k_all, v_all, bias, prob, score = refs[1 + slots :]
    rows = q_ref.shape[0]
    scale = 1.0 / HDIM**0.5
    me = meta[0]
    side = lax.rem(me, 2)

    @pl.when(pl.program_id(0) == 0)
    def _():
        token = lax.broadcasted_iota(jnp.int32, (1, rows), 1) + me * rows
        begin = jnp.zeros((1, rows), jnp.int32)
        edge = jnp.int32(0)
        for doc in range(docs):
            edge = edge + meta[1 + doc]
            begin = jnp.where(token >= edge, edge, begin)
        row = lax.broadcasted_iota(jnp.int32, (rows, rows), 0)
        for slot, base in enumerate(slot_bases(me, rows, hops)):
            key = row + base
            visible = (key <= token) & (key >= begin)
            bias[slot * rows : (slot + 1) * rows, :] = jnp.where(visible, 0.0, -1e30)

    k_all[0:rows, :] = k_ref[...]
    v_all[0:rows, :] = v_ref[...]
    for slot in range(1, slots - 1):
        k_all[slot * rows : (slot + 1) * rows, :] = moved[slot - 1][0]
        v_all[slot * rows : (slot + 1) * rows, :] = moved[slot - 1][1]

    @pl.when(side == 1)
    def _():
        k_all[(slots - 1) * rows :, :] = moved[slots - 2][0]
        v_all[(slots - 1) * rows :, :] = moved[slots - 2][1]

    @pl.when(side == 0)
    def _():
        k_all[(slots - 1) * rows :, :] = moved[slots - 1][0]
        v_all[(slots - 1) * rows :, :] = moved[slots - 1][1]

    queries = head_rows(q_ref[...])
    gout = head_rows(gout_ref[...])
    keys = k_all[...]
    values = v_all[...]
    hidden = bias[...]
    hidden = jnp.concatenate([hidden, hidden], axis=1)
    for two in range(GROUP // 2):
        at = slice(2 * two * rows, (2 * two + 2) * rows)
        lse = jnp.concatenate(
            [lse_ref[2 * two : 2 * two + 1, :], lse_ref[2 * two + 1 : 2 * two + 2, :]], axis=1
        )
        delta = jnp.concatenate(
            [delta_ref[2 * two : 2 * two + 1, :], delta_ref[2 * two + 1 : 2 * two + 2, :]], axis=1
        )
        raw = contract_last(keys, queries[at])
        attn = jnp.exp2(raw * (scale * LOG2E) - lse * LOG2E + hidden)
        grad = contract_last(values, gout[at])
        prob[:, at] = attn.astype(jnp.bfloat16)
        score[:, at] = (attn * (grad - delta)).astype(jnp.bfloat16)
    scores = score[...]
    grad_k = jnp.dot(scores, queries, preferred_element_type=jnp.float32) * scale
    grad_v = jnp.dot(prob[...], gout, preferred_element_type=jnp.float32)
    for slot in range(slots):
        at = slice(slot * rows, (slot + 1) * rows)
        parts[slot][0] = grad_k[at].astype(parts[slot].dtype)
        parts[slot][1] = grad_v[at].astype(parts[slot].dtype)
    grad_q = contract_first(keys, scores) * scale
    for h in range(GROUP):
        gq_ref[:, h * HDIM : (h + 1) * HDIM] = (
            grad_q[:, h * rows : (h + 1) * rows].T.astype(jnp.bfloat16)
        )


def attend(meta, queries, grad_out, lse, delta, keys, values, moved, grad_q, chunk, per, hops):
    rows = queries.shape[0]
    slots = 2 * hops + 1
    wide = pl.BlockSpec((rows, GROUP * HDIM), lambda g, m: (0, chunk * per + g))
    stat = pl.BlockSpec((GROUP, rows), lambda g, m: (chunk * per + g, 0))
    own = pl.BlockSpec((rows, HDIM), lambda g, m: (0, chunk * per + g))
    both = pl.BlockSpec((2, rows, HDIM), lambda g, m: (0, 0, g))
    aliased = 0 if grad_q is None else 1
    in_specs = [wide, wide, stat, stat, own, own] + [both] * len(moved)
    operands = [meta, queries, grad_out, lse, delta, keys, values] + moved
    aliases = {}
    if aliased:
        in_specs.append(pl.BlockSpec(memory_space=pl.ANY))
        operands.append(grad_q)
        aliases = {len(operands) - 1: 0}
    kinds = [jnp.float32] * (hops + 1) + [jnp.bfloat16] * hops
    out_shape = [jax.ShapeDtypeStruct(queries.shape, jnp.bfloat16)] + [
        jax.ShapeDtypeStruct((2, rows, per * HDIM), kind) for kind in kinds
    ]
    pairs = slots * rows * rows * GROUP * per
    return pl.pallas_call(
        functools.partial(attend_kernel, hops, meta.shape[0] - 1, aliased),
        grid_spec=pltpu.PrefetchScalarGridSpec(
            num_scalar_prefetch=1,
            grid=(per,),
            in_specs=in_specs,
            out_specs=[wide] + [both] * slots,
            scratch_shapes=[
                pltpu.VMEM((slots * rows, HDIM), jnp.bfloat16),
                pltpu.VMEM((slots * rows, HDIM), jnp.bfloat16),
                pltpu.VMEM((slots * rows, rows), jnp.float32),
                pltpu.VMEM((slots * rows, GROUP * rows), jnp.bfloat16),
                pltpu.VMEM((slots * rows, GROUP * rows), jnp.bfloat16),
            ],
        ),
        out_shape=out_shape,
        input_output_aliases=aliases,
        compiler_params=pltpu.CompilerParams(vmem_limit_bytes=40 * 1024 * 1024),
        cost_estimate=pl.CostEstimate(
            flops=10 * pairs * HDIM,
            bytes_accessed=per * rows * HDIM * 2 * (3 * GROUP + 6 * slots),
            transcendentals=pairs,
        ),
        name="attend",
    )(*operands)


def shards(queries, keys, values, outputs, grad_out, lse_saved, doc_lengths):
    seq = lax.axis_size("seq")
    me = lax.axis_index("seq")
    side = lax.rem(me, 2)
    hops = seq // 4
    per = KVH // CHUNKS
    width = per * HDIM
    onward = [(s, s + 2) for s in range(seq - 2)]
    back = [(s + 2, s) for s in range(seq - 2)]
    swap = [(s, s + 1 - 2 * (s % 2)) for s in range(seq)]
    to_odd = [(s, s + 1) for s in range(0, seq, 2)]
    to_even = [(s + 1, s) for s in range(0, seq, 2)]

    def send(array, pairs):
        return lax.ppermute(array, "seq", pairs)

    meta = jnp.concatenate([me.astype(jnp.int32).reshape(1), doc_lengths])
    arrived = []
    for chunk in range(CHUNKS):
        at = slice(chunk * width, (chunk + 1) * width)
        own = jnp.stack([keys[:, at], values[:, at]])
        same = [own]
        for hop in range(hops):
            same.append(send(same[-1], onward))
        other = [send(same[hop], swap) for hop in range(1, hops)]
        edge = [send(own, to_odd), send(same[hops], to_even)]
        arrived.append(same[1:] + other + edge)
    delta = delta_rows(outputs, grad_out)
    lse = lse_saved.T

    grad_q = None
    sums = []
    for chunk in range(CHUNKS):
        grad_q, *parts = attend(
            meta, queries, grad_out, lse, delta, keys, values, arrived[chunk], grad_q, chunk, per, hops
        )
        same, other, edge = parts[: hops + 1], parts[hops + 1 : 2 * hops], parts[2 * hops]
        other = [send(part, swap) for part in other]
        edge = send(edge, swap).astype(jnp.float32)
        total = same[hops] + jnp.where(side == 1, edge, 0.0)
        for hop in range(hops - 1, 0, -1):
            far = send(total.astype(jnp.bfloat16), back)
            total = same[hop] + other[hop - 1].astype(jnp.float32) + far.astype(jnp.float32)
        far = send(total.astype(jnp.bfloat16), back)
        total = same[0] + jnp.where(side == 0, edge, 0.0) + far.astype(jnp.float32)
        sums.append(total.astype(jnp.bfloat16))
    grad_keys = jnp.concatenate([total[0] for total in sums], axis=1)
    grad_values = jnp.concatenate([total[1] for total in sums], axis=1)
    return (grad_q, grad_keys, grad_values)


def solution(mesh):
    rows = P(("packs", "seq"), None)
    return jax.shard_map(
        shards,
        mesh=mesh,
        in_specs=(rows, rows, rows, rows, rows, rows, P("packs")),
        out_specs=(rows, rows, rows),
        check_vma=False,
    )
```

```python
import functools

import jax
import jax.numpy as jnp
from jax import lax
from jax.experimental import pallas as pl
from jax.experimental.pallas import tpu as pltpu
from jax.sharding import PartitionSpec as P

HEADS = 64
KVH = 8
HDIM = 128
GROUP = HEADS // KVH
CHUNKS = 2
LOG2E = 1.4426950408889634
VMEM = 60 * 1024 * 1024


def contract_last(first, second):
    return lax.dot_general(
        first, second, (((1,), (1,)), ((), ())), preferred_element_type=jnp.float32
    )


def contract_first(first, second):
    return lax.dot_general(
        first, second, (((0,), (0,)), ((), ())), preferred_element_type=jnp.float32
    )


def head_rows(block):
    return jnp.concatenate(
        [block[:, h * HDIM : (h + 1) * HDIM] for h in range(GROUP)], axis=0
    )


def stats_kernel(out_ref, gout_ref, lse_ref, stats_ref, sums):
    step = pl.program_id(0)
    product = out_ref[...].astype(jnp.float32) * gout_ref[...].astype(jnp.float32)
    high = product.astype(jnp.bfloat16)
    low = (product - high.astype(jnp.float32)).astype(jnp.bfloat16)
    depth = product.shape[1]
    row = lax.broadcasted_iota(jnp.int32, (depth, HDIM), 0)
    head = lax.broadcasted_iota(jnp.int32, (depth, HDIM), 1)
    ones = jnp.where(row // HDIM + step * GROUP == head, 1.0, 0.0).astype(jnp.bfloat16)
    total = jnp.dot(high, ones, preferred_element_type=jnp.float32) + jnp.dot(
        low, ones, preferred_element_type=jnp.float32
    )

    @pl.when(step == 0)
    def _():
        sums[...] = total

    @pl.when(step > 0)
    def _():
        sums[...] += total

    @pl.when(step == pl.num_programs(0) - 1)
    def _():
        both = jnp.concatenate([sums[:, :HEADS], lse_ref[...]], axis=1)
        stats_ref[...] = both.T


def stat_rows(outputs, grad_out, lse_saved):
    rows = outputs.shape[0]
    return pl.pallas_call(
        stats_kernel,
        grid=(KVH,),
        in_specs=[pl.BlockSpec((rows, GROUP * HDIM), lambda g: (0, g))] * 2
        + [pl.BlockSpec((rows, HEADS), lambda g: (0, 0))],
        out_specs=pl.BlockSpec((2 * HEADS, rows), lambda g: (0, 0)),
        out_shape=jax.ShapeDtypeStruct((2 * HEADS, rows), jnp.float32),
        scratch_shapes=[pltpu.VMEM((rows, HDIM), jnp.float32)],
        compiler_params=pltpu.CompilerParams(vmem_limit_bytes=VMEM),
        cost_estimate=pl.CostEstimate(
            flops=4 * rows * HEADS * HDIM * HDIM,
            bytes_accessed=4 * rows * HEADS * HDIM,
            transcendentals=0,
        ),
        name="stats",
    )(outputs, grad_out, lse_saved)


def slot_shards(me, hops):
    side = lax.rem(me, 2)
    found = [me - 2 * hop for hop in range(hops + 1)]
    found += [me - 2 * hop + 1 - 2 * side for hop in range(1, hops)]
    found.append(jnp.where(side == 1, me - 1, me - 2 * hops + 1))
    return found


def attend_kernel(hops, docs, aliased, meta, q_ref, gout_ref, lse_ref, delta_ref, k_ref, v_ref, *refs):
    slots = 2 * hops + 1
    moved = refs[: slots - 1]
    refs = refs[slots - 1 + aliased :]
    gq_ref = refs[0]
    parts = refs[1 : 1 + slots]
    k_all, v_all, bias, prob, score = refs[1 + slots :]
    rows = q_ref.shape[0]
    scale = 1.0 / HDIM**0.5
    me = meta[0]

    @pl.when(pl.program_id(0) == 0)
    def _():
        token = lax.broadcasted_iota(jnp.int32, (1, rows), 1) + me * rows
        begin = jnp.zeros((1, rows), jnp.int32)
        edge = jnp.int32(0)
        for doc in range(docs):
            edge = edge + meta[1 + doc]
            begin = jnp.where(token >= edge, edge, begin)
        row = lax.broadcasted_iota(jnp.int32, (rows, rows), 0)
        for slot, shard in enumerate(slot_shards(me, hops)):
            key = row + shard * rows
            visible = (key <= token) & (key >= begin)
            bias[slot * rows : (slot + 1) * rows, :] = jnp.where(visible, 0.0, -1e30)

    k_all[0:rows, :] = k_ref[...]
    v_all[0:rows, :] = v_ref[...]
    for slot in range(1, slots):
        k_all[slot * rows : (slot + 1) * rows, :] = moved[slot - 1][0, 0]
        v_all[slot * rows : (slot + 1) * rows, :] = moved[slot - 1][0, 1]

    queries = head_rows(q_ref[...])
    gout = head_rows(gout_ref[...])
    keys = k_all[...]
    values = v_all[...]
    hidden = bias[...]
    hidden = jnp.concatenate([hidden, hidden], axis=1)
    for two in range(GROUP // 2):
        at = slice(2 * two * rows, (2 * two + 2) * rows)
        lse = jnp.concatenate(
            [lse_ref[2 * two : 2 * two + 1, :], lse_ref[2 * two + 1 : 2 * two + 2, :]], axis=1
        )
        delta = jnp.concatenate(
            [delta_ref[2 * two : 2 * two + 1, :], delta_ref[2 * two + 1 : 2 * two + 2, :]], axis=1
        )
        raw = contract_last(keys, queries[at])
        attn = jnp.exp2(raw * (scale * LOG2E) - lse * LOG2E + hidden)
        grad = contract_last(values, gout[at])
        prob[:, at] = attn.astype(jnp.bfloat16)
        score[:, at] = (attn * (grad - delta)).astype(jnp.bfloat16)
    scores = score[...]
    grad_k = jnp.dot(scores, queries, preferred_element_type=jnp.float32) * scale
    grad_v = jnp.dot(prob[...], gout, preferred_element_type=jnp.float32)
    for slot in range(slots):
        at = slice(slot * rows, (slot + 1) * rows)
        parts[slot][0] = grad_k[at].astype(parts[slot].dtype)
        parts[slot][1] = grad_v[at].astype(parts[slot].dtype)
    grad_q = contract_first(keys, scores) * scale
    for h in range(GROUP):
        gq_ref[:, h * HDIM : (h + 1) * HDIM] = (
            grad_q[:, h * rows : (h + 1) * rows].T.astype(jnp.bfloat16)
        )


def attend(meta, queries, grad_out, stats, keys, values, gathered, grad_q, chunk, per, hops):
    rows = queries.shape[0]
    slots = 2 * hops + 1
    wide = pl.BlockSpec((rows, GROUP * HDIM), lambda g, m: (0, chunk * per + g))
    delta = pl.BlockSpec((GROUP, rows), lambda g, m: (chunk * per + g, 0))
    lse = pl.BlockSpec((GROUP, rows), lambda g, m: (KVH + chunk * per + g, 0))
    own = pl.BlockSpec((rows, HDIM), lambda g, m: (0, chunk * per + g))
    both = pl.BlockSpec((2, rows, HDIM), lambda g, m: (0, 0, g))

    def moved(slot):
        return pl.BlockSpec(
            (1, 2, rows, HDIM),
            lambda g, m: (jnp.maximum(slot_shards(m[0], hops)[slot], 0), 0, 0, g),
        )

    aliased = 0 if grad_q is None else 1
    in_specs = [wide, wide, lse, delta, own, own] + [moved(slot) for slot in range(1, slots)]
    operands = [meta, queries, grad_out, stats, stats, keys, values] + [gathered] * (slots - 1)
    aliases = {}
    if aliased:
        in_specs.append(pl.BlockSpec(memory_space=pl.ANY))
        operands.append(grad_q)
        aliases = {len(operands) - 1: 0}
    kinds = [jnp.float32] * (hops + 1) + [jnp.bfloat16] * hops
    out_shape = [jax.ShapeDtypeStruct(queries.shape, jnp.bfloat16)] + [
        jax.ShapeDtypeStruct((2, rows, per * HDIM), kind) for kind in kinds
    ]
    pairs = slots * rows * rows * GROUP * per
    return pl.pallas_call(
        functools.partial(attend_kernel, hops, meta.shape[0] - 1, aliased),
        grid_spec=pltpu.PrefetchScalarGridSpec(
            num_scalar_prefetch=1,
            grid=(per,),
            in_specs=in_specs,
            out_specs=[wide] + [both] * slots,
            scratch_shapes=[
                pltpu.VMEM((slots * rows, HDIM), jnp.bfloat16),
                pltpu.VMEM((slots * rows, HDIM), jnp.bfloat16),
                pltpu.VMEM((slots * rows, rows), jnp.float32),
                pltpu.VMEM((slots * rows, GROUP * rows), jnp.bfloat16),
                pltpu.VMEM((slots * rows, GROUP * rows), jnp.bfloat16),
            ],
        ),
        out_shape=out_shape,
        input_output_aliases=aliases,
        compiler_params=pltpu.CompilerParams(vmem_limit_bytes=VMEM),
        cost_estimate=pl.CostEstimate(
            flops=10 * pairs * HDIM,
            bytes_accessed=per * rows * HDIM * 2 * (3 * GROUP + 6 * slots),
            transcendentals=pairs,
        ),
        name="attend",
    )(*operands)


def shards(queries, keys, values, outputs, grad_out, lse_saved, doc_lengths):
    seq = lax.axis_size("seq")
    me = lax.axis_index("seq")
    side = lax.rem(me, 2)
    hops = seq // 4
    per = KVH // CHUNKS
    width = per * HDIM
    back = [(s + 2, s) for s in range(seq - 2)]
    swap = [(s, s + 1 - 2 * (s % 2)) for s in range(seq)]

    def send(array, pairs):
        return lax.ppermute(array, "seq", pairs)

    meta = jnp.concatenate([me.astype(jnp.int32).reshape(1), doc_lengths])
    gathered = []
    for chunk in range(CHUNKS):
        at = slice(chunk * width, (chunk + 1) * width)
        gathered.append(lax.all_gather(jnp.stack([keys[:, at], values[:, at]]), "seq"))
    stats = stat_rows(outputs, grad_out, lse_saved)

    grad_q = None
    sums = []
    for chunk in range(CHUNKS):
        grad_q, *parts = attend(
            meta, queries, grad_out, stats, keys, values, gathered[chunk], grad_q, chunk, per, hops
        )
        same, other, edge = parts[: hops + 1], parts[hops + 1 : 2 * hops], parts[2 * hops]
        other = [send(part, swap) for part in other]
        edge = send(edge, swap).astype(jnp.float32)
        total = same[hops] + jnp.where(side == 1, edge, 0.0)
        for hop in range(hops - 1, 0, -1):
            far = send(total.astype(jnp.bfloat16), back)
            total = same[hop] + other[hop - 1].astype(jnp.float32) + far.astype(jnp.float32)
        far = send(total.astype(jnp.bfloat16), back)
        total = same[0] + jnp.where(side == 0, edge, 0.0) + far.astype(jnp.float32)
        sums.append(total.astype(jnp.bfloat16))
    grad_keys = jnp.concatenate([total[0] for total in sums], axis=1)
    grad_values = jnp.concatenate([total[1] for total in sums], axis=1)
    return (grad_q, grad_keys, grad_values)


def solution(mesh):
    rows = P(("packs", "seq"), None)
    return jax.shard_map(
        shards,
        mesh=mesh,
        in_specs=(rows, rows, rows, rows, rows, rows, P("packs")),
        out_specs=(rows, rows, rows),
        check_vma=False,
    )
```

```python
import functools

import jax
import jax.numpy as jnp
from jax import lax
from jax.experimental import pallas as pl
from jax.experimental.pallas import tpu as pltpu
from jax.sharding import PartitionSpec as P

HEADS = 64
KVH = 8
HDIM = 128
GROUP = HEADS // KVH
CHUNKS = (4, 4)
LOG2E = 1.4426950408889634
VMEM = 60 * 1024 * 1024


def contract_last(first, second):
    return lax.dot_general(
        first, second, (((1,), (1,)), ((), ())), preferred_element_type=jnp.float32
    )


def contract_first(first, second):
    return lax.dot_general(
        first, second, (((0,), (0,)), ((), ())), preferred_element_type=jnp.float32
    )


def head_rows(block):
    return jnp.concatenate(
        [block[:, h * HDIM : (h + 1) * HDIM] for h in range(GROUP)], axis=0
    )


def stats_kernel(steps, out_ref, gout_ref, lse_ref, stats_ref, sums):
    step = pl.program_id(0)
    rows = out_ref.shape[0]
    wide = GROUP * HDIM
    row = lax.broadcasted_iota(jnp.int32, (wide, HDIM), 0)
    head = lax.broadcasted_iota(jnp.int32, (wide, HDIM), 1)
    total = jnp.zeros((rows, HDIM), jnp.float32)
    for group in range(KVH // steps):
        at = slice(group * wide, (group + 1) * wide)
        product = out_ref[:, at].astype(jnp.float32) * gout_ref[:, at].astype(jnp.float32)
        high = product.astype(jnp.bfloat16)
        low = (product - high.astype(jnp.float32)).astype(jnp.bfloat16)
        first = (step * (KVH // steps) + group) * GROUP
        owner = (row >= (head - first) * HDIM) & (row < (head - first + 1) * HDIM)
        ones = jnp.where(owner, 1.0, 0.0).astype(jnp.bfloat16)
        total += jnp.dot(high, ones, preferred_element_type=jnp.float32)
        total += jnp.dot(low, ones, preferred_element_type=jnp.float32)

    @pl.when(step == 0)
    def _():
        sums[...] = total

    @pl.when(step > 0)
    def _():
        sums[...] += total

    @pl.when(step == steps - 1)
    def _():
        both = jnp.concatenate([sums[:, :HEADS], lse_ref[...]], axis=1)
        stats_ref[...] = both.T


def stat_rows(outputs, grad_out, lse_saved):
    rows = outputs.shape[0]
    steps = 2
    return pl.pallas_call(
        functools.partial(stats_kernel, steps),
        grid=(steps,),
        in_specs=[pl.BlockSpec((rows, HEADS * HDIM // steps), lambda g: (0, g))] * 2
        + [pl.BlockSpec((rows, HEADS), lambda g: (0, 0))],
        out_specs=pl.BlockSpec((2 * HEADS, rows), lambda g: (0, 0)),
        out_shape=jax.ShapeDtypeStruct((2 * HEADS, rows), jnp.float32),
        scratch_shapes=[pltpu.VMEM((rows, HDIM), jnp.float32)],
        compiler_params=pltpu.CompilerParams(vmem_limit_bytes=VMEM),
        cost_estimate=pl.CostEstimate(
            flops=4 * rows * HEADS * HDIM * HDIM,
            bytes_accessed=8 * rows * HEADS * HDIM,
            transcendentals=0,
        ),
        name="stats",
    )(outputs, grad_out, lse_saved)


def attend_kernel(plan, docs, meta, q_ref, gout_ref, lse_ref, delta_ref, *refs):
    shards_of, edge, start, finish = plan
    slots = len(shards_of)
    fixed = slots - 1 if edge else slots
    moved, refs = refs[:fixed], refs[fixed:]
    if edge:
        (odd_edge, even_edge), refs = refs[:2], refs[2:]
    if not start:
        carry_in, refs = refs[0], refs[1:]
    if finish == 2:
        refs = refs[1:]
    gq_ref, parts, (k_all, v_all, bias, prob, score) = refs[0], refs[1 : 1 + slots], refs[1 + slots :]
    rows = q_ref.shape[0]
    scale = 1.0 / HDIM**0.5
    me = meta[0]
    side = lax.rem(me, 2)

    @pl.when(pl.program_id(0) == 0)
    def _():
        token = lax.broadcasted_iota(jnp.int32, (1, rows), 1) + me * rows
        begin = jnp.zeros((1, rows), jnp.int32)
        bound = jnp.int32(0)
        for doc in range(docs):
            bound = bound + meta[1 + doc]
            begin = jnp.where(token >= bound, bound, begin)
        row = lax.broadcasted_iota(jnp.int32, (rows, rows), 0)
        for slot in range(slots):
            key = row + shards_of[slot](me, side) * rows
            visible = (key <= token) & (key >= begin)
            bias[slot * rows : (slot + 1) * rows, :] = jnp.where(visible, 0.0, -1e30)

    for slot in range(fixed):
        k_all[slot * rows : (slot + 1) * rows, :] = moved[slot][0]
        v_all[slot * rows : (slot + 1) * rows, :] = moved[slot][1]

    if edge:

        @pl.when(side == 1)
        def _():
            k_all[fixed * rows :, :] = odd_edge[0]
            v_all[fixed * rows :, :] = odd_edge[1]

        @pl.when(side == 0)
        def _():
            k_all[fixed * rows :, :] = even_edge[0]
            v_all[fixed * rows :, :] = even_edge[1]

    queries = head_rows(q_ref[...])
    gout = head_rows(gout_ref[...])
    keys = k_all[...]
    values = v_all[...]
    hidden = bias[...]
    hidden = jnp.concatenate([hidden, hidden], axis=1)
    for two in range(GROUP // 2):
        at = slice(2 * two * rows, (2 * two + 2) * rows)
        lse = jnp.concatenate(
            [lse_ref[2 * two : 2 * two + 1, :], lse_ref[2 * two + 1 : 2 * two + 2, :]], axis=1
        )
        delta = jnp.concatenate(
            [delta_ref[2 * two : 2 * two + 1, :], delta_ref[2 * two + 1 : 2 * two + 2, :]], axis=1
        )
        raw = contract_last(keys, queries[at])
        attn = jnp.exp2(raw * (scale * LOG2E) - lse * LOG2E + hidden)
        grad = contract_last(values, gout[at])
        prob[:, at] = attn.astype(jnp.bfloat16)
        score[:, at] = (attn * (grad - delta)).astype(jnp.bfloat16)
    scores = score[...]
    grad_k = jnp.dot(scores, queries, preferred_element_type=jnp.float32) * scale
    grad_v = jnp.dot(prob[...], gout, preferred_element_type=jnp.float32)
    for slot in range(slots):
        at = slice(slot * rows, (slot + 1) * rows)
        parts[slot][0] = grad_k[at].astype(parts[slot].dtype)
        parts[slot][1] = grad_v[at].astype(parts[slot].dtype)
    grad_q = contract_first(keys, scores)
    if not start:
        grad_q += carry_in[...]
    if finish:
        grad_q *= scale
        for h in range(GROUP):
            gq_ref[:, h * HDIM : (h + 1) * HDIM] = (
                grad_q[:, h * rows : (h + 1) * rows].T.astype(jnp.bfloat16)
            )
    else:
        gq_ref[...] = grad_q


def attend(meta, queries, grad_out, stats, moved, shards_of, kinds, edge, carry, finish, grad_q, head, per):
    rows = queries.shape[0]
    slots = len(shards_of)
    wide = pl.BlockSpec((rows, GROUP * HDIM), lambda g, m: (0, head + g))
    lse = pl.BlockSpec((GROUP, rows), lambda g, m: (KVH + head + g, 0))
    delta = pl.BlockSpec((GROUP, rows), lambda g, m: (head + g, 0))
    both = pl.BlockSpec((2, rows, HDIM), lambda g, m: (0, 0, g))
    held = pl.BlockSpec((HDIM, GROUP * rows), lambda g, m: (g, 0))
    in_specs = [wide, wide, lse, delta] + [both] * len(moved)
    operands = [meta, queries, grad_out, stats, stats] + moved
    aliases = {}
    if carry is not None:
        in_specs.append(held)
        operands.append(carry)
    if finish and grad_q is not None:
        in_specs.append(pl.BlockSpec(memory_space=pl.ANY))
        operands.append(grad_q)
        aliases = {len(operands) - 1: 0}
        finish = 2
    if finish:
        result = jax.ShapeDtypeStruct(queries.shape, jnp.bfloat16)
    else:
        result = jax.ShapeDtypeStruct((per * HDIM, GROUP * rows), jnp.float32)
    out_shape = [result] + [jax.ShapeDtypeStruct((2, rows, per * HDIM), kind) for kind in kinds]
    pairs = slots * rows * rows * GROUP * per
    plan = (shards_of, edge, carry is None, finish)
    return pl.pallas_call(
        functools.partial(attend_kernel, plan, meta.shape[0] - 1),
        grid_spec=pltpu.PrefetchScalarGridSpec(
            num_scalar_prefetch=1,
            grid=(per,),
            in_specs=in_specs,
            out_specs=[wide if finish else held] + [both] * slots,
            scratch_shapes=[
                pltpu.VMEM((slots * rows, HDIM), jnp.bfloat16),
                pltpu.VMEM((slots * rows, HDIM), jnp.bfloat16),
                pltpu.VMEM((slots * rows, rows), jnp.float32),
                pltpu.VMEM((slots * rows, GROUP * rows), jnp.bfloat16),
                pltpu.VMEM((slots * rows, GROUP * rows), jnp.bfloat16),
            ],
        ),
        out_shape=out_shape,
        input_output_aliases=aliases,
        compiler_params=pltpu.CompilerParams(vmem_limit_bytes=VMEM),
        cost_estimate=pl.CostEstimate(
            flops=40 * pairs * HDIM,
            bytes_accessed=per * rows * HDIM * 2 * (3 * GROUP + 6 * slots),
            transcendentals=pairs,
        ),
        name="attend_far" if edge else "attend_near",
    )(*operands)


def finish_kernel(aliased, meta, own_ref, edge_ref, far_ref, *refs):
    key_ref, value_ref = refs[2 * aliased :]
    kept = jnp.where(lax.rem(meta[0], 2) == 0, 1.0, 0.0)
    total = own_ref[...] + edge_ref[...].astype(jnp.float32) * kept + far_ref[...].astype(jnp.float32)
    key_ref[...] = total[0].astype(jnp.bfloat16)
    value_ref[...] = total[1].astype(jnp.bfloat16)


def finish_sums(meta, own, edge, far, grads, head, per, shape):
    rows = shape[0]
    block = pl.BlockSpec((rows, HDIM), lambda g, m: (0, head + g))
    both = pl.BlockSpec((2, rows, HDIM), lambda g, m: (0, 0, g))
    in_specs = [both] * 3
    operands = [meta, own, edge, far]
    aliases = {}
    if grads is not None:
        in_specs += [pl.BlockSpec(memory_space=pl.ANY)] * 2
        operands += grads
        aliases = {4: 0, 5: 1}
    return pl.pallas_call(
        functools.partial(finish_kernel, 1 if aliases else 0),
        grid_spec=pltpu.PrefetchScalarGridSpec(
            num_scalar_prefetch=1, grid=(per,), in_specs=in_specs, out_specs=[block] * 2
        ),
        out_shape=[jax.ShapeDtypeStruct(shape, jnp.bfloat16)] * 2,
        input_output_aliases=aliases,
        compiler_params=pltpu.CompilerParams(vmem_limit_bytes=VMEM),
        cost_estimate=pl.CostEstimate(
            flops=4 * rows * per * HDIM, bytes_accessed=24 * rows * per * HDIM, transcendentals=0
        ),
        name="finish",
    )(*operands)


def same_column(hop):
    return lambda me, side: me - 2 * hop


def other_column(hop):
    return lambda me, side: me - 2 * hop + 1 - 2 * side


def edge_shard(hops):
    return lambda me, side: jnp.where(side == 1, me - 1, me - 2 * hops + 1)


def shards(queries, keys, values, outputs, grad_out, lse_saved, doc_lengths):
    seq = lax.axis_size("seq")
    me = lax.axis_index("seq").astype(jnp.int32)
    side = lax.rem(me, 2)
    hops = seq // 4
    onward = [(s, s + 2) for s in range(seq - 2)]
    back = [(s + 2, s) for s in range(seq - 2)]
    swap = [(s, s + 1 - 2 * (s % 2)) for s in range(seq)]
    to_odd = [(s, s + 1) for s in range(0, seq, 2)]
    to_even = [(s + 1, s) for s in range(0, seq, 2)]

    def send(array, pairs):
        return lax.ppermute(array, "seq", pairs)

    meta = jnp.concatenate([me.reshape(1), doc_lengths])
    heads = [sum(CHUNKS[:chunk]) for chunk in range(len(CHUNKS))]
    same, other, edge = [], [], []
    for head, per in zip(heads, CHUNKS):
        at = slice(head * HDIM, (head + per) * HDIM)
        column = [jnp.stack([keys[:, at], values[:, at]])]
        for hop in range(hops):
            column.append(send(column[-1], onward))
        same.append(column)
        other.append([send(column[hop], swap) for hop in range(1, hops)])
        edge.append([send(column[0], to_odd), send(column[hops], to_even)])
    stats = stat_rows(outputs, grad_out, lse_saved)

    wide, half = jnp.float32, jnp.bfloat16
    carries, nears = [], []
    for chunk, (head, per) in enumerate(zip(heads, CHUNKS)):
        carry, *parts = attend(
            meta, queries, grad_out, stats, same[chunk][:2],
            [same_column(0), same_column(1)], [wide, wide], False, None, 0, None, head, per,
        )
        carries.append(carry)
        nears.append(parts)
    grad_q, grads = None, None
    for chunk, (head, per) in enumerate(zip(heads, CHUNKS)):
        far_same = range(2, hops + 1)
        far_other = range(1, hops)
        shards_of = [same_column(hop) for hop in far_same]
        shards_of += [other_column(hop) for hop in far_other] + [edge_shard(hops)]
        kinds = [wide] * len(far_same) + [half] * hops
        grad_q, *parts = attend(
            meta, queries, grad_out, stats, same[chunk][2:] + other[chunk] + edge[chunk],
            shards_of, kinds, True, carries[chunk], 1, grad_q, head, per,
        )
        column = nears[chunk] + parts[: hops - 1]
        edge_part = send(parts[-1], swap)
        others = [send(part, swap) for part in parts[hops - 1 : -1]]
        total = column[hops] + jnp.where(side == 1, edge_part.astype(wide), 0.0)
        for hop in range(hops - 1, 0, -1):
            far = send(total.astype(half), back)
            total = column[hop] + others[hop - 1].astype(wide) + far.astype(wide)
        far = send(total.astype(half), back)
        grads = finish_sums(meta, column[0], edge_part, far, grads, head, per, keys.shape)
    return (grad_q, grads[0], grads[1])


def solution(mesh):
    rows = P(("packs", "seq"), None)
    return jax.shard_map(
        shards,
        mesh=mesh,
        in_specs=(rows, rows, rows, rows, rows, rows, P("packs")),
        out_specs=(rows, rows, rows),
        check_vma=False,
    )
```

```python
import functools

import jax
import jax.numpy as jnp
from jax import lax
from jax.experimental import pallas as pl
from jax.experimental.pallas import tpu as pltpu
from jax.sharding import PartitionSpec as P

HEADS = 64
KVH = 8
HDIM = 128
GROUP = HEADS // KVH
CHUNKS = (4, 4)
LOG2E = 1.4426950408889634
VMEM = 60 * 1024 * 1024


def contract_last(first, second):
    return lax.dot_general(
        first, second, (((1,), (1,)), ((), ())), preferred_element_type=jnp.float32
    )


def contract_first(first, second):
    return lax.dot_general(
        first, second, (((0,), (0,)), ((), ())), preferred_element_type=jnp.float32
    )


def head_rows(block):
    return jnp.concatenate(
        [block[:, h * HDIM : (h + 1) * HDIM] for h in range(GROUP)], axis=0
    )


def delta_kernel(out_ref, gout_ref, delta_ref):
    rows = out_ref.shape[0]
    wide = GROUP * HDIM
    first = lax.broadcasted_iota(jnp.int32, (wide, HDIM), 1) * HDIM
    row = lax.broadcasted_iota(jnp.int32, (wide, HDIM), 0)
    ones = jnp.where((row >= first) & (row < first + HDIM), 1.0, 0.0).astype(jnp.bfloat16)
    for group in range(out_ref.shape[1] // wide):
        at = slice(group * wide, (group + 1) * wide)
        product = out_ref[:, at].astype(jnp.float32) * gout_ref[:, at].astype(jnp.float32)
        high = product.astype(jnp.bfloat16)
        low = (product - high.astype(jnp.float32)).astype(jnp.bfloat16)
        total = jnp.dot(high, ones, preferred_element_type=jnp.float32)
        total += jnp.dot(low, ones, preferred_element_type=jnp.float32)
        delta_ref[group * GROUP : (group + 1) * GROUP, :] = total.T[:GROUP]


def delta_rows(outputs, grad_out):
    rows = outputs.shape[0]
    steps = 2
    return pl.pallas_call(
        delta_kernel,
        grid=(steps,),
        in_specs=[pl.BlockSpec((rows, HEADS * HDIM // steps), lambda g: (0, g))] * 2,
        out_specs=pl.BlockSpec((HEADS // steps, rows), lambda g: (g, 0)),
        out_shape=jax.ShapeDtypeStruct((HEADS, rows), jnp.float32),
        compiler_params=pltpu.CompilerParams(vmem_limit_bytes=VMEM),
        cost_estimate=pl.CostEstimate(
            flops=4 * rows * HEADS * HDIM * HDIM,
            bytes_accessed=8 * rows * HEADS * HDIM,
            transcendentals=0,
        ),
        name="delta",
    )(outputs, grad_out)


def slot_shards(me, hops):
    side = lax.rem(me, 2)
    found = [me - 2 * hop for hop in range(hops + 1)]
    found += [me - 2 * hop + 1 - 2 * side for hop in range(1, hops)]
    found.append(jnp.where(side == 1, me - 1, me - 2 * hops + 1))
    return found


def attend_kernel(hops, aliased, docs, q_ref, gout_ref, lse_ref, delta_ref, *refs):
    slots = 2 * hops + 1
    moved, odd_edge, even_edge = refs[: slots - 1], refs[slots - 1], refs[slots]
    refs = refs[slots + 1 + aliased :]
    gq_ref, parts, lateral = refs[0], refs[1 : hops + 2], refs[hops + 2]
    k_all, v_all, bias, prob, score = refs[hops + 3 :]
    rows = q_ref.shape[0]
    scale = 1.0 / HDIM**0.5
    me = lax.axis_index("seq")
    side = lax.rem(me, 2)

    @pl.when(pl.program_id(0) == 0)
    def _():
        token = lax.broadcasted_iota(jnp.int32, (1, rows), 1) + me * rows
        begin = jnp.zeros((1, rows), jnp.int32)
        bound = jnp.int32(0)
        for doc in range(docs.shape[0]):
            bound = bound + docs[doc]
            begin = jnp.where(token >= bound, bound, begin)
        row = lax.broadcasted_iota(jnp.int32, (rows, rows), 0)
        for slot, shard in enumerate(slot_shards(me, hops)):
            key = row + shard * rows
            visible = (key <= token) & (key >= begin)
            bias[slot * rows : (slot + 1) * rows, :] = jnp.where(visible, 0.0, -1e30)

    for slot in range(slots - 1):
        k_all[slot * rows : (slot + 1) * rows, :] = moved[slot][0]
        v_all[slot * rows : (slot + 1) * rows, :] = moved[slot][1]

    @pl.when(side == 1)
    def _():
        k_all[(slots - 1) * rows :, :] = odd_edge[0]
        v_all[(slots - 1) * rows :, :] = odd_edge[1]

    @pl.when(side == 0)
    def _():
        k_all[(slots - 1) * rows :, :] = even_edge[0]
        v_all[(slots - 1) * rows :, :] = even_edge[1]

    queries = head_rows(q_ref[...])
    gout = head_rows(gout_ref[...])
    keys = k_all[...]
    values = v_all[...]
    hidden = bias[...]
    hidden = jnp.concatenate([hidden, hidden], axis=1)
    for two in range(GROUP // 2):
        at = slice(2 * two * rows, (2 * two + 2) * rows)
        lse = jnp.concatenate(
            [lse_ref[2 * two : 2 * two + 1, :], lse_ref[2 * two + 1 : 2 * two + 2, :]], axis=1
        )
        delta = jnp.concatenate(
            [delta_ref[2 * two : 2 * two + 1, :], delta_ref[2 * two + 1 : 2 * two + 2, :]], axis=1
        )
        raw = contract_last(keys, queries[at])
        attn = jnp.exp2(raw * (scale * LOG2E) - lse * LOG2E + hidden)
        grad = contract_last(values, gout[at])
        prob[:, at] = attn.astype(jnp.bfloat16)
        score[:, at] = (attn * (grad - delta)).astype(jnp.bfloat16)
    scores = score[...]
    grad_k = jnp.dot(scores, queries, preferred_element_type=jnp.float32) * scale
    grad_v = jnp.dot(prob[...], gout, preferred_element_type=jnp.float32)
    for slot in range(slots):
        at = slice(slot * rows, (slot + 1) * rows)
        part = parts[slot] if slot <= hops else lateral.at[slot - hops - 1]
        part[0] = grad_k[at].astype(part.dtype)
        part[1] = grad_v[at].astype(part.dtype)
    grad_q = contract_first(keys, scores) * scale
    for h in range(GROUP):
        gq_ref[:, h * HDIM : (h + 1) * HDIM] = (
            grad_q[:, h * rows : (h + 1) * rows].T.astype(jnp.bfloat16)
        )


def attend(docs, queries, grad_out, lse, delta, moved, grad_q, head, per, hops):
    rows = queries.shape[0]
    slots = 2 * hops + 1
    wide = pl.BlockSpec((rows, GROUP * HDIM), lambda g, m: (0, head + g))
    stat = pl.BlockSpec((GROUP, rows), lambda g, m: (head + g, 0))
    both = pl.BlockSpec((2, rows, HDIM), lambda g, m: (0, 0, g))
    several = pl.BlockSpec((hops, 2, rows, HDIM), lambda g, m: (0, 0, 0, g))
    in_specs = [wide, wide, stat, stat] + [both] * len(moved)
    operands = [docs, queries, grad_out, lse, delta] + moved
    aliases = {}
    if grad_q is not None:
        in_specs.append(pl.BlockSpec(memory_space=pl.ANY))
        operands.append(grad_q)
        aliases = {len(operands) - 1: 0}
    out_shape = [jax.ShapeDtypeStruct(queries.shape, jnp.bfloat16)]
    out_shape += [jax.ShapeDtypeStruct((2, rows, per * HDIM), jnp.float32)] * (hops + 1)
    out_shape += [jax.ShapeDtypeStruct((hops, 2, rows, per * HDIM), jnp.bfloat16)]
    pairs = slots * rows * rows * GROUP * per
    return pl.pallas_call(
        functools.partial(attend_kernel, hops, len(aliases)),
        grid_spec=pltpu.PrefetchScalarGridSpec(
            num_scalar_prefetch=1,
            grid=(per,),
            in_specs=in_specs,
            out_specs=[wide] + [both] * (hops + 1) + [several],
            scratch_shapes=[
                pltpu.VMEM((slots * rows, HDIM), jnp.bfloat16),
                pltpu.VMEM((slots * rows, HDIM), jnp.bfloat16),
                pltpu.VMEM((slots * rows, rows), jnp.float32),
                pltpu.VMEM((slots * rows, GROUP * rows), jnp.bfloat16),
                pltpu.VMEM((slots * rows, GROUP * rows), jnp.bfloat16),
            ],
        ),
        out_shape=out_shape,
        input_output_aliases=aliases,
        compiler_params=pltpu.CompilerParams(vmem_limit_bytes=VMEM),
        cost_estimate=pl.CostEstimate(
            flops=40 * pairs * HDIM,
            bytes_accessed=per * rows * HDIM * 2 * (3 * GROUP + 6 * slots),
            transcendentals=pairs,
        ),
        name="attend",
    )(*operands)


def shards(queries, keys, values, outputs, grad_out, lse_saved, doc_lengths):
    seq = lax.axis_size("seq")
    me = lax.axis_index("seq").astype(jnp.int32)
    side = lax.rem(me, 2)
    hops = seq // 4
    onward = [(s, s + 2) for s in range(seq - 2)]
    back = [(s + 2, s) for s in range(seq - 2)]
    swap = [(s, s + 1 - 2 * (s % 2)) for s in range(seq)]
    to_odd = [(s, s + 1) for s in range(0, seq, 2)]
    to_even = [(s + 1, s) for s in range(0, seq, 2)]

    def send(array, pairs):
        return lax.ppermute(array, "seq", pairs)

    heads = [sum(CHUNKS[:chunk]) for chunk in range(len(CHUNKS))]
    arrived = []
    for head, per in zip(heads, CHUNKS):
        at = slice(head * HDIM, (head + per) * HDIM)
        column = [jnp.stack([keys[:, at], values[:, at]])]
        for hop in range(hops):
            column.append(send(column[-1], onward))
        other = [send(column[hop], swap) for hop in range(1, hops)]
        edge = [send(column[0], to_odd), send(column[hops], to_even)]
        arrived.append(column + other + edge)
    delta = delta_rows(outputs, grad_out)
    lse = lse_saved.T

    wide, half = jnp.float32, jnp.bfloat16
    grad_q = None
    sums = []
    for head, per, moved in zip(heads, CHUNKS, arrived):
        grad_q, *column, lateral = attend(
            doc_lengths, queries, grad_out, lse, delta, moved, grad_q, head, per, hops
        )
        lateral = send(lateral, swap).astype(wide)
        total = column[hops] + jnp.where(side == 1, lateral[hops - 1], 0.0)
        for hop in range(hops - 1, 0, -1):
            far = send(total.astype(half), back)
            total = column[hop] + lateral[hop - 1] + far.astype(wide)
        far = send(total.astype(half), back)
        total = column[0] + jnp.where(side == 0, lateral[hops - 1], 0.0) + far.astype(wide)
        sums.append(total.astype(half))
    grad_keys = jnp.concatenate([total[0] for total in sums], axis=1)
    grad_values = jnp.concatenate([total[1] for total in sums], axis=1)
    return (grad_q, grad_keys, grad_values)


def solution(mesh):
    rows = P(("packs", "seq"), None)
    return jax.shard_map(
        shards,
        mesh=mesh,
        in_specs=(rows, rows, rows, rows, rows, rows, P("packs")),
        out_specs=(rows, rows, rows),
        check_vma=False,
    )
```

```python
import functools

import jax
import jax.numpy as jnp
from jax import lax
from jax.experimental import pallas as pl
from jax.experimental.pallas import tpu as pltpu
from jax.sharding import PartitionSpec as P

HEADS = 64
KVH = 8
HDIM = 128
GROUP = HEADS // KVH
CHUNKS = ((4,), (2, 2))
LOG2E = 1.4426950408889634
VMEM = 60 * 1024 * 1024


def contract_last(first, second):
    return lax.dot_general(
        first, second, (((1,), (1,)), ((), ())), preferred_element_type=jnp.float32
    )


def contract_first(first, second):
    return lax.dot_general(
        first, second, (((0,), (0,)), ((), ())), preferred_element_type=jnp.float32
    )


def head_rows(block):
    return jnp.concatenate(
        [block[:, h * HDIM : (h + 1) * HDIM] for h in range(GROUP)], axis=0
    )


def delta_kernel(out_ref, gout_ref, delta_ref):
    rows = out_ref.shape[0]
    wide = GROUP * HDIM
    first = lax.broadcasted_iota(jnp.int32, (wide, HDIM), 1) * HDIM
    row = lax.broadcasted_iota(jnp.int32, (wide, HDIM), 0)
    ones = jnp.where((row >= first) & (row < first + HDIM), 1.0, 0.0).astype(jnp.bfloat16)
    for group in range(out_ref.shape[1] // wide):
        at = slice(group * wide, (group + 1) * wide)
        product = out_ref[:, at].astype(jnp.float32) * gout_ref[:, at].astype(jnp.float32)
        high = product.astype(jnp.bfloat16)
        low = (product - high.astype(jnp.float32)).astype(jnp.bfloat16)
        total = jnp.dot(high, ones, preferred_element_type=jnp.float32)
        total += jnp.dot(low, ones, preferred_element_type=jnp.float32)
        delta_ref[group * GROUP : (group + 1) * GROUP, :] = total.T[:GROUP]


def delta_rows(outputs, grad_out):
    rows = outputs.shape[0]
    steps = 4
    return pl.pallas_call(
        delta_kernel,
        grid=(steps,),
        in_specs=[pl.BlockSpec((rows, HEADS * HDIM // steps), lambda g: (0, g))] * 2,
        out_specs=pl.BlockSpec((HEADS // steps, rows), lambda g: (g, 0)),
        out_shape=jax.ShapeDtypeStruct((HEADS, rows), jnp.float32),
        compiler_params=pltpu.CompilerParams(vmem_limit_bytes=VMEM),
        cost_estimate=pl.CostEstimate(
            flops=4 * rows * HEADS * HDIM * HDIM,
            bytes_accessed=8 * rows * HEADS * HDIM,
            transcendentals=0,
        ),
        name="delta",
    )(outputs, grad_out)


def slot_shards(me, hops):
    side = lax.rem(me, 2)
    found = [me - 2 * hop for hop in range(hops + 1)]
    found += [me - 2 * hop + 1 - 2 * side for hop in range(1, hops)]
    found.append(jnp.where(side == 1, me - 1, me - 2 * hops + 1))
    return found


def attend_kernel(hops, aliased, docs, q_ref, gout_ref, lse_ref, delta_ref, *refs):
    slots = 2 * hops + 1
    moved, odd_edge, even_edge = refs[: slots - 1], refs[slots - 1], refs[slots]
    refs = refs[slots + 1 + aliased :]
    gq_ref, parts, lateral = refs[0], refs[1 : hops + 2], refs[hops + 2]
    k_all, v_all, bias, prob, score = refs[hops + 3 :]
    rows = q_ref.shape[0]
    scale = 1.0 / HDIM**0.5
    me = lax.axis_index("seq")
    side = lax.rem(me, 2)

    @pl.when(pl.program_id(0) == 0)
    def _():
        token = lax.broadcasted_iota(jnp.int32, (1, rows), 1) + me * rows
        begin = jnp.zeros((1, rows), jnp.int32)
        bound = jnp.int32(0)
        for doc in range(docs.shape[0]):
            bound = bound + docs[doc]
            begin = jnp.where(token >= bound, bound, begin)
        row = lax.broadcasted_iota(jnp.int32, (rows, rows), 0)
        for slot, shard in enumerate(slot_shards(me, hops)):
            key = row + shard * rows
            visible = (key <= token) & (key >= begin)
            bias[slot * rows : (slot + 1) * rows, :] = jnp.where(visible, 0.0, -1e30)

    for slot in range(slots - 1):
        k_all[slot * rows : (slot + 1) * rows, :] = moved[slot][0]
        v_all[slot * rows : (slot + 1) * rows, :] = moved[slot][1]

    @pl.when(side == 1)
    def _():
        k_all[(slots - 1) * rows :, :] = odd_edge[0]
        v_all[(slots - 1) * rows :, :] = odd_edge[1]

    @pl.when(side == 0)
    def _():
        k_all[(slots - 1) * rows :, :] = even_edge[0]
        v_all[(slots - 1) * rows :, :] = even_edge[1]

    queries = head_rows(q_ref[...])
    gout = head_rows(gout_ref[...])
    keys = k_all[...]
    values = v_all[...]
    hidden = bias[...]
    hidden = jnp.concatenate([hidden, hidden], axis=1)
    for two in range(GROUP // 2):
        at = slice(2 * two * rows, (2 * two + 2) * rows)
        lse = jnp.concatenate(
            [lse_ref[2 * two : 2 * two + 1, :], lse_ref[2 * two + 1 : 2 * two + 2, :]], axis=1
        )
        delta = jnp.concatenate(
            [delta_ref[2 * two : 2 * two + 1, :], delta_ref[2 * two + 1 : 2 * two + 2, :]], axis=1
        )
        raw = contract_last(keys, queries[at])
        attn = jnp.exp2(raw * (scale * LOG2E) - lse * LOG2E + hidden)
        grad = contract_last(values, gout[at])
        prob[:, at] = attn.astype(jnp.bfloat16)
        score[:, at] = (attn * (grad - delta)).astype(jnp.bfloat16)
    scores = score[...]
    grad_k = jnp.dot(scores, queries, preferred_element_type=jnp.float32) * scale
    grad_v = jnp.dot(prob[...], gout, preferred_element_type=jnp.float32)
    for slot in range(slots):
        at = slice(slot * rows, (slot + 1) * rows)
        part = parts[slot] if slot <= hops else lateral.at[slot - hops - 1]
        part[0] = grad_k[at].astype(part.dtype)
        part[1] = grad_v[at].astype(part.dtype)
    grad_q = contract_first(keys, scores) * scale
    for h in range(GROUP):
        gq_ref[:, h * HDIM : (h + 1) * HDIM] = (
            grad_q[:, h * rows : (h + 1) * rows].T.astype(jnp.bfloat16)
        )


def attend(docs, queries, grad_out, lse, delta, moved, grad_q, first, head, per, hops):
    rows = queries.shape[0]
    slots = 2 * hops + 1
    wide = pl.BlockSpec((rows, GROUP * HDIM), lambda g, m: (0, head + g))
    stat = pl.BlockSpec((GROUP, rows), lambda g, m: (head + g, 0))
    held = pl.BlockSpec((2, rows, HDIM), lambda g, m: (0, 0, head - first + g))
    both = pl.BlockSpec((2, rows, HDIM), lambda g, m: (0, 0, g))
    several = pl.BlockSpec((hops, 2, rows, HDIM), lambda g, m: (0, 0, 0, g))
    in_specs = [wide, wide, stat, stat] + [held] * len(moved)
    operands = [docs, queries, grad_out, lse, delta] + moved
    aliases = {}
    if grad_q is not None:
        in_specs.append(pl.BlockSpec(memory_space=pl.ANY))
        operands.append(grad_q)
        aliases = {len(operands) - 1: 0}
    out_shape = [jax.ShapeDtypeStruct(queries.shape, jnp.bfloat16)]
    out_shape += [jax.ShapeDtypeStruct((2, rows, per * HDIM), jnp.float32)] * (hops + 1)
    out_shape += [jax.ShapeDtypeStruct((hops, 2, rows, per * HDIM), jnp.bfloat16)]
    pairs = slots * rows * rows * GROUP * per
    return pl.pallas_call(
        functools.partial(attend_kernel, hops, len(aliases)),
        grid_spec=pltpu.PrefetchScalarGridSpec(
            num_scalar_prefetch=1,
            grid=(per,),
            in_specs=in_specs,
            out_specs=[wide] + [both] * (hops + 1) + [several],
            scratch_shapes=[
                pltpu.VMEM((slots * rows, HDIM), jnp.bfloat16),
                pltpu.VMEM((slots * rows, HDIM), jnp.bfloat16),
                pltpu.VMEM((slots * rows, rows), jnp.float32),
                pltpu.VMEM((slots * rows, GROUP * rows), jnp.bfloat16),
                pltpu.VMEM((slots * rows, GROUP * rows), jnp.bfloat16),
            ],
        ),
        out_shape=out_shape,
        input_output_aliases=aliases,
        compiler_params=pltpu.CompilerParams(vmem_limit_bytes=VMEM),
        cost_estimate=pl.CostEstimate(
            flops=40 * pairs * HDIM,
            bytes_accessed=per * rows * HDIM * 2 * (3 * GROUP + 6 * slots),
            transcendentals=pairs,
        ),
        name="attend",
    )(*operands)


def shards(queries, keys, values, outputs, grad_out, lse_saved, doc_lengths):
    seq = lax.axis_size("seq")
    me = lax.axis_index("seq").astype(jnp.int32)
    side = lax.rem(me, 2)
    hops = seq // 4
    def onward(hop):
        return [(s, s + 2) for s in range(2 * hop - 2, seq - 2)]

    def back(hop):
        return [(s, s - 2) for s in range(2 * hop, seq)]

    def to_odd(hop):
        return [(s, s + 1) for s in range(2 * hop, seq, 2)]

    def to_even(hop):
        return [(s + 1, s) for s in range(2 * hop, seq, 2)]

    def send(array, pairs):
        return lax.ppermute(array, "seq", pairs)

    def after(array, *others):
        return lax.optimization_barrier((array,) + others)[0]

    delta = delta_rows(outputs, grad_out)
    lse = lse_saved.T
    starts = [sum(map(sum, CHUNKS[:chunk])) for chunk in range(len(CHUNKS))]
    arrived = []
    for head, split in zip(starts, CHUNKS):
        at = slice(head * HDIM, (head + sum(split)) * HDIM)
        own = jnp.stack([keys[:, at], values[:, at]])
        column = [own, send(own, onward(1))]
        column[1], delta = lax.optimization_barrier((column[1], delta))
        for hop in range(2, hops + 1):
            column.append(send(column[-1], onward(hop)))
        ready = [arrived[-1][hops]] if arrived else []
        other = [
            send(after(column[hop], *ready), to_odd(hop) + to_even(hop)) for hop in range(1, hops)
        ]
        edge = [send(own, to_odd(0)), send(column[hops], to_even(hops))]
        arrived.append(column + other + edge)

    wide, half = jnp.float32, jnp.bfloat16
    grad_q = None
    sums = []
    before = [[] for hop in range(hops + 1)]
    for first, split, moved in zip(starts, CHUNKS, arrived):
        head = first
        for per in split:
            grad_q, *column, lateral = attend(
                doc_lengths, queries, grad_out, lse, delta, moved, grad_q, first, head, per, hops
            )
            head += per
            lateral = send(after(lateral, *before[hops]), to_odd(1) + to_even(0))
            before[hops] = [lateral]
            lateral = lateral.astype(wide)
            total = column[hops] + jnp.where(side == 1, lateral[hops - 1], 0.0)
            for hop in range(hops - 1, -1, -1):
                far = send(after(total.astype(half), *before[hop]), back(hop + 1))
                before[hop] = [far]
                if hop:
                    total = column[hop] + lateral[hop - 1] + far.astype(wide)
            total = column[0] + jnp.where(side == 0, lateral[hops - 1], 0.0) + far.astype(wide)
            sums.append(total.astype(half))
    grad_keys = jnp.concatenate([total[0] for total in sums], axis=1)
    grad_values = jnp.concatenate([total[1] for total in sums], axis=1)
    return (grad_q, grad_keys, grad_values)


def solution(mesh):
    rows = P(("packs", "seq"), None)
    return jax.shard_map(
        shards,
        mesh=mesh,
        in_specs=(rows, rows, rows, rows, rows, rows, P("packs")),
        out_specs=(rows, rows, rows),
        check_vma=False,
    )
```

```python
import functools

import jax
import jax.numpy as jnp
from jax import lax
from jax.experimental import pallas as pl
from jax.experimental.pallas import tpu as pltpu
from jax.sharding import PartitionSpec as P

HEADS = 64
KVH = 8
HDIM = 128
GROUP = HEADS // KVH
CHUNKS = ((4,), (4,))
LOG2E = 1.4426950408889634
VMEM = 60 * 1024 * 1024


def contract_last(first, second):
    return lax.dot_general(
        first, second, (((1,), (1,)), ((), ())), preferred_element_type=jnp.float32
    )


def contract_first(first, second):
    return lax.dot_general(
        first, second, (((0,), (0,)), ((), ())), preferred_element_type=jnp.float32
    )


def head_rows(block):
    return jnp.concatenate(
        [block[:, h * HDIM : (h + 1) * HDIM] for h in range(GROUP)], axis=0
    )


def delta_kernel(out_ref, gout_ref, delta_ref):
    rows = out_ref.shape[0]
    wide = GROUP * HDIM
    first = lax.broadcasted_iota(jnp.int32, (wide, HDIM), 1) * HDIM
    row = lax.broadcasted_iota(jnp.int32, (wide, HDIM), 0)
    ones = jnp.where((row >= first) & (row < first + HDIM), 1.0, 0.0).astype(jnp.bfloat16)
    for group in range(out_ref.shape[1] // wide):
        at = slice(group * wide, (group + 1) * wide)
        product = out_ref[:, at].astype(jnp.float32) * gout_ref[:, at].astype(jnp.float32)
        high = product.astype(jnp.bfloat16)
        low = (product - high.astype(jnp.float32)).astype(jnp.bfloat16)
        total = jnp.dot(high, ones, preferred_element_type=jnp.float32)
        total += jnp.dot(low, ones, preferred_element_type=jnp.float32)
        delta_ref[group * GROUP : (group + 1) * GROUP, :] = total.T[:GROUP]


def delta_rows(outputs, grad_out):
    rows = outputs.shape[0]
    steps = 4
    return pl.pallas_call(
        delta_kernel,
        grid=(steps,),
        in_specs=[pl.BlockSpec((rows, HEADS * HDIM // steps), lambda g: (0, g))] * 2,
        out_specs=pl.BlockSpec((HEADS // steps, rows), lambda g: (g, 0)),
        out_shape=jax.ShapeDtypeStruct((HEADS, rows), jnp.float32),
        compiler_params=pltpu.CompilerParams(vmem_limit_bytes=VMEM),
        cost_estimate=pl.CostEstimate(
            flops=4 * rows * HEADS * HDIM * HDIM,
            bytes_accessed=8 * rows * HEADS * HDIM,
            transcendentals=0,
        ),
        name="delta",
    )(outputs, grad_out)


def slot_shards(me, hops):
    side = lax.rem(me, 2)
    found = [me - 2 * hop for hop in range(hops + 1)]
    found += [me - 2 * hop + 1 - 2 * side for hop in range(1, hops)]
    found.append(jnp.where(side == 1, me - 1, me - 2 * hops + 1))
    return found


def attend_kernel(hops, aliased, docs, other, q_ref, gout_ref, lse_ref, delta_ref, *refs):
    slots = 2 * hops + 1
    moved, refs = refs[:slots], refs[slots + aliased :]
    gq_ref, parts, lateral = refs[0], refs[1 : hops + 2], refs[hops + 2]
    k_all, v_all, bias, prob, score = refs[hops + 3 :]
    rows = q_ref.shape[0]
    scale = 1.0 / HDIM**0.5
    me = lax.axis_index("seq")

    @pl.when(pl.program_id(0) == 0)
    def _():
        token = lax.broadcasted_iota(jnp.int32, (1, rows), 1) + me * rows
        begin = jnp.zeros((1, rows), jnp.int32)
        bound = jnp.int32(0)
        for doc in range(docs.shape[0]):
            bound = bound + docs[doc]
            begin = jnp.where(token >= bound, bound, begin)
        row = lax.broadcasted_iota(jnp.int32, (rows, rows), 0)
        for slot, shard in enumerate(slot_shards(me, hops)):
            key = row + shard * rows
            visible = (key <= token) & (key >= begin)
            bias[slot * rows : (slot + 1) * rows, :] = jnp.where(visible, 0.0, -1e30)

    for slot in range(slots):
        pair = moved[slot] if slot <= hops else moved[slot].at[0]
        k_all[slot * rows : (slot + 1) * rows, :] = pair[0]
        v_all[slot * rows : (slot + 1) * rows, :] = pair[1]

    queries = head_rows(q_ref[...])
    gout = head_rows(gout_ref[...])
    keys = k_all[...]
    values = v_all[...]
    hidden = bias[...]
    hidden = jnp.concatenate([hidden, hidden], axis=1)
    for two in range(GROUP // 2):
        at = slice(2 * two * rows, (2 * two + 2) * rows)
        lse = jnp.concatenate(
            [lse_ref[2 * two : 2 * two + 1, :], lse_ref[2 * two + 1 : 2 * two + 2, :]], axis=1
        )
        delta = jnp.concatenate(
            [delta_ref[2 * two : 2 * two + 1, :], delta_ref[2 * two + 1 : 2 * two + 2, :]], axis=1
        )
        raw = contract_last(keys, queries[at])
        attn = jnp.exp2(raw * (scale * LOG2E) - lse * LOG2E + hidden)
        grad = contract_last(values, gout[at])
        prob[:, at] = attn.astype(jnp.bfloat16)
        score[:, at] = (attn * (grad - delta)).astype(jnp.bfloat16)
    scores = score[...]
    grad_k = jnp.dot(scores, queries, preferred_element_type=jnp.float32) * scale
    grad_v = jnp.dot(prob[...], gout, preferred_element_type=jnp.float32)
    for slot in range(slots):
        at = slice(slot * rows, (slot + 1) * rows)
        part = parts[slot] if slot <= hops else lateral.at[slot - hops - 1]
        part[0] = grad_k[at].astype(part.dtype)
        part[1] = grad_v[at].astype(part.dtype)
    grad_q = contract_first(keys, scores) * scale
    for h in range(GROUP):
        gq_ref[:, h * HDIM : (h + 1) * HDIM] = (
            grad_q[:, h * rows : (h + 1) * rows].T.astype(jnp.bfloat16)
        )


def attend(docs, other, queries, grad_out, lse, delta, moved, grad_q, first, head, per, hops):
    rows = queries.shape[0]
    slots = 2 * hops + 1
    wide = pl.BlockSpec((rows, GROUP * HDIM), lambda g, d, o: (0, head + g))
    stat = pl.BlockSpec((GROUP, rows), lambda g, d, o: (head + g, 0))
    held = pl.BlockSpec((2, rows, HDIM), lambda g, d, o: (0, 0, head - first + g))
    crossed = pl.BlockSpec((1, 2, rows, HDIM), lambda g, d, o: (o[0], 0, 0, head - first + g))
    both = pl.BlockSpec((2, rows, HDIM), lambda g, d, o: (0, 0, g))
    several = pl.BlockSpec((hops, 2, rows, HDIM), lambda g, d, o: (0, 0, 0, g))
    in_specs = [wide, wide, stat, stat] + [held] * (hops + 1) + [crossed] * hops
    operands = [docs, other, queries, grad_out, lse, delta] + moved
    aliases = {}
    if grad_q is not None:
        in_specs.append(pl.BlockSpec(memory_space=pl.ANY))
        operands.append(grad_q)
        aliases = {len(operands) - 1: 0}
    out_shape = [jax.ShapeDtypeStruct(queries.shape, jnp.bfloat16)]
    out_shape += [jax.ShapeDtypeStruct((2, rows, per * HDIM), jnp.float32)] * (hops + 1)
    out_shape += [jax.ShapeDtypeStruct((hops, 2, rows, per * HDIM), jnp.bfloat16)]
    pairs = slots * rows * rows * GROUP * per
    return pl.pallas_call(
        functools.partial(attend_kernel, hops, len(aliases)),
        grid_spec=pltpu.PrefetchScalarGridSpec(
            num_scalar_prefetch=2,
            grid=(per,),
            in_specs=in_specs,
            out_specs=[wide] + [both] * (hops + 1) + [several],
            scratch_shapes=[
                pltpu.VMEM((slots * rows, HDIM), jnp.bfloat16),
                pltpu.VMEM((slots * rows, HDIM), jnp.bfloat16),
                pltpu.VMEM((slots * rows, rows), jnp.float32),
                pltpu.VMEM((slots * rows, GROUP * rows), jnp.bfloat16),
                pltpu.VMEM((slots * rows, GROUP * rows), jnp.bfloat16),
            ],
        ),
        out_shape=out_shape,
        input_output_aliases=aliases,
        compiler_params=pltpu.CompilerParams(vmem_limit_bytes=VMEM),
        cost_estimate=pl.CostEstimate(
            flops=40 * pairs * HDIM,
            bytes_accessed=per * rows * HDIM * 2 * (3 * GROUP + 6 * slots),
            transcendentals=pairs,
        ),
        name="attend",
    )(*operands)


def shards(queries, keys, values, outputs, grad_out, lse_saved, doc_lengths):
    seq = lax.axis_size("seq")
    me = lax.axis_index("seq").astype(jnp.int32)
    side = lax.rem(me, 2)
    hops = seq // 4
    def onward(hop):
        return [(s, s + 2) for s in range(2 * hop - 2, seq - 2)]

    def back(hop):
        return [(s, s - 2) for s in range(2 * hop, seq)]

    def to_odd(hop):
        return [(s, s + 1) for s in range(2 * hop, seq, 2)]

    def to_even(hop):
        return [(s + 1, s) for s in range(2 * hop, seq, 2)]

    def send(array, pairs):
        return lax.ppermute(array, "seq", pairs)

    def cross(array):
        groups = [[s, s + 1] for s in range(0, seq, 2)]
        return lax.all_gather(array, "seq", axis_index_groups=groups)

    def after(array, *others):
        return lax.optimization_barrier((array,) + others)[0]

    delta = delta_rows(outputs, grad_out)
    lse = lse_saved.T
    other = (1 - side).astype(jnp.int32).reshape(1)
    starts = [sum(map(sum, CHUNKS[:chunk])) for chunk in range(len(CHUNKS))]
    arrived = []
    for head, split in zip(starts, CHUNKS):
        at = slice(head * HDIM, (head + sum(split)) * HDIM)
        own = jnp.stack([keys[:, at], values[:, at]])
        column = [own, send(own, onward(1))]
        column[1], delta = lax.optimization_barrier((column[1], delta))
        for hop in range(2, hops + 1):
            column.append(send(column[-1], onward(hop)))
        sent = column[1:hops] + [jnp.where(side == 0, own, column[hops])]
        arrived.append(column + [cross(array) for array in sent])

    wide, half = jnp.float32, jnp.bfloat16
    grad_q = None
    sums = []
    before = [[] for hop in range(hops + 1)]
    for first, split, moved in zip(starts, CHUNKS, arrived):
        head = first
        for per in split:
            grad_q, *column, lateral = attend(
                doc_lengths, other, queries, grad_out, lse, delta, moved, grad_q, first, head, per, hops
            )
            head += per
            lateral = send(after(lateral, *before[hops]), to_odd(1) + to_even(0))
            before[hops] = [lateral]
            lateral = lateral.astype(wide)
            total = column[hops] + jnp.where(side == 1, lateral[hops - 1], 0.0)
            for hop in range(hops - 1, -1, -1):
                far = send(after(total.astype(half), *before[hop]), back(hop + 1))
                before[hop] = [far]
                if hop:
                    total = column[hop] + lateral[hop - 1] + far.astype(wide)
            total = column[0] + jnp.where(side == 0, lateral[hops - 1], 0.0) + far.astype(wide)
            sums.append(total.astype(half))
    grad_keys = jnp.concatenate([total[0] for total in sums], axis=1)
    grad_values = jnp.concatenate([total[1] for total in sums], axis=1)
    return (grad_q, grad_keys, grad_values)


def solution(mesh):
    rows = P(("packs", "seq"), None)
    return jax.shard_map(
        shards,
        mesh=mesh,
        in_specs=(rows, rows, rows, rows, rows, rows, P("packs")),
        out_specs=(rows, rows, rows),
        check_vma=False,
    )
```

```python
import functools

import jax
import jax.numpy as jnp
from jax import lax
from jax.experimental import pallas as pl
from jax.experimental.pallas import tpu as pltpu
from jax.sharding import PartitionSpec as P

HEADS = 64
KVH = 8
HDIM = 128
GROUP = HEADS // KVH
CHUNKS = (4, 4)
STEP = 2
LOG2E = 1.4426950408889634
VMEM = 60 * 1024 * 1024


def contract_last(first, second):
    return lax.dot_general(
        first, second, (((1,), (1,)), ((), ())), preferred_element_type=jnp.float32
    )


def contract_first(first, second):
    return lax.dot_general(
        first, second, (((0,), (0,)), ((), ())), preferred_element_type=jnp.float32
    )


def head_rows(block):
    return jnp.concatenate(
        [block[:, h * HDIM : (h + 1) * HDIM] for h in range(GROUP)], axis=0
    )


def delta_kernel(out_ref, gout_ref, delta_ref):
    rows = out_ref.shape[0]
    wide = GROUP * HDIM
    first = lax.broadcasted_iota(jnp.int32, (wide, HDIM), 1) * HDIM
    row = lax.broadcasted_iota(jnp.int32, (wide, HDIM), 0)
    ones = jnp.where((row >= first) & (row < first + HDIM), 1.0, 0.0).astype(jnp.bfloat16)
    for group in range(out_ref.shape[1] // wide):
        at = slice(group * wide, (group + 1) * wide)
        product = out_ref[:, at].astype(jnp.float32) * gout_ref[:, at].astype(jnp.float32)
        high = product.astype(jnp.bfloat16)
        low = (product - high.astype(jnp.float32)).astype(jnp.bfloat16)
        total = jnp.dot(high, ones, preferred_element_type=jnp.float32)
        total += jnp.dot(low, ones, preferred_element_type=jnp.float32)
        delta_ref[group * GROUP : (group + 1) * GROUP, :] = total.T[:GROUP]


def delta_rows(outputs, grad_out):
    rows = outputs.shape[0]
    steps = 4
    return pl.pallas_call(
        delta_kernel,
        grid=(steps,),
        in_specs=[pl.BlockSpec((rows, HEADS * HDIM // steps), lambda g: (0, g))] * 2,
        out_specs=pl.BlockSpec((HEADS // steps, rows), lambda g: (g, 0)),
        out_shape=jax.ShapeDtypeStruct((HEADS, rows), jnp.float32),
        compiler_params=pltpu.CompilerParams(vmem_limit_bytes=VMEM),
        cost_estimate=pl.CostEstimate(
            flops=4 * rows * HEADS * HDIM * HDIM,
            bytes_accessed=8 * rows * HEADS * HDIM,
            transcendentals=0,
        ),
        name="delta",
    )(outputs, grad_out)


def slot_shards(me, hops):
    side = lax.rem(me, 2)
    found = [me - 2 * hop for hop in range(hops + 1)]
    found += [me - 2 * hop + 1 - 2 * side for hop in range(1, hops)]
    found.append(jnp.where(side == 1, me - 1, me - 2 * hops + 1))
    return found


def attend_kernel(hops, aliased, docs, q_ref, gout_ref, lse_ref, delta_ref, *refs):
    slots = 2 * hops + 1
    moved, refs = refs[:slots], refs[slots + aliased :]
    gq_ref, parts, (k_all, v_all, bias, prob, score) = refs[0], refs[1 : 1 + slots], refs[1 + slots :]
    rows = q_ref.shape[0]
    scale = 1.0 / HDIM**0.5
    me = lax.axis_index("seq")

    @pl.when(pl.program_id(0) == 0)
    def _():
        token = lax.broadcasted_iota(jnp.int32, (1, rows), 1) + me * rows
        begin = jnp.zeros((1, rows), jnp.int32)
        bound = jnp.int32(0)
        for doc in range(docs.shape[0]):
            bound = bound + docs[doc]
            begin = jnp.where(token >= bound, bound, begin)
        row = lax.broadcasted_iota(jnp.int32, (rows, rows), 0)
        for slot, shard in enumerate(slot_shards(me, hops)):
            key = row + shard * rows
            visible = (key <= token) & (key >= begin)
            bias[slot * rows : (slot + 1) * rows, :] = jnp.where(visible, 0.0, -1e30)

    hidden = bias[...]
    hidden = jnp.concatenate([hidden, hidden], axis=1)
    for sub in range(STEP):
        column = slice(sub * HDIM, (sub + 1) * HDIM)
        wide = slice(sub * GROUP * HDIM, (sub + 1) * GROUP * HDIM)
        for slot in range(slots):
            pair = moved[slot].at[0]
            k_all[sub, slot * rows : (slot + 1) * rows, :] = pair[0, :, column]
            v_all[sub, slot * rows : (slot + 1) * rows, :] = pair[1, :, column]
        queries = head_rows(q_ref[:, wide])
        gout = head_rows(gout_ref[:, wide])
        keys = k_all[sub]
        values = v_all[sub]
        for two in range(GROUP // 2):
            at = slice(2 * two * rows, (2 * two + 2) * rows)
            head = sub * GROUP + 2 * two
            lse = jnp.concatenate([lse_ref[head : head + 1, :], lse_ref[head + 1 : head + 2, :]], axis=1)
            delta = jnp.concatenate(
                [delta_ref[head : head + 1, :], delta_ref[head + 1 : head + 2, :]], axis=1
            )
            raw = contract_last(keys, queries[at])
            attn = jnp.exp2(raw * (scale * LOG2E) - lse * LOG2E + hidden)
            grad = contract_last(values, gout[at])
            prob[sub, :, at] = attn.astype(jnp.bfloat16)
            score[sub, :, at] = (attn * (grad - delta)).astype(jnp.bfloat16)
        scores = score[sub]
        grad_k = jnp.dot(scores, queries, preferred_element_type=jnp.float32) * scale
        grad_v = jnp.dot(prob[sub], gout, preferred_element_type=jnp.float32)
        for slot in range(slots):
            at = slice(slot * rows, (slot + 1) * rows)
            part = parts[slot]
            part[0, :, column] = grad_k[at].astype(part.dtype)
            part[1, :, column] = grad_v[at].astype(part.dtype)
        grad_q = contract_first(keys, scores) * scale
        for h in range(GROUP):
            gq_ref[:, (sub * GROUP + h) * HDIM : (sub * GROUP + h + 1) * HDIM] = (
                grad_q[:, h * rows : (h + 1) * rows].T.astype(jnp.bfloat16)
            )


def attend(docs, queries, grad_out, lse, delta, moved, grad_q, head, per, hops):
    rows = queries.shape[0]
    slots = 2 * hops + 1
    base = head // STEP
    wide = pl.BlockSpec((rows, STEP * GROUP * HDIM), lambda g, d: (0, base + g))
    stat = pl.BlockSpec((STEP * GROUP, rows), lambda g, d: (base + g, 0))
    both = pl.BlockSpec((2, rows, STEP * HDIM), lambda g, d: (0, 0, g))

    def held(index):
        return pl.BlockSpec((1, 2, rows, STEP * HDIM), lambda g, d: (index, 0, 0, g))

    in_specs = [wide, wide, stat, stat] + [held(index) for array, index in moved]
    operands = [docs, queries, grad_out, lse, delta] + [array for array, index in moved]
    aliases = {}
    if grad_q is not None:
        in_specs.append(pl.BlockSpec(memory_space=pl.ANY))
        operands.append(grad_q)
        aliases = {len(operands) - 1: 0}
    kinds = [jnp.float32] * (hops + 1) + [jnp.bfloat16] * hops
    out_shape = [jax.ShapeDtypeStruct(queries.shape, jnp.bfloat16)] + [
        jax.ShapeDtypeStruct((2, rows, per * HDIM), kind) for kind in kinds
    ]
    pairs = slots * rows * rows * GROUP * per
    return pl.pallas_call(
        functools.partial(attend_kernel, hops, len(aliases)),
        grid_spec=pltpu.PrefetchScalarGridSpec(
            num_scalar_prefetch=1,
            grid=(per // STEP,),
            in_specs=in_specs,
            out_specs=[wide] + [both] * slots,
            scratch_shapes=[
                pltpu.VMEM((STEP, slots * rows, HDIM), jnp.bfloat16),
                pltpu.VMEM((STEP, slots * rows, HDIM), jnp.bfloat16),
                pltpu.VMEM((slots * rows, rows), jnp.float32),
                pltpu.VMEM((STEP, slots * rows, GROUP * rows), jnp.bfloat16),
                pltpu.VMEM((STEP, slots * rows, GROUP * rows), jnp.bfloat16),
            ],
        ),
        out_shape=out_shape,
        input_output_aliases=aliases,
        compiler_params=pltpu.CompilerParams(vmem_limit_bytes=VMEM),
        cost_estimate=pl.CostEstimate(
            flops=40 * pairs * HDIM,
            bytes_accessed=per * rows * HDIM * 2 * (3 * GROUP + 6 * slots),
            transcendentals=pairs,
        ),
        name="attend",
    )(*operands)


def shards(queries, keys, values, outputs, grad_out, lse_saved, doc_lengths):
    seq = lax.axis_size("seq")
    me = lax.axis_index("seq").astype(jnp.int32)
    side = lax.rem(me, 2)
    hops = seq // 4
    def onward(hop):
        return [(s, s + 2) for s in range(2 * hop - 2, seq - 2)]

    def back(hop):
        return [(s, s - 2) for s in range(2 * hop, seq)]

    def to_odd(hop):
        return [(s, s + 1) for s in range(2 * hop, seq, 2)]

    def to_even(hop):
        return [(s + 1, s) for s in range(2 * hop, seq, 2)]

    def send(array, pairs):
        return lax.ppermute(array, "seq", pairs)

    def after(array, *others):
        return lax.optimization_barrier((array,) + others)[0]

    delta = delta_rows(outputs, grad_out)
    lse = lse_saved.T
    heads = [sum(CHUNKS[:chunk]) for chunk in range(len(CHUNKS))]
    columns = []
    for head, per in zip(heads, CHUNKS):
        at = slice(head * HDIM, (head + per) * HDIM)
        own = jnp.stack([keys[:, at], values[:, at]])
        columns.append([own, send(own, onward(1))])
        columns[-1][1], delta = lax.optimization_barrier((columns[-1][1], delta))
    for column in columns:
        for hop in range(2, hops + 1):
            column.append(send(column[-1], onward(hop)))
    arrived = []
    for chunk, column in enumerate(columns):
        edge = jnp.where(side == 0, column[0], column[hops])
        moved = [(array[None], 0) for array in column]
        if chunk == 0:
            crossed = [send(array, to_odd(1) + to_even(1)) for array in column[1:hops]]
            crossed.append(send(edge, to_odd(0) + to_even(hops)))
            moved += [(array[None], 0) for array in crossed]
        else:
            crossed = send(jnp.stack(column[1:hops] + [edge]), to_odd(0) + to_even(1))
            moved += [(crossed, hop) for hop in range(hops)]
        arrived.append(moved)

    wide, half = jnp.float32, jnp.bfloat16
    grad_q = None
    sums = []
    for chunk, (head, per) in enumerate(zip(heads, CHUNKS)):
        grad_q, *parts = attend(
            doc_lengths, queries, grad_out, lse, delta, arrived[chunk], grad_q, head, per, hops
        )
        column, crossed = parts[: hops + 1], parts[hops + 1 :]
        if chunk == len(CHUNKS) - 1:
            edge = send(crossed[-1], to_odd(hops) + to_even(0))
            crossed = [send(part, to_odd(hop + 1) + to_even(hop + 1)) for hop, part in enumerate(crossed[:-1])]
        else:
            crossed = send(jnp.stack(crossed), to_odd(1) + to_even(0))
            crossed, edge = [crossed[hop] for hop in range(hops - 1)], crossed[-1]
        edge = edge.astype(wide)
        total = column[hops] + jnp.where(side == 1, edge, 0.0)
        for hop in range(hops - 1, -1, -1):
            far = send(total.astype(half), back(hop + 1)).astype(wide)
            if hop:
                total = column[hop] + crossed[hop - 1].astype(wide) + far
        total = column[0] + jnp.where(side == 0, edge, 0.0) + far
        sums.append(total.astype(half))
    grad_keys = jnp.concatenate([total[0] for total in sums], axis=1)
    grad_values = jnp.concatenate([total[1] for total in sums], axis=1)
    return (grad_q, grad_keys, grad_values)


def solution(mesh):
    rows = P(("packs", "seq"), None)
    return jax.shard_map(
        shards,
        mesh=mesh,
        in_specs=(rows, rows, rows, rows, rows, rows, P("packs")),
        out_specs=(rows, rows, rows),
        check_vma=False,
    )
```

```python
import functools

import jax
import jax.numpy as jnp
from jax import lax
from jax.experimental import pallas as pl
from jax.experimental.pallas import tpu as pltpu
from jax.sharding import PartitionSpec as P

HEADS = 64
KVH = 8
HDIM = 128
GROUP = HEADS // KVH
CHUNKS = (4, 4)
STEP = 2
LOG2E = 1.4426950408889634
VMEM = 60 * 1024 * 1024


def contract_last(first, second):
    return lax.dot_general(
        first, second, (((1,), (1,)), ((), ())), preferred_element_type=jnp.float32
    )


def contract_first(first, second):
    return lax.dot_general(
        first, second, (((0,), (0,)), ((), ())), preferred_element_type=jnp.float32
    )


def head_rows(block):
    return jnp.concatenate(
        [block[:, h * HDIM : (h + 1) * HDIM] for h in range(GROUP)], axis=0
    )


def delta_kernel(out_ref, gout_ref, delta_ref):
    rows = out_ref.shape[0]
    wide = GROUP * HDIM
    first = lax.broadcasted_iota(jnp.int32, (wide, HDIM), 1) * HDIM
    row = lax.broadcasted_iota(jnp.int32, (wide, HDIM), 0)
    ones = jnp.where((row >= first) & (row < first + HDIM), 1.0, 0.0).astype(jnp.bfloat16)
    for group in range(out_ref.shape[1] // wide):
        at = slice(group * wide, (group + 1) * wide)
        product = out_ref[:, at].astype(jnp.float32) * gout_ref[:, at].astype(jnp.float32)
        high = product.astype(jnp.bfloat16)
        low = (product - high.astype(jnp.float32)).astype(jnp.bfloat16)
        total = jnp.dot(high, ones, preferred_element_type=jnp.float32)
        total += jnp.dot(low, ones, preferred_element_type=jnp.float32)
        delta_ref[group * GROUP : (group + 1) * GROUP, :] = total.T[:GROUP]


def delta_rows(outputs, grad_out):
    rows = outputs.shape[0]
    steps = 4
    return pl.pallas_call(
        delta_kernel,
        grid=(steps,),
        in_specs=[pl.BlockSpec((rows, HEADS * HDIM // steps), lambda g: (0, g))] * 2,
        out_specs=pl.BlockSpec((HEADS // steps, rows), lambda g: (g, 0)),
        out_shape=jax.ShapeDtypeStruct((HEADS, rows), jnp.float32),
        compiler_params=pltpu.CompilerParams(vmem_limit_bytes=VMEM),
        cost_estimate=pl.CostEstimate(
            flops=4 * rows * HEADS * HDIM * HDIM,
            bytes_accessed=8 * rows * HEADS * HDIM,
            transcendentals=0,
        ),
        name="delta",
    )(outputs, grad_out)


def slot_shards(me, hops):
    side = lax.rem(me, 2)
    found = [me - 2 * hop for hop in range(hops + 1)]
    found += [me - 2 * hop + 1 - 2 * side for hop in range(1, hops)]
    found.append(jnp.where(side == 1, me - 1, me - 2 * hops + 1))
    return found


def attend_kernel(hops, joined, aliased, docs, q_ref, gout_ref, lse_ref, delta_ref, *refs):
    slots = 2 * hops + 1
    moved, refs = refs[:slots], refs[slots + aliased :]
    gq_ref, refs = refs[0], refs[1:]
    if joined:
        parts = refs[: hops + 1] + tuple(refs[hops + 1].at[hop] for hop in range(hops))
    else:
        parts = refs[:slots]
    k_all, v_all, bias, prob, score = refs[-5:]
    rows = q_ref.shape[0]
    scale = 1.0 / HDIM**0.5
    me = lax.axis_index("seq")

    @pl.when(pl.program_id(0) == 0)
    def _():
        token = lax.broadcasted_iota(jnp.int32, (1, rows), 1) + me * rows
        begin = jnp.zeros((1, rows), jnp.int32)
        bound = jnp.int32(0)
        for doc in range(docs.shape[0]):
            bound = bound + docs[doc]
            begin = jnp.where(token >= bound, bound, begin)
        row = lax.broadcasted_iota(jnp.int32, (rows, rows), 0)
        for slot, shard in enumerate(slot_shards(me, hops)):
            key = row + shard * rows
            visible = (key <= token) & (key >= begin)
            bias[slot * rows : (slot + 1) * rows, :] = jnp.where(visible, 0.0, -1e30)

    hidden = bias[...]
    hidden = jnp.concatenate([hidden, hidden], axis=1)
    for sub in range(STEP):
        column = slice(sub * HDIM, (sub + 1) * HDIM)
        wide = slice(sub * GROUP * HDIM, (sub + 1) * GROUP * HDIM)
        for slot in range(slots):
            pair = moved[slot].at[0]
            k_all[sub, slot * rows : (slot + 1) * rows, :] = pair[0, :, column]
            v_all[sub, slot * rows : (slot + 1) * rows, :] = pair[1, :, column]
        queries = head_rows(q_ref[:, wide])
        gout = head_rows(gout_ref[:, wide])
        keys = k_all[sub]
        values = v_all[sub]
        for two in range(GROUP // 2):
            at = slice(2 * two * rows, (2 * two + 2) * rows)
            head = sub * GROUP + 2 * two
            lse = jnp.concatenate([lse_ref[head : head + 1, :], lse_ref[head + 1 : head + 2, :]], axis=1)
            delta = jnp.concatenate(
                [delta_ref[head : head + 1, :], delta_ref[head + 1 : head + 2, :]], axis=1
            )
            raw = contract_last(keys, queries[at])
            attn = jnp.exp2(raw * (scale * LOG2E) - lse * LOG2E + hidden)
            grad = contract_last(values, gout[at])
            prob[sub, :, at] = attn.astype(jnp.bfloat16)
            score[sub, :, at] = (attn * (grad - delta)).astype(jnp.bfloat16)
        scores = score[sub]
        grad_k = jnp.dot(scores, queries, preferred_element_type=jnp.float32) * scale
        grad_v = jnp.dot(prob[sub], gout, preferred_element_type=jnp.float32)
        for slot in range(slots):
            at = slice(slot * rows, (slot + 1) * rows)
            part = parts[slot]
            part[0, :, column] = grad_k[at].astype(part.dtype)
            part[1, :, column] = grad_v[at].astype(part.dtype)
        grad_q = (contract_first(scores, keys) * scale).astype(jnp.bfloat16)
        for h in range(GROUP):
            gq_ref[:, (sub * GROUP + h) * HDIM : (sub * GROUP + h + 1) * HDIM] = (
                grad_q[h * rows : (h + 1) * rows]
            )


def attend(docs, queries, grad_out, lse, delta, moved, grad_q, head, per, hops, joined):
    rows = queries.shape[0]
    slots = 2 * hops + 1
    base = head // STEP
    wide = pl.BlockSpec((rows, STEP * GROUP * HDIM), lambda g, d: (0, base + g))
    stat = pl.BlockSpec((STEP * GROUP, rows), lambda g, d: (base + g, 0))
    both = pl.BlockSpec((2, rows, STEP * HDIM), lambda g, d: (0, 0, g))

    def held(index):
        return pl.BlockSpec((1, 2, rows, STEP * HDIM), lambda g, d: (index, 0, 0, g))

    in_specs = [wide, wide, stat, stat] + [held(index) for array, index in moved]
    operands = [docs, queries, grad_out, lse, delta] + [array for array, index in moved]
    aliases = {}
    if grad_q is not None:
        in_specs.append(pl.BlockSpec(memory_space=pl.ANY))
        operands.append(grad_q)
        aliases = {len(operands) - 1: 0}
    out_shape = [jax.ShapeDtypeStruct(queries.shape, jnp.bfloat16)]
    out_shape += [jax.ShapeDtypeStruct((2, rows, per * HDIM), jnp.float32)] * (hops + 1)
    if joined:
        out_shape += [jax.ShapeDtypeStruct((hops, 2, rows, per * HDIM), jnp.bfloat16)]
        crossing = [pl.BlockSpec((hops, 2, rows, STEP * HDIM), lambda g, d: (0, 0, 0, g))]
    else:
        out_shape += [jax.ShapeDtypeStruct((2, rows, per * HDIM), jnp.bfloat16)] * hops
        crossing = [both] * hops
    pairs = slots * rows * rows * GROUP * per
    return pl.pallas_call(
        functools.partial(attend_kernel, hops, joined, len(aliases)),
        grid_spec=pltpu.PrefetchScalarGridSpec(
            num_scalar_prefetch=1,
            grid=(per // STEP,),
            in_specs=in_specs,
            out_specs=[wide] + [both] * (hops + 1) + crossing,
            scratch_shapes=[
                pltpu.VMEM((STEP, slots * rows, HDIM), jnp.bfloat16),
                pltpu.VMEM((STEP, slots * rows, HDIM), jnp.bfloat16),
                pltpu.VMEM((slots * rows, rows), jnp.float32),
                pltpu.VMEM((STEP, slots * rows, GROUP * rows), jnp.bfloat16),
                pltpu.VMEM((STEP, slots * rows, GROUP * rows), jnp.bfloat16),
            ],
        ),
        out_shape=out_shape,
        input_output_aliases=aliases,
        compiler_params=pltpu.CompilerParams(vmem_limit_bytes=VMEM),
        cost_estimate=pl.CostEstimate(
            flops=40 * pairs * HDIM,
            bytes_accessed=per * rows * HDIM * 2 * (3 * GROUP + 6 * slots),
            transcendentals=pairs,
        ),
        name="attend",
    )(*operands)


def shards(queries, keys, values, outputs, grad_out, lse_saved, doc_lengths):
    seq = lax.axis_size("seq")
    me = lax.axis_index("seq").astype(jnp.int32)
    side = lax.rem(me, 2)
    hops = seq // 4
    def onward(hop):
        return [(s, s + 2) for s in range(2 * hop - 2, seq - 2)]

    def back(hop):
        return [(s, s - 2) for s in range(2 * hop, seq)]

    def to_odd(hop):
        return [(s, s + 1) for s in range(2 * hop, seq, 2)]

    def to_even(hop):
        return [(s + 1, s) for s in range(2 * hop, seq, 2)]

    def send(array, pairs):
        return lax.ppermute(array, "seq", pairs)

    def after(array, *others):
        return lax.optimization_barrier((array,) + others)[0]

    delta = delta_rows(outputs, grad_out)
    lse = lse_saved.T
    heads = [sum(CHUNKS[:chunk]) for chunk in range(len(CHUNKS))]
    columns = []
    for head, per in zip(heads, CHUNKS):
        at = slice(head * HDIM, (head + per) * HDIM)
        own = jnp.stack([keys[:, at], values[:, at]])
        columns.append([own, send(own, onward(1))])
        columns[-1][1], delta = lax.optimization_barrier((columns[-1][1], delta))
    others = []
    for chunk, column in enumerate(columns):
        for hop in range(2, hops + 1):
            column.append(send(after(column[-1], *others), onward(hop)))
        if chunk == 0:
            others = [send(array, to_odd(1) + to_even(1)) for array in column[1:hops]]
            first_crossed = others[:]
            others.append(column[hops])
    arrived = []
    for chunk, column in enumerate(columns):
        edge = jnp.where(side == 0, column[0], column[hops])
        moved = [(array[None], 0) for array in column]
        if chunk == 0:
            crossed = first_crossed + [send(edge, to_odd(0) + to_even(hops))]
            moved += [(array[None], 0) for array in crossed]
        else:
            crossed = send(jnp.stack(column[1:hops] + [edge]), to_odd(0) + to_even(1))
            moved += [(crossed, hop) for hop in range(hops)]
        arrived.append(moved)

    wide, half = jnp.float32, jnp.bfloat16
    grad_q = None
    sums = []
    for chunk, (head, per) in enumerate(zip(heads, CHUNKS)):
        joined = chunk < len(CHUNKS) - 1
        grad_q, *parts = attend(
            doc_lengths, queries, grad_out, lse, delta, arrived[chunk], grad_q, head, per, hops, joined
        )
        column, crossed = parts[: hops + 1], parts[hops + 1 :]
        if joined:
            crossed = send(crossed[0], to_odd(1) + to_even(0))
            edge = crossed[hops - 1]
        else:
            edge = send(crossed[-1], to_odd(hops) + to_even(0))
            crossed = [send(crossed[hop - 1], to_odd(hop) + to_even(hop)) for hop in range(1, hops)]
        edge = edge.astype(wide)
        total = column[hops] + jnp.where(side == 1, edge, 0.0)
        for hop in range(hops - 1, -1, -1):
            far = send(total.astype(half), back(hop + 1)).astype(wide)
            if hop:
                total = column[hop] + crossed[hop - 1].astype(wide) + far
        total = column[0] + jnp.where(side == 0, edge, 0.0) + far
        sums.append(total.astype(half))
    grad_keys = jnp.concatenate([total[0] for total in sums], axis=1)
    grad_values = jnp.concatenate([total[1] for total in sums], axis=1)
    return (grad_q, grad_keys, grad_values)


def solution(mesh):
    rows = P(("packs", "seq"), None)
    return jax.shard_map(
        shards,
        mesh=mesh,
        in_specs=(rows, rows, rows, rows, rows, rows, P("packs")),
        out_specs=(rows, rows, rows),
        check_vma=False,
    )
```

```python
import functools

import jax
import jax.numpy as jnp
from jax import lax
from jax.experimental import pallas as pl
from jax.experimental.pallas import tpu as pltpu
from jax.sharding import PartitionSpec as P

HEADS = 64
KVH = 8
HDIM = 128
GROUP = HEADS // KVH
CHUNKS = (5, 3)
STEP = 1
VMEM = 60 * 1024 * 1024


def contract_last(first, second):
    return lax.dot_general(
        first, second, (((1,), (1,)), ((), ())), preferred_element_type=jnp.float32
    )


def contract_first(first, second):
    return lax.dot_general(
        first, second, (((0,), (0,)), ((), ())), preferred_element_type=jnp.float32
    )


def head_rows(block):
    return jnp.concatenate(
        [block[:, h * HDIM : (h + 1) * HDIM] for h in range(GROUP)], axis=0
    )


def delta_kernel(out_ref, gout_ref, delta_ref):
    rows = out_ref.shape[0]
    wide = GROUP * HDIM
    first = lax.broadcasted_iota(jnp.int32, (wide, HDIM), 1) * HDIM
    row = lax.broadcasted_iota(jnp.int32, (wide, HDIM), 0)
    ones = jnp.where((row >= first) & (row < first + HDIM), 1.0, 0.0).astype(jnp.bfloat16)
    for group in range(out_ref.shape[1] // wide):
        at = slice(group * wide, (group + 1) * wide)
        product = out_ref[:, at].astype(jnp.float32) * gout_ref[:, at].astype(jnp.float32)
        high = product.astype(jnp.bfloat16)
        low = (product - high.astype(jnp.float32)).astype(jnp.bfloat16)
        total = jnp.dot(high, ones, preferred_element_type=jnp.float32)
        total += jnp.dot(low, ones, preferred_element_type=jnp.float32)
        delta_ref[group * GROUP : (group + 1) * GROUP, :] = total.T[:GROUP]


def delta_rows(outputs, grad_out):
    rows = outputs.shape[0]
    steps = 4
    return pl.pallas_call(
        delta_kernel,
        grid=(steps,),
        in_specs=[pl.BlockSpec((rows, HEADS * HDIM // steps), lambda g: (0, g))] * 2,
        out_specs=pl.BlockSpec((HEADS // steps, rows), lambda g: (g, 0)),
        out_shape=jax.ShapeDtypeStruct((HEADS, rows), jnp.float32),
        compiler_params=pltpu.CompilerParams(vmem_limit_bytes=VMEM),
        cost_estimate=pl.CostEstimate(
            flops=4 * rows * HEADS * HDIM * HDIM,
            bytes_accessed=8 * rows * HEADS * HDIM,
            transcendentals=0,
        ),
        name="delta",
    )(outputs, grad_out)


def slot_shards(me, hops):
    side = lax.rem(me, 2)
    found = [me - 2 * hop for hop in range(hops + 1)]
    found += [me - 2 * hop + 1 - 2 * side for hop in range(1, hops)]
    found.append(jnp.where(side == 1, me - 1, me - 2 * hops + 1))
    return found


def attend_kernel(hops, joined, aliased, docs, q_ref, gout_ref, lse_ref, delta_ref, *refs):
    slots = 2 * hops + 1
    moved, refs = refs[:slots], refs[slots + aliased :]
    gq_ref, refs = refs[0], refs[1:]
    if joined:
        parts = refs[: hops + 1] + tuple(refs[hops + 1].at[hop] for hop in range(hops))
    else:
        parts = refs[:slots]
    k_all, v_all, bias, prob, score = refs[-5:]
    rows = q_ref.shape[0]
    scale = 1.0 / HDIM**0.5
    me = lax.axis_index("seq")

    @pl.when(pl.program_id(0) == 0)
    def _():
        token = lax.broadcasted_iota(jnp.int32, (1, rows), 1) + me * rows
        begin = jnp.zeros((1, rows), jnp.int32)
        bound = jnp.int32(0)
        for doc in range(docs.shape[0]):
            bound = bound + docs[doc]
            begin = jnp.where(token >= bound, bound, begin)
        row = lax.broadcasted_iota(jnp.int32, (rows, rows), 0)
        for slot, shard in enumerate(slot_shards(me, hops)):
            key = row + shard * rows
            visible = (key <= token) & (key >= begin)
            bias[slot * rows : (slot + 1) * rows, :] = jnp.where(visible, 0.0, -1e30)

    for sub in range(STEP):
        column = slice(sub * HDIM, (sub + 1) * HDIM)
        wide = slice(sub * GROUP * HDIM, (sub + 1) * GROUP * HDIM)
        for slot in range(slots):
            pair = moved[slot].at[0]
            k_all[sub, slot * rows : (slot + 1) * rows, :] = pair[0, :, column]
            v_all[sub, slot * rows : (slot + 1) * rows, :] = pair[1, :, column]
        queries = head_rows(q_ref[:, wide])
        gout = head_rows(gout_ref[:, wide])
        keys = k_all[sub]
        values = v_all[sub]
        for two in range(GROUP // 2):
            at = slice(2 * two * rows, (2 * two + 2) * rows)
            head = sub * GROUP + 2 * two
            lse = jnp.concatenate([lse_ref[head : head + 1, :], lse_ref[head + 1 : head + 2, :]], axis=1)
            delta = jnp.concatenate(
                [delta_ref[head : head + 1, :], delta_ref[head + 1 : head + 2, :]], axis=1
            )
            for slot in range(slots):
                here = slice(slot * rows, (slot + 1) * rows)
                hidden = bias[here, :]
                hidden = jnp.concatenate([hidden, hidden], axis=1)
                raw = contract_last(keys[here], queries[at])
                attn = jnp.exp(raw * scale - lse + hidden)
                grad = contract_last(values[here], gout[at])
                prob[sub, here, at] = attn.astype(jnp.bfloat16)
                score[sub, here, at] = (attn * (grad - delta)).astype(jnp.bfloat16)
        scores = score[sub]
        grad_k = jnp.dot(scores, queries, preferred_element_type=jnp.float32) * scale
        grad_v = jnp.dot(prob[sub], gout, preferred_element_type=jnp.float32)
        for slot in range(slots):
            at = slice(slot * rows, (slot + 1) * rows)
            part = parts[slot]
            part[0, :, column] = grad_k[at].astype(part.dtype)
            part[1, :, column] = grad_v[at].astype(part.dtype)
        grad_q = (contract_first(keys, scores) * scale).astype(jnp.bfloat16)
        for h in range(GROUP):
            gq_ref[:, (sub * GROUP + h) * HDIM : (sub * GROUP + h + 1) * HDIM] = (
                grad_q[:, h * rows : (h + 1) * rows].T
            )


def attend(docs, queries, grad_out, lse, delta, moved, grad_q, head, per, hops, joined):
    rows = queries.shape[0]
    slots = 2 * hops + 1
    base = head // STEP
    wide = pl.BlockSpec((rows, STEP * GROUP * HDIM), lambda g, d: (0, base + g))
    stat = pl.BlockSpec((STEP * GROUP, rows), lambda g, d: (base + g, 0))
    both = pl.BlockSpec((2, rows, STEP * HDIM), lambda g, d: (0, 0, g))

    def held(index):
        return pl.BlockSpec((1, 2, rows, STEP * HDIM), lambda g, d: (index, 0, 0, g))

    in_specs = [wide, wide, stat, stat] + [held(index) for array, index in moved]
    operands = [docs, queries, grad_out, lse, delta] + [array for array, index in moved]
    aliases = {}
    if grad_q is not None:
        in_specs.append(pl.BlockSpec(memory_space=pl.ANY))
        operands.append(grad_q)
        aliases = {len(operands) - 1: 0}
    out_shape = [jax.ShapeDtypeStruct(queries.shape, jnp.bfloat16)]
    kinds = [jnp.float32] + [jnp.bfloat16] * hops
    out_shape += [jax.ShapeDtypeStruct((2, rows, per * HDIM), kind) for kind in kinds]
    if joined:
        out_shape += [jax.ShapeDtypeStruct((hops, 2, rows, per * HDIM), jnp.bfloat16)]
        crossing = [pl.BlockSpec((hops, 2, rows, STEP * HDIM), lambda g, d: (0, 0, 0, g))]
    else:
        out_shape += [jax.ShapeDtypeStruct((2, rows, per * HDIM), jnp.bfloat16)] * hops
        crossing = [both] * hops
    pairs = slots * rows * rows * GROUP * per
    return pl.pallas_call(
        functools.partial(attend_kernel, hops, joined, len(aliases)),
        grid_spec=pltpu.PrefetchScalarGridSpec(
            num_scalar_prefetch=1,
            grid=(per // STEP,),
            in_specs=in_specs,
            out_specs=[wide] + [both] * (hops + 1) + crossing,
            scratch_shapes=[
                pltpu.VMEM((STEP, slots * rows, HDIM), jnp.bfloat16),
                pltpu.VMEM((STEP, slots * rows, HDIM), jnp.bfloat16),
                pltpu.VMEM((slots * rows, rows), jnp.float32),
                pltpu.VMEM((STEP, slots * rows, GROUP * rows), jnp.bfloat16),
                pltpu.VMEM((STEP, slots * rows, GROUP * rows), jnp.bfloat16),
            ],
        ),
        out_shape=out_shape,
        input_output_aliases=aliases,
        compiler_params=pltpu.CompilerParams(vmem_limit_bytes=VMEM),
        cost_estimate=pl.CostEstimate(
            flops=40 * pairs * HDIM,
            bytes_accessed=per * rows * HDIM * 2 * (3 * GROUP + 6 * slots),
            transcendentals=pairs,
        ),
        name="attend",
    )(*operands)


def shards(queries, keys, values, outputs, grad_out, lse_saved, doc_lengths):
    seq = lax.axis_size("seq")
    me = lax.axis_index("seq").astype(jnp.int32)
    side = lax.rem(me, 2)
    hops = seq // 4
    def onward(hop):
        return [(s, s + 2) for s in range(2 * hop - 2, seq - 2)]

    def back(hop):
        return [(s, s - 2) for s in range(2 * hop, seq)]

    def to_odd(hop):
        return [(s, s + 1) for s in range(2 * hop, seq, 2)]

    def to_even(hop):
        return [(s + 1, s) for s in range(2 * hop, seq, 2)]

    def send(array, pairs):
        return lax.ppermute(array, "seq", pairs)

    def after(array, *others):
        return lax.optimization_barrier((array,) + others)[0]

    delta = delta_rows(outputs, grad_out)
    lse = lse_saved.T
    heads = [sum(CHUNKS[:chunk]) for chunk in range(len(CHUNKS))]
    columns = []
    for head, per in zip(heads, CHUNKS):
        at = slice(head * HDIM, (head + per) * HDIM)
        own = jnp.stack([keys[:, at], values[:, at]])
        columns.append([own, send(own, onward(1))])
        columns[-1][1], delta = lax.optimization_barrier((columns[-1][1], delta))
    others = []
    for chunk, column in enumerate(columns):
        for hop in range(2, hops + 1):
            column.append(send(after(column[-1], *others), onward(hop)))
        if chunk == 0:
            others = [send(array, to_odd(1) + to_even(1)) for array in column[1:hops]]
            first_crossed = others[:]
            others.append(column[hops])
    arrived = []
    for chunk, column in enumerate(columns):
        edge = jnp.where(side == 0, column[0], column[hops])
        moved = [(array[None], 0) for array in column]
        if chunk == 0:
            crossed = first_crossed + [send(edge, to_odd(0) + to_even(hops))]
            moved += [(array[None], 0) for array in crossed]
        else:
            crossed = send(jnp.stack(column[1:hops] + [edge]), to_odd(0) + to_even(1))
            moved += [(crossed, hop) for hop in range(hops)]
        arrived.append(moved)

    wide, half = jnp.float32, jnp.bfloat16
    grad_q = None
    sums = []
    for chunk, (head, per) in enumerate(zip(heads, CHUNKS)):
        joined = chunk < len(CHUNKS) - 1
        grad_q, *parts = attend(
            doc_lengths, queries, grad_out, lse, delta, arrived[chunk], grad_q, head, per, hops, joined
        )
        column, crossed = parts[: hops + 1], parts[hops + 1 :]
        if joined:
            crossed = send(crossed[0], to_odd(1) + to_even(0))
            edge = crossed[hops - 1]
        else:
            edge = send(crossed[-1], to_odd(hops) + to_even(0))
            crossed = [send(crossed[hop - 1], to_odd(hop) + to_even(hop)) for hop in range(1, hops)]
        edge = edge.astype(wide)
        total = column[hops].astype(wide) + jnp.where(side == 1, edge, 0.0)
        for hop in range(hops - 1, -1, -1):
            far = send(total.astype(half), back(hop + 1)).astype(wide)
            if hop:
                total = column[hop].astype(wide) + crossed[hop - 1].astype(wide) + far
        total = column[0] + jnp.where(side == 0, edge, 0.0) + far
        sums.append(total.astype(half))
    grad_keys = jnp.concatenate([total[0] for total in sums], axis=1)
    grad_values = jnp.concatenate([total[1] for total in sums], axis=1)
    return (grad_q, grad_keys, grad_values)


def solution(mesh):
    rows = P(("packs", "seq"), None)
    return jax.shard_map(
        shards,
        mesh=mesh,
        in_specs=(rows, rows, rows, rows, rows, rows, P("packs")),
        out_specs=(rows, rows, rows),
        check_vma=False,
    )
```

```python
import functools

import jax
import jax.numpy as jnp
from jax import lax
from jax.experimental import pallas as pl
from jax.experimental.pallas import tpu as pltpu
from jax.sharding import PartitionSpec as P

HEADS = 64
KVH = 8
HDIM = 128
GROUP = HEADS // KVH
CHUNKS = (4, 4)
VMEM = 28 * 1024 * 1024


def contract_last(first, second):
    return lax.dot_general(
        first, second, (((1,), (1,)), ((), ())), preferred_element_type=jnp.float32
    )


def contract_first(first, second):
    return lax.dot_general(
        first, second, (((0,), (0,)), ((), ())), preferred_element_type=jnp.float32
    )


def head_rows(block):
    return jnp.concatenate(
        [block[:, h * HDIM : (h + 1) * HDIM] for h in range(GROUP)], axis=0
    )


def delta_kernel(out_ref, gout_ref, delta_ref):
    rows = out_ref.shape[0]
    wide = GROUP * HDIM
    first = lax.broadcasted_iota(jnp.int32, (wide, HDIM), 1) * HDIM
    row = lax.broadcasted_iota(jnp.int32, (wide, HDIM), 0)
    ones = jnp.where((row >= first) & (row < first + HDIM), 1.0, 0.0).astype(jnp.bfloat16)
    for group in range(out_ref.shape[1] // wide):
        at = slice(group * wide, (group + 1) * wide)
        product = out_ref[:, at].astype(jnp.float32) * gout_ref[:, at].astype(jnp.float32)
        high = product.astype(jnp.bfloat16)
        low = (product - high.astype(jnp.float32)).astype(jnp.bfloat16)
        total = jnp.dot(high, ones, preferred_element_type=jnp.float32)
        total += jnp.dot(low, ones, preferred_element_type=jnp.float32)
        delta_ref[group * GROUP : (group + 1) * GROUP, :] = total.T[:GROUP]


def delta_rows(outputs, grad_out):
    rows = outputs.shape[0]
    steps = 4
    return pl.pallas_call(
        delta_kernel,
        grid=(steps,),
        in_specs=[pl.BlockSpec((rows, HEADS * HDIM // steps), lambda g: (0, g))] * 2,
        out_specs=pl.BlockSpec((HEADS // steps, rows), lambda g: (g, 0)),
        out_shape=jax.ShapeDtypeStruct((HEADS, rows), jnp.float32),
        compiler_params=pltpu.CompilerParams(vmem_limit_bytes=VMEM),
        cost_estimate=pl.CostEstimate(
            flops=4 * rows * HEADS * HDIM * HDIM,
            bytes_accessed=8 * rows * HEADS * HDIM,
            transcendentals=0,
        ),
        name="delta",
    )(outputs, grad_out)


def slot_shards(me, hops):
    side = lax.rem(me, 2)
    found = [me - 2 * hop for hop in range(hops + 1)]
    found += [me - 2 * hop + 1 - 2 * side for hop in range(1, hops)]
    found.append(jnp.where(side == 1, me - 1, me - 2 * hops + 1))
    return found


def attend_kernel(hops, joined, first, places, docs, q_ref, gout_ref, lse_ref, delta_ref, *refs):
    slots = 2 * hops + 1
    moved, refs = refs[:slots], refs[slots:]
    gq_ref, refs = refs[0], refs[1:]
    if joined:
        parts = refs[: hops + 1] + tuple(refs[hops + 1].at[hop] for hop in range(hops))
    else:
        parts = refs[:slots]
    k_all, v_all, bias, prob, score = refs[-5:]
    rows = q_ref.shape[0]
    scale = 1.0 / HDIM**0.5
    me = lax.axis_index("seq")

    token = lax.broadcasted_iota(jnp.int32, (1, rows), 1) + me * rows
    begin = jnp.zeros((1, rows), jnp.int32)
    bound = jnp.int32(0)
    for doc in range(docs.shape[0]):
        bound = bound + docs[doc]
        begin = jnp.where(token >= bound, bound, begin)
    row = lax.broadcasted_iota(jnp.int32, (rows, rows), 0)
    for slot, shard in enumerate(slot_shards(me, hops)):
        key = row + shard * rows
        visible = (key <= token) & (key >= begin)
        bias[slot * rows : (slot + 1) * rows, :] = jnp.where(visible, 0.0, -1e30)

    @pl.loop(0, moved[0].shape[-1] // HDIM)
    def _(index):
        column = pl.ds(pl.multiple_of(index * HDIM, HDIM), HDIM)
        wide = pl.ds(pl.multiple_of((first + index) * GROUP * HDIM, GROUP * HDIM), GROUP * HDIM)
        stat = pl.ds(pl.multiple_of((first + index) * GROUP, GROUP), GROUP)
        for slot in range(slots):
            here = slice(slot * rows, (slot + 1) * rows)
            k_all[here, :] = moved[slot][places[slot], 0, :, column]
            v_all[here, :] = moved[slot][places[slot], 1, :, column]
        queries = head_rows(q_ref[:, wide])
        gout = head_rows(gout_ref[:, wide])
        lses = lse_ref[stat, :]
        deltas = delta_ref[stat, :]
        keys = k_all[...]
        values = v_all[...]
        hidden = bias[...]
        hidden = jnp.concatenate([hidden, hidden], axis=1)
        for two in range(GROUP // 2):
            at = slice(2 * two * rows, (2 * two + 2) * rows)
            lse = jnp.concatenate([lses[2 * two : 2 * two + 1], lses[2 * two + 1 : 2 * two + 2]], axis=1)
            delta = jnp.concatenate(
                [deltas[2 * two : 2 * two + 1], deltas[2 * two + 1 : 2 * two + 2]], axis=1
            )
            raw = contract_last(keys, queries[at])
            attn = jnp.exp(raw * scale - lse + hidden)
            grad = contract_last(values, gout[at])
            prob[:, at] = attn.astype(jnp.bfloat16)
            score[:, at] = (attn * (grad - delta)).astype(jnp.bfloat16)
        scores = score[...]
        grad_k = jnp.dot(scores, queries, preferred_element_type=jnp.float32) * scale
        grad_v = jnp.dot(prob[...], gout, preferred_element_type=jnp.float32)
        for slot in range(slots):
            here = slice(slot * rows, (slot + 1) * rows)
            part = parts[slot]
            part[0, :, column] = grad_k[here].astype(part.dtype)
            part[1, :, column] = grad_v[here].astype(part.dtype)
        grad_q = (contract_first(keys, scores) * scale).astype(jnp.bfloat16)
        mine = pl.ds(pl.multiple_of(index * GROUP * HDIM, GROUP * HDIM), GROUP * HDIM)
        gq_ref[:, mine] = jnp.concatenate(
            [grad_q[:, h * rows : (h + 1) * rows].T for h in range(GROUP)], axis=1
        )


def attend(docs, queries, grad_out, lse, delta, moved, head, per, hops, joined):
    rows = queries.shape[0]
    slots = 2 * hops + 1
    local = pl.BlockSpec(memory_space=pltpu.VMEM)
    operands = [docs, queries, grad_out, lse, delta] + [array for array, index in moved]
    out_shape = [jax.ShapeDtypeStruct((rows, per * GROUP * HDIM), jnp.bfloat16)]
    kinds = [jnp.float32] + [jnp.bfloat16] * hops
    out_shape += [jax.ShapeDtypeStruct((2, rows, per * HDIM), kind) for kind in kinds]
    if joined:
        out_shape += [jax.ShapeDtypeStruct((hops, 2, rows, per * HDIM), jnp.bfloat16)]
    else:
        out_shape += [jax.ShapeDtypeStruct((2, rows, per * HDIM), jnp.bfloat16)] * hops
    pairs = slots * rows * rows * GROUP * per
    places = [index for array, index in moved]
    return pl.pallas_call(
        functools.partial(attend_kernel, hops, joined, head, places),
        in_specs=[pl.BlockSpec(memory_space=pltpu.SMEM)] + [local] * (len(operands) - 1),
        out_specs=[local] * len(out_shape),
        scratch_shapes=[
            pltpu.VMEM((slots * rows, HDIM), jnp.bfloat16),
            pltpu.VMEM((slots * rows, HDIM), jnp.bfloat16),
            pltpu.VMEM((slots * rows, rows), jnp.float32),
            pltpu.VMEM((slots * rows, GROUP * rows), jnp.bfloat16),
            pltpu.VMEM((slots * rows, GROUP * rows), jnp.bfloat16),
        ],
        out_shape=out_shape,
        compiler_params=pltpu.CompilerParams(vmem_limit_bytes=VMEM),
        cost_estimate=pl.CostEstimate(
            flops=40 * pairs * HDIM,
            bytes_accessed=per * rows * HDIM * 2 * (3 * GROUP + 6 * slots),
            transcendentals=pairs,
        ),
        name="attend",
    )(*operands)


def shards(queries, keys, values, outputs, grad_out, lse_saved, doc_lengths):
    seq = lax.axis_size("seq")
    me = lax.axis_index("seq").astype(jnp.int32)
    side = lax.rem(me, 2)
    hops = seq // 4
    def onward(hop):
        return [(s, s + 2) for s in range(2 * hop - 2, seq - 2)]

    def back(hop):
        return [(s, s - 2) for s in range(2 * hop, seq)]

    def to_odd(hop):
        return [(s, s + 1) for s in range(2 * hop, seq, 2)]

    def to_even(hop):
        return [(s + 1, s) for s in range(2 * hop, seq, 2)]

    def send(array, pairs):
        return lax.ppermute(array, "seq", pairs)

    def after(array, *others):
        return lax.optimization_barrier((array,) + others)[0]

    delta = delta_rows(outputs, grad_out)
    lse = lse_saved.T
    heads = [sum(CHUNKS[:chunk]) for chunk in range(len(CHUNKS))]
    columns = []
    for head, per in zip(heads, CHUNKS):
        at = slice(head * HDIM, (head + per) * HDIM)
        own = jnp.stack([keys[:, at], values[:, at]])
        columns.append([own, send(own, onward(1))])
        columns[-1][1], delta = lax.optimization_barrier((columns[-1][1], delta))
    others = []
    for chunk, column in enumerate(columns):
        for hop in range(2, hops + 1):
            column.append(send(after(column[-1], *others), onward(hop)))
        if chunk == 0:
            others = [send(array, to_odd(1) + to_even(1)) for array in column[1:hops]]
            first_crossed = others[:]
            others.append(column[hops])
    arrived = []
    for chunk, column in enumerate(columns):
        edge = jnp.where(side == 0, column[0], column[hops])
        moved = [(array[None], 0) for array in column]
        if chunk == 0:
            crossed = first_crossed + [send(edge, to_odd(0) + to_even(hops))]
            moved += [(array[None], 0) for array in crossed]
        else:
            joint = jnp.stack(column[1:hops] + [edge])
            crossed = send(joint, to_odd(0) + to_even(1))
            moved += [(crossed, hop) for hop in range(hops)]
            arrived[0][-1] = (after(arrived[0][-1][0], joint), 0)
        arrived.append(moved)

    wide, half = jnp.float32, jnp.bfloat16
    grads_q, sums, outputs_of = [], [], []
    for chunk, (head, per) in enumerate(zip(heads, CHUNKS)):
        joined = chunk < len(CHUNKS) - 1
        grad_q, *parts = attend(
            doc_lengths, queries, grad_out, lse, delta, arrived[chunk], head, per, hops, joined
        )
        grads_q.append(grad_q)
        outputs_of.append((parts[: hops + 1], parts[hops + 1 :], joined))
    for column, crossed, joined in outputs_of:
        if joined:
            crossed = send(crossed[0], to_odd(1) + to_even(0))
            crossed = after(crossed, outputs_of[-1][1][-1])
            edge = crossed[hops - 1]
        else:
            edge = send(crossed[-1], to_odd(hops) + to_even(0))
            crossed = [send(crossed[hop - 1], to_odd(hop) + to_even(hop)) for hop in range(1, hops)]
        edge = edge.astype(wide)
        total = column[hops].astype(wide) + jnp.where(side == 1, edge, 0.0)
        for hop in range(hops - 1, -1, -1):
            far = send(total.astype(half), back(hop + 1)).astype(wide)
            if hop:
                total = column[hop].astype(wide) + crossed[hop - 1].astype(wide) + far
        total = column[0] + jnp.where(side == 0, edge, 0.0) + far
        sums.append(total.astype(half))
    grads_q[-1] = after(grads_q[-1], edge)
    grad_q = jnp.concatenate(grads_q, axis=1)
    grad_keys = jnp.concatenate([total[0] for total in sums], axis=1)
    grad_values = jnp.concatenate([total[1] for total in sums], axis=1)
    return (grad_q, grad_keys, grad_values)


def solution(mesh):
    rows = P(("packs", "seq"), None)
    return jax.shard_map(
        shards,
        mesh=mesh,
        in_specs=(rows, rows, rows, rows, rows, rows, P("packs")),
        out_specs=(rows, rows, rows),
        check_vma=False,
    )
```

```python
import functools

import jax
import jax.numpy as jnp
from jax import lax
from jax.experimental import pallas as pl
from jax.experimental.pallas import tpu as pltpu
from jax.sharding import PartitionSpec as P

HEADS = 64
KVH = 8
HDIM = 128
GROUP = HEADS // KVH
CHUNKS = (4, 4)
VMEM = 28 * 1024 * 1024


def contract_last(first, second):
    return lax.dot_general(
        first, second, (((1,), (1,)), ((), ())), preferred_element_type=jnp.float32
    )


def contract_first(first, second):
    return lax.dot_general(
        first, second, (((0,), (0,)), ((), ())), preferred_element_type=jnp.float32
    )


def head_rows(block):
    return jnp.concatenate(
        [block[:, h * HDIM : (h + 1) * HDIM] for h in range(GROUP)], axis=0
    )


PIECES = 4


def delta_kernel(outputs, grad_out, queries, delta_ref, gout_ref, q_ref, out_ref, out_sems, gout_sems, q_sem):
    rows = out_ref.shape[0]
    wide = GROUP * HDIM
    size = out_ref.shape[1] // PIECES
    pieces = []
    for piece in range(PIECES):
        at = slice(piece * size, (piece + 1) * size)
        pieces.append(
            (
                pltpu.make_async_copy(outputs.at[:, at], out_ref.at[:, at], out_sems.at[piece]),
                pltpu.make_async_copy(grad_out.at[:, at], gout_ref.at[:, at], gout_sems.at[piece]),
            )
        )
    for one, two in pieces:
        one.start()
        two.start()
    copy = pltpu.make_async_copy(queries, q_ref, q_sem)
    copy.start()
    first = lax.broadcasted_iota(jnp.int32, (wide, HDIM), 1) * HDIM
    row = lax.broadcasted_iota(jnp.int32, (wide, HDIM), 0)
    ones = jnp.where((row >= first) & (row < first + HDIM), 1.0, 0.0).astype(jnp.bfloat16)
    for group in range(out_ref.shape[1] // wide):
        if group * wide % size == 0:
            one, two = pieces[group * wide // size]
            one.wait()
            two.wait()
        at = slice(group * wide, (group + 1) * wide)
        product = out_ref[:, at].astype(jnp.float32) * gout_ref[:, at].astype(jnp.float32)
        high = product.astype(jnp.bfloat16)
        low = (product - high.astype(jnp.float32)).astype(jnp.bfloat16)
        total = jnp.dot(high, ones, preferred_element_type=jnp.float32)
        total += jnp.dot(low, ones, preferred_element_type=jnp.float32)
        delta_ref[group * GROUP : (group + 1) * GROUP, :] = total.T[:GROUP]
    copy.wait()


def delta_rows(outputs, grad_out, queries):
    rows = outputs.shape[0]
    return pl.pallas_call(
        delta_kernel,
        in_specs=[pl.BlockSpec(memory_space=pl.ANY)] * 3,
        out_specs=[pl.BlockSpec(memory_space=pltpu.VMEM)] * 3,
        out_shape=[
            jax.ShapeDtypeStruct((HEADS, rows), jnp.float32),
            jax.ShapeDtypeStruct(grad_out.shape, grad_out.dtype),
            jax.ShapeDtypeStruct(queries.shape, queries.dtype),
        ],
        scratch_shapes=[
            pltpu.VMEM(outputs.shape, outputs.dtype),
            pltpu.SemaphoreType.DMA((PIECES,)),
            pltpu.SemaphoreType.DMA((PIECES,)),
            pltpu.SemaphoreType.DMA,
        ],
        compiler_params=pltpu.CompilerParams(vmem_limit_bytes=VMEM),
        cost_estimate=pl.CostEstimate(
            flops=4 * rows * HEADS * HDIM * HDIM,
            bytes_accessed=10 * rows * HEADS * HDIM,
            transcendentals=0,
        ),
        name="delta",
    )(outputs, grad_out, queries)


def slot_shards(me, hops):
    side = lax.rem(me, 2)
    found = [me - 2 * hop for hop in range(hops + 1)]
    found += [me - 2 * hop + 1 - 2 * side for hop in range(1, hops)]
    found.append(jnp.where(side == 1, me - 1, me - 2 * hops + 1))
    return found


def attend_kernel(hops, joined, first, places, docs, q_ref, gout_ref, lse_ref, delta_ref, *refs):
    slots = 2 * hops + 1
    moved, refs = refs[:slots], refs[slots:]
    gq_ref, refs = refs[0], refs[1:]
    if joined:
        parts = refs[: hops + 1] + tuple(refs[hops + 1].at[hop] for hop in range(hops))
    else:
        parts = refs[:slots]
    k_all, v_all, bias, prob, score = refs[-5:]
    rows = q_ref.shape[0]
    scale = 1.0 / HDIM**0.5
    me = lax.axis_index("seq")

    token = lax.broadcasted_iota(jnp.int32, (1, rows), 1) + me * rows
    begin = jnp.zeros((1, rows), jnp.int32)
    bound = jnp.int32(0)
    for doc in range(docs.shape[0]):
        bound = bound + docs[doc]
        begin = jnp.where(token >= bound, bound, begin)
    row = lax.broadcasted_iota(jnp.int32, (rows, rows), 0)
    for slot, shard in enumerate(slot_shards(me, hops)):
        key = row + shard * rows
        visible = (key <= token) & (key >= begin)
        bias[slot * rows : (slot + 1) * rows, :] = jnp.where(visible, 0.0, -1e30)

    @pl.loop(0, moved[0].shape[-1] // HDIM)
    def _(index):
        column = pl.ds(pl.multiple_of(index * HDIM, HDIM), HDIM)
        wide = pl.ds(pl.multiple_of((first + index) * GROUP * HDIM, GROUP * HDIM), GROUP * HDIM)
        stat = pl.ds(pl.multiple_of((first + index) * GROUP, GROUP), GROUP)
        for slot in range(slots):
            here = slice(slot * rows, (slot + 1) * rows)
            pair = moved[slot] if places[slot] is None else moved[slot].at[places[slot]]
            k_all[here, :] = pair[0, :, column]
            v_all[here, :] = pair[1, :, column]
        queries = head_rows(q_ref[:, wide])
        gout = head_rows(gout_ref[:, wide])
        lses = lse_ref[stat, :]
        deltas = delta_ref[stat, :]
        keys = k_all[...]
        values = v_all[...]
        hidden = bias[...]
        hidden = jnp.concatenate([hidden, hidden], axis=1)
        for two in range(GROUP // 2):
            at = slice(2 * two * rows, (2 * two + 2) * rows)
            lse = jnp.concatenate([lses[2 * two : 2 * two + 1], lses[2 * two + 1 : 2 * two + 2]], axis=1)
            delta = jnp.concatenate(
                [deltas[2 * two : 2 * two + 1], deltas[2 * two + 1 : 2 * two + 2]], axis=1
            )
            raw = contract_last(keys, queries[at])
            attn = jnp.exp(raw * scale - lse + hidden)
            grad = contract_last(values, gout[at])
            prob[:, at] = attn.astype(jnp.bfloat16)
            score[:, at] = (attn * (grad - delta)).astype(jnp.bfloat16)
        scores = score[...]
        grad_k = jnp.dot(scores, queries, preferred_element_type=jnp.float32) * scale
        grad_v = jnp.dot(prob[...], gout, preferred_element_type=jnp.float32)
        for slot in range(slots):
            here = slice(slot * rows, (slot + 1) * rows)
            part = parts[slot]
            part[0, :, column] = grad_k[here].astype(part.dtype)
            part[1, :, column] = grad_v[here].astype(part.dtype)
        grad_q = (contract_first(keys, scores) * scale).astype(jnp.bfloat16)
        mine = pl.ds(pl.multiple_of(index * GROUP * HDIM, GROUP * HDIM), GROUP * HDIM)
        gq_ref[:, mine] = jnp.concatenate(
            [grad_q[:, h * rows : (h + 1) * rows].T for h in range(GROUP)], axis=1
        )


def attend(docs, queries, grad_out, lse, delta, moved, head, per, hops, joined):
    rows = queries.shape[0]
    slots = 2 * hops + 1
    local = pl.BlockSpec(memory_space=pltpu.VMEM)
    operands = [docs, queries, grad_out, lse, delta] + [array for array, index in moved]
    out_shape = [jax.ShapeDtypeStruct((rows, per * GROUP * HDIM), jnp.bfloat16)]
    kinds = [jnp.float32] + [jnp.bfloat16] * hops
    out_shape += [jax.ShapeDtypeStruct((2, rows, per * HDIM), kind) for kind in kinds]
    if joined:
        out_shape += [jax.ShapeDtypeStruct((hops, 2, rows, per * HDIM), jnp.bfloat16)]
    else:
        out_shape += [jax.ShapeDtypeStruct((2, rows, per * HDIM), jnp.bfloat16)] * hops
    pairs = slots * rows * rows * GROUP * per
    places = [index for array, index in moved]
    return pl.pallas_call(
        functools.partial(attend_kernel, hops, joined, head, places),
        in_specs=[pl.BlockSpec(memory_space=pltpu.SMEM)] + [local] * (len(operands) - 1),
        out_specs=[local] * len(out_shape),
        scratch_shapes=[
            pltpu.VMEM((slots * rows, HDIM), jnp.bfloat16),
            pltpu.VMEM((slots * rows, HDIM), jnp.bfloat16),
            pltpu.VMEM((slots * rows, rows), jnp.float32),
            pltpu.VMEM((slots * rows, GROUP * rows), jnp.bfloat16),
            pltpu.VMEM((slots * rows, GROUP * rows), jnp.bfloat16),
        ],
        out_shape=out_shape,
        compiler_params=pltpu.CompilerParams(vmem_limit_bytes=VMEM),
        cost_estimate=pl.CostEstimate(
            flops=40 * pairs * HDIM,
            bytes_accessed=per * rows * HDIM * 2 * (3 * GROUP + 6 * slots),
            transcendentals=pairs,
        ),
        name="attend",
    )(*operands)


def shards(queries, keys, values, outputs, grad_out, lse_saved, doc_lengths):
    seq = lax.axis_size("seq")
    me = lax.axis_index("seq").astype(jnp.int32)
    side = lax.rem(me, 2)
    hops = seq // 4
    def onward(hop):
        return [(s, s + 2) for s in range(2 * hop - 2, seq - 2)]

    def back(hop):
        return [(s, s - 2) for s in range(2 * hop, seq)]

    def to_odd(hop):
        return [(s, s + 1) for s in range(2 * hop, seq, 2)]

    def to_even(hop):
        return [(s + 1, s) for s in range(2 * hop, seq, 2)]

    def send(array, pairs):
        return lax.ppermute(array, "seq", pairs)

    def after(array, *others):
        return lax.optimization_barrier((array,) + others)[0]

    delta, grad_out, queries = delta_rows(outputs, grad_out, queries)
    lse = lse_saved.T
    heads = [sum(CHUNKS[:chunk]) for chunk in range(len(CHUNKS))]
    columns = []
    for head, per in zip(heads, CHUNKS):
        at = slice(head * HDIM, (head + per) * HDIM)
        own = jnp.stack([keys[:, at], values[:, at]])
        columns.append([own, send(own, onward(1))])
        columns[-1][1], delta = lax.optimization_barrier((columns[-1][1], delta))
    for column in columns:
        for hop in range(2, hops + 1):
            column.append(send(column[-1], onward(hop)))
    arrived = []
    for chunk, column in enumerate(columns):
        edge = jnp.where(side == 0, column[0], column[hops])
        moved = [(array, None) for array in column]
        if chunk == 0:
            crossed = [send(array, to_odd(1) + to_even(1)) for array in column[1:hops]]
            crossed.append(send(after(edge, *crossed), to_odd(0) + to_even(hops)))
            moved += [(array, None) for array in crossed]
        else:
            joint = jnp.stack(column[1:hops] + [edge])
            crossed = send(joint, to_odd(0) + to_even(1))
            moved += [(crossed, hop) for hop in range(hops)]
            arrived[0][-1] = (after(arrived[0][-1][0], joint), None)
        arrived.append(moved)

    wide, half = jnp.float32, jnp.bfloat16
    grads_q, sums, outputs_of = [], [], []
    for chunk, (head, per) in enumerate(zip(heads, CHUNKS)):
        joined = chunk < len(CHUNKS) - 1
        grad_q, *parts = attend(
            doc_lengths, queries, grad_out, lse, delta, arrived[chunk], head, per, hops, joined
        )
        grads_q.append(grad_q)
        outputs_of.append((parts[: hops + 1], parts[hops + 1 :], joined))
    for column, crossed, joined in outputs_of:
        if joined:
            crossed = send(crossed[0], to_odd(1) + to_even(0))
            crossed = after(crossed, outputs_of[-1][1][-1])
            edge = crossed[hops - 1]
        else:
            edge = send(crossed[-1], to_odd(hops) + to_even(0))
            crossed = [send(crossed[hop - 1], to_odd(hop) + to_even(hop)) for hop in range(1, hops)]
        edge = edge.astype(wide)
        total = column[hops].astype(wide) + jnp.where(side == 1, edge, 0.0)
        for hop in range(hops - 1, -1, -1):
            far = send(total.astype(half), back(hop + 1)).astype(wide)
            if hop:
                total = column[hop].astype(wide) + crossed[hop - 1].astype(wide) + far
        total = column[0] + jnp.where(side == 0, edge, 0.0) + far
        sums.append(total.astype(half))
    grads_q[-1] = after(grads_q[-1], edge)
    grad_q = jnp.concatenate(grads_q, axis=1)
    grad_keys = jnp.concatenate([total[0] for total in sums], axis=1)
    grad_values = jnp.concatenate([total[1] for total in sums], axis=1)
    return (grad_q, grad_keys, grad_values)


def solution(mesh):
    rows = P(("packs", "seq"), None)
    return jax.shard_map(
        shards,
        mesh=mesh,
        in_specs=(rows, rows, rows, rows, rows, rows, P("packs")),
        out_specs=(rows, rows, rows),
        check_vma=False,
    )
```

```python
import functools

import jax
import jax.numpy as jnp
from jax import lax
from jax.experimental import pallas as pl
from jax.experimental.pallas import tpu as pltpu
from jax.sharding import PartitionSpec as P

HEADS = 64
KVH = 8
HDIM = 128
GROUP = HEADS // KVH
CHUNKS = (4, 4)
VMEM = 16 * 1024 * 1024


def contract_last(first, second):
    return lax.dot_general(
        first, second, (((1,), (1,)), ((), ())), preferred_element_type=jnp.float32
    )


def contract_first(first, second):
    return lax.dot_general(
        first, second, (((0,), (0,)), ((), ())), preferred_element_type=jnp.float32
    )


def head_rows(block):
    return jnp.concatenate(
        [block[:, h * HDIM : (h + 1) * HDIM] for h in range(GROUP)], axis=0
    )


def delta_kernel(out_ref, gout_ref, q_ref, delta_ref):
    rows = out_ref.shape[0]
    wide = GROUP * HDIM
    first = lax.broadcasted_iota(jnp.int32, (wide, HDIM), 1) * HDIM
    row = lax.broadcasted_iota(jnp.int32, (wide, HDIM), 0)
    ones = jnp.where((row >= first) & (row < first + HDIM), 1.0, 0.0).astype(jnp.bfloat16)
    for group in range(out_ref.shape[1] // wide):
        at = slice(group * wide, (group + 1) * wide)
        product = out_ref[:, at].astype(jnp.float32) * gout_ref[:, at].astype(jnp.float32)
        high = product.astype(jnp.bfloat16)
        low = (product - high.astype(jnp.float32)).astype(jnp.bfloat16)
        total = jnp.dot(high, ones, preferred_element_type=jnp.float32)
        total += jnp.dot(low, ones, preferred_element_type=jnp.float32)
        delta_ref[group * GROUP : (group + 1) * GROUP, :] = total.T[:GROUP]


def delta_rows(outputs, grad_out, queries):
    rows = outputs.shape[0]
    local = pl.BlockSpec(memory_space=pltpu.VMEM)
    return pl.pallas_call(
        delta_kernel,
        in_specs=[local] * 3,
        out_specs=local,
        out_shape=jax.ShapeDtypeStruct((HEADS, rows), jnp.float32),
        compiler_params=pltpu.CompilerParams(vmem_limit_bytes=VMEM),
        cost_estimate=pl.CostEstimate(
            flops=4 * rows * HEADS * HDIM * HDIM,
            bytes_accessed=6 * rows * HEADS * HDIM,
            transcendentals=0,
        ),
        name="delta",
    )(outputs, grad_out, queries)


def slot_shards(me, hops):
    side = lax.rem(me, 2)
    found = [me - 2 * hop for hop in range(hops + 1)]
    found += [me - 2 * hop + 1 - 2 * side for hop in range(1, hops)]
    found.append(jnp.where(side == 1, me - 1, me - 2 * hops + 1))
    return found


def attend_kernel(hops, joined, first, places, docs, q_ref, gout_ref, lse_ref, delta_ref, *refs):
    slots = 2 * hops + 1
    moved, refs = refs[:slots], refs[slots:]
    gq_ref, refs = refs[0], refs[1:]
    if joined:
        parts = refs[: hops + 1] + tuple(refs[hops + 1].at[hop] for hop in range(hops))
    else:
        parts = refs[:slots]
    k_all, v_all, bias, prob, score = refs[-5:]
    rows = q_ref.shape[0]
    scale = 1.0 / HDIM**0.5
    me = lax.axis_index("seq")

    token = lax.broadcasted_iota(jnp.int32, (1, rows), 1) + me * rows
    begin = jnp.zeros((1, rows), jnp.int32)
    bound = jnp.int32(0)
    for doc in range(docs.shape[0]):
        bound = bound + docs[doc]
        begin = jnp.where(token >= bound, bound, begin)
    row = lax.broadcasted_iota(jnp.int32, (rows, rows), 0)
    for slot, shard in enumerate(slot_shards(me, hops)):
        key = row + shard * rows
        visible = (key <= token) & (key >= begin)
        bias[slot * rows : (slot + 1) * rows, :] = jnp.where(visible, 0.0, -1e30)

    @pl.loop(0, moved[0].shape[-1] // HDIM)
    def _(index):
        column = pl.ds(pl.multiple_of(index * HDIM, HDIM), HDIM)
        wide = pl.ds(pl.multiple_of((first + index) * GROUP * HDIM, GROUP * HDIM), GROUP * HDIM)
        stat = pl.ds(pl.multiple_of((first + index) * GROUP, GROUP), GROUP)
        for slot in range(slots):
            here = slice(slot * rows, (slot + 1) * rows)
            pair = moved[slot] if places[slot] is None else moved[slot].at[places[slot]]
            k_all[here, :] = pair[0, :, column]
            v_all[here, :] = pair[1, :, column]
        queries = head_rows(q_ref[:, wide])
        gout = head_rows(gout_ref[:, wide])
        lses = lse_ref[stat, :]
        deltas = delta_ref[stat, :]
        keys = k_all[...]
        values = v_all[...]
        hidden = bias[...]
        hidden = jnp.concatenate([hidden, hidden], axis=1)
        for two in range(GROUP // 2):
            at = slice(2 * two * rows, (2 * two + 2) * rows)
            lse = jnp.concatenate([lses[2 * two : 2 * two + 1], lses[2 * two + 1 : 2 * two + 2]], axis=1)
            delta = jnp.concatenate(
                [deltas[2 * two : 2 * two + 1], deltas[2 * two + 1 : 2 * two + 2]], axis=1
            )
            raw = contract_last(keys, queries[at])
            attn = jnp.exp(raw * scale - lse + hidden)
            grad = contract_last(values, gout[at])
            prob[:, at] = attn.astype(jnp.bfloat16)
            score[:, at] = (attn * (grad - delta)).astype(jnp.bfloat16)
        scores = score[...]
        grad_k = jnp.dot(scores, queries, preferred_element_type=jnp.float32) * scale
        grad_v = jnp.dot(prob[...], gout, preferred_element_type=jnp.float32)
        for slot in range(slots):
            here = slice(slot * rows, (slot + 1) * rows)
            part = parts[slot]
            part[0, :, column] = grad_k[here].astype(part.dtype)
            part[1, :, column] = grad_v[here].astype(part.dtype)
        grad_q = (contract_first(keys, scores) * scale).astype(jnp.bfloat16)
        mine = pl.ds(pl.multiple_of(index * GROUP * HDIM, GROUP * HDIM), GROUP * HDIM)
        gq_ref[:, mine] = jnp.concatenate(
            [grad_q[:, h * rows : (h + 1) * rows].T for h in range(GROUP)], axis=1
        )


def attend(docs, queries, grad_out, lse, delta, moved, head, per, hops, joined):
    rows = queries.shape[0]
    slots = 2 * hops + 1
    local = pl.BlockSpec(memory_space=pltpu.VMEM)
    operands = [docs, queries, grad_out, lse, delta] + [array for array, index in moved]
    out_shape = [jax.ShapeDtypeStruct((rows, per * GROUP * HDIM), jnp.bfloat16)]
    kinds = [jnp.float32] + [jnp.bfloat16] * hops
    out_shape += [jax.ShapeDtypeStruct((2, rows, per * HDIM), kind) for kind in kinds]
    if joined:
        out_shape += [jax.ShapeDtypeStruct((hops, 2, rows, per * HDIM), jnp.bfloat16)]
    else:
        out_shape += [jax.ShapeDtypeStruct((2, rows, per * HDIM), jnp.bfloat16)] * hops
    pairs = slots * rows * rows * GROUP * per
    places = [index for array, index in moved]
    return pl.pallas_call(
        functools.partial(attend_kernel, hops, joined, head, places),
        in_specs=[pl.BlockSpec(memory_space=pltpu.SMEM)] + [local] * (len(operands) - 1),
        out_specs=[local] * len(out_shape),
        scratch_shapes=[
            pltpu.VMEM((slots * rows, HDIM), jnp.bfloat16),
            pltpu.VMEM((slots * rows, HDIM), jnp.bfloat16),
            pltpu.VMEM((slots * rows, rows), jnp.float32),
            pltpu.VMEM((slots * rows, GROUP * rows), jnp.bfloat16),
            pltpu.VMEM((slots * rows, GROUP * rows), jnp.bfloat16),
        ],
        out_shape=out_shape,
        compiler_params=pltpu.CompilerParams(vmem_limit_bytes=VMEM),
        cost_estimate=pl.CostEstimate(
            flops=40 * pairs * HDIM,
            bytes_accessed=per * rows * HDIM * 2 * (3 * GROUP + 6 * slots),
            transcendentals=pairs,
        ),
        name="attend",
    )(*operands)


def shards(queries, keys, values, outputs, grad_out, lse_saved, doc_lengths):
    seq = lax.axis_size("seq")
    me = lax.axis_index("seq").astype(jnp.int32)
    side = lax.rem(me, 2)
    hops = seq // 4
    def onward(hop):
        return [(s, s + 2) for s in range(2 * hop - 2, seq - 2)]

    def back(hop):
        return [(s, s - 2) for s in range(2 * hop, seq)]

    def to_odd(hop):
        return [(s, s + 1) for s in range(2 * hop, seq, 2)]

    def to_even(hop):
        return [(s + 1, s) for s in range(2 * hop, seq, 2)]

    def send(array, pairs):
        return lax.ppermute(array, "seq", pairs)

    def after(array, *others):
        return lax.optimization_barrier((array,) + others)[0]

    delta = delta_rows(outputs, grad_out, queries)
    lse = lse_saved.T
    heads = [sum(CHUNKS[:chunk]) for chunk in range(len(CHUNKS))]
    columns = []
    for head, per in zip(heads, CHUNKS):
        at = slice(head * HDIM, (head + per) * HDIM)
        own = jnp.stack([keys[:, at], values[:, at]])
        columns.append([own, send(own, onward(1))])
        columns[-1][1], delta = lax.optimization_barrier((columns[-1][1], delta))
    for column in columns:
        for hop in range(2, hops + 1):
            column.append(send(column[-1], onward(hop)))
    arrived = []
    for chunk, column in enumerate(columns):
        edge = jnp.where(side == 0, column[0], column[hops])
        moved = [(array, None) for array in column]
        if chunk == 0:
            crossed = [send(array, to_odd(1) + to_even(1)) for array in column[1:hops]]
            crossed.append(send(after(edge, *crossed), to_odd(0) + to_even(hops)))
            moved += [(array, None) for array in crossed]
        else:
            joint = jnp.stack(column[1:hops] + [edge])
            crossed = send(joint, to_odd(0) + to_even(1))
            moved += [(crossed, hop) for hop in range(hops)]
            arrived[0][-1] = (after(arrived[0][-1][0], joint), None)
        arrived.append(moved)

    wide, half = jnp.float32, jnp.bfloat16
    grads_q, sums, outputs_of = [], [], []
    for chunk, (head, per) in enumerate(zip(heads, CHUNKS)):
        joined = chunk < len(CHUNKS) - 1
        grad_q, *parts = attend(
            doc_lengths, queries, grad_out, lse, delta, arrived[chunk], head, per, hops, joined
        )
        grads_q.append(grad_q)
        outputs_of.append((parts[: hops + 1], parts[hops + 1 :], joined))
    before = []
    for column, crossed, joined in outputs_of:
        if joined:
            crossed = send(crossed[0], to_odd(1) + to_even(0))
            crossed = after(crossed, outputs_of[-1][1][-1])
            edge = crossed[hops - 1]
        else:
            edge = send(crossed[-1], to_odd(hops) + to_even(0))
            crossed = [
                send(after(crossed[hop - 1], *before), to_odd(hop) + to_even(hop)) for hop in range(1, hops)
            ]
        edge = edge.astype(wide)
        total = column[hops].astype(wide) + jnp.where(side == 1, edge, 0.0)
        for hop in range(hops - 1, -1, -1):
            total = total.astype(half)
            if hop == hops - 1:
                before = [total]
            far = send(total, back(hop + 1)).astype(wide)
            if hop:
                total = column[hop].astype(wide) + crossed[hop - 1].astype(wide) + far
        total = column[0] + jnp.where(side == 0, edge, 0.0) + far
        sums.append(total.astype(half))
    grads_q[-1] = after(grads_q[-1], edge)
    grad_q = jnp.concatenate(grads_q, axis=1)
    grad_keys = jnp.concatenate([total[0] for total in sums], axis=1)
    grad_values = jnp.concatenate([total[1] for total in sums], axis=1)
    return (grad_q, grad_keys, grad_values)


def solution(mesh):
    rows = P(("packs", "seq"), None)
    return jax.shard_map(
        shards,
        mesh=mesh,
        in_specs=(rows, rows, rows, rows, rows, rows, P("packs")),
        out_specs=(rows, rows, rows),
        check_vma=False,
    )
```

```python
import functools

import jax
import jax.numpy as jnp
from jax import lax
from jax.experimental import pallas as pl
from jax.experimental.pallas import tpu as pltpu
from jax.sharding import PartitionSpec as P

HEADS = 64
KVH = 8
HDIM = 128
GROUP = HEADS // KVH
CHUNKS = (4, 4)
VMEM = 16 * 1024 * 1024


def contract_last(first, second):
    return lax.dot_general(
        first, second, (((1,), (1,)), ((), ())), preferred_element_type=jnp.float32
    )


def contract_first(first, second):
    return lax.dot_general(
        first, second, (((0,), (0,)), ((), ())), preferred_element_type=jnp.float32
    )


def head_rows(block):
    return jnp.concatenate(
        [block[:, h * HDIM : (h + 1) * HDIM] for h in range(GROUP)], axis=0
    )


def delta_kernel(out_ref, gout_ref, delta_ref):
    rows = out_ref.shape[0]
    wide = GROUP * HDIM
    first = lax.broadcasted_iota(jnp.int32, (wide, HDIM), 1) * HDIM
    row = lax.broadcasted_iota(jnp.int32, (wide, HDIM), 0)
    ones = jnp.where((row >= first) & (row < first + HDIM), 1.0, 0.0).astype(jnp.bfloat16)
    for group in range(out_ref.shape[1] // wide):
        at = slice(group * wide, (group + 1) * wide)
        product = out_ref[:, at].astype(jnp.float32) * gout_ref[:, at].astype(jnp.float32)
        high = product.astype(jnp.bfloat16)
        low = (product - high.astype(jnp.float32)).astype(jnp.bfloat16)
        total = jnp.dot(high, ones, preferred_element_type=jnp.float32)
        total += jnp.dot(low, ones, preferred_element_type=jnp.float32)
        delta_ref[group * GROUP : (group + 1) * GROUP, :] = total.T[:GROUP]


def delta_rows(outputs, grad_out):
    rows = outputs.shape[0]
    local = pl.BlockSpec(memory_space=pltpu.VMEM)
    return pl.pallas_call(
        delta_kernel,
        in_specs=[local] * 2,
        out_specs=local,
        out_shape=jax.ShapeDtypeStruct((HEADS, rows), jnp.float32),
        compiler_params=pltpu.CompilerParams(vmem_limit_bytes=VMEM),
        cost_estimate=pl.CostEstimate(
            flops=4 * rows * HEADS * HDIM * HDIM,
            bytes_accessed=4 * rows * HEADS * HDIM,
            transcendentals=0,
        ),
        name="delta",
    )(outputs, grad_out)


def edge_kernel(own_ref, *refs):
    side = lax.rem(lax.axis_index("seq"), 2)
    arrays, edge_ref = refs[:-1], refs[-1]
    for place, array in enumerate(arrays[:-1]):
        edge_ref[place] = array[...]

    @pl.when(side == 0)
    def _():
        edge_ref[len(arrays) - 1] = own_ref[...]

    @pl.when(side == 1)
    def _():
        edge_ref[len(arrays) - 1] = arrays[-1][...]


def edge_operand(own, arrays):
    local = pl.BlockSpec(memory_space=pltpu.VMEM)
    shape = (len(arrays),) + own.shape
    return pl.pallas_call(
        edge_kernel,
        in_specs=[local] * (1 + len(arrays)),
        out_specs=local,
        out_shape=jax.ShapeDtypeStruct(shape, own.dtype),
        compiler_params=pltpu.CompilerParams(vmem_limit_bytes=VMEM),
        cost_estimate=pl.CostEstimate(
            flops=0, bytes_accessed=4 * len(arrays) * own.size, transcendentals=0
        ),
        name="edge",
    )(own, *arrays)


def slot_shards(me, hops):
    side = lax.rem(me, 2)
    found = [me - 2 * hop for hop in range(hops + 1)]
    found += [me - 2 * hop + 1 - 2 * side for hop in range(1, hops)]
    found.append(jnp.where(side == 1, me - 1, me - 2 * hops + 1))
    return found


def attend_kernel(hops, joined, first, places, docs, q_ref, gout_ref, lse_ref, delta_ref, *refs):
    slots = 2 * hops + 1
    moved, refs = refs[:slots], refs[slots:]
    gq_ref, refs = refs[0], refs[1:]
    if joined:
        parts = refs[: hops + 1] + tuple(refs[hops + 1].at[hop] for hop in range(hops))
    else:
        parts = refs[:slots]
    k_all, v_all, bias, prob, score = refs[-5:]
    rows = q_ref.shape[0]
    scale = 1.0 / HDIM**0.5
    me = lax.axis_index("seq")

    token = lax.broadcasted_iota(jnp.int32, (1, rows), 1) + me * rows
    begin = jnp.zeros((1, rows), jnp.int32)
    bound = jnp.int32(0)
    for doc in range(docs.shape[0]):
        bound = bound + docs[doc]
        begin = jnp.where(token >= bound, bound, begin)
    row = lax.broadcasted_iota(jnp.int32, (rows, rows), 0)
    for slot, shard in enumerate(slot_shards(me, hops)):
        key = row + shard * rows
        visible = (key <= token) & (key >= begin)
        bias[slot * rows : (slot + 1) * rows, :] = jnp.where(visible, 0.0, -1e30)

    @pl.loop(0, moved[0].shape[-1] // HDIM)
    def _(index):
        column = pl.ds(pl.multiple_of(index * HDIM, HDIM), HDIM)
        wide = pl.ds(pl.multiple_of((first + index) * GROUP * HDIM, GROUP * HDIM), GROUP * HDIM)
        stat = pl.ds(pl.multiple_of((first + index) * GROUP, GROUP), GROUP)
        for slot in range(slots):
            here = slice(slot * rows, (slot + 1) * rows)
            pair = moved[slot] if places[slot] is None else moved[slot].at[places[slot]]
            k_all[here, :] = pair[0, :, column]
            v_all[here, :] = pair[1, :, column]
        queries = head_rows(q_ref[:, wide])
        gout = head_rows(gout_ref[:, wide])
        lses = lse_ref[stat, :]
        deltas = delta_ref[stat, :]
        keys = k_all[...]
        values = v_all[...]
        hidden = bias[...]
        hidden = jnp.concatenate([hidden, hidden], axis=1)
        for two in range(GROUP // 2):
            at = slice(2 * two * rows, (2 * two + 2) * rows)
            lse = jnp.concatenate([lses[2 * two : 2 * two + 1], lses[2 * two + 1 : 2 * two + 2]], axis=1)
            delta = jnp.concatenate(
                [deltas[2 * two : 2 * two + 1], deltas[2 * two + 1 : 2 * two + 2]], axis=1
            )
            raw = contract_last(keys, queries[at])
            attn = jnp.exp(raw * scale - lse + hidden)
            grad = contract_last(values, gout[at])
            prob[:, at] = attn.astype(jnp.bfloat16)
            score[:, at] = (attn * (grad - delta)).astype(jnp.bfloat16)
        scores = score[...]
        grad_k = jnp.dot(scores, queries, preferred_element_type=jnp.float32) * scale
        grad_v = jnp.dot(prob[...], gout, preferred_element_type=jnp.float32)
        for slot in range(slots):
            here = slice(slot * rows, (slot + 1) * rows)
            part = parts[slot]
            part[0, :, column] = grad_k[here].astype(part.dtype)
            part[1, :, column] = grad_v[here].astype(part.dtype)
        grad_q = (contract_first(keys, scores) * scale).astype(jnp.bfloat16)
        mine = pl.ds(pl.multiple_of(index * GROUP * HDIM, GROUP * HDIM), GROUP * HDIM)
        gq_ref[:, mine] = jnp.concatenate(
            [grad_q[:, h * rows : (h + 1) * rows].T for h in range(GROUP)], axis=1
        )


def attend(docs, queries, grad_out, lse, delta, moved, head, per, hops, joined):
    rows = queries.shape[0]
    slots = 2 * hops + 1
    local = pl.BlockSpec(memory_space=pltpu.VMEM)
    operands = [docs, queries, grad_out, lse, delta] + [array for array, index in moved]
    out_shape = [jax.ShapeDtypeStruct((rows, per * GROUP * HDIM), jnp.bfloat16)]
    kinds = [jnp.float32] + [jnp.bfloat16] * hops
    out_shape += [jax.ShapeDtypeStruct((2, rows, per * HDIM), kind) for kind in kinds]
    if joined:
        out_shape += [jax.ShapeDtypeStruct((hops, 2, rows, per * HDIM), jnp.bfloat16)]
    else:
        out_shape += [jax.ShapeDtypeStruct((2, rows, per * HDIM), jnp.bfloat16)] * hops
    pairs = slots * rows * rows * GROUP * per
    places = [index for array, index in moved]
    return pl.pallas_call(
        functools.partial(attend_kernel, hops, joined, head, places),
        in_specs=[pl.BlockSpec(memory_space=pltpu.SMEM)] + [local] * (len(operands) - 1),
        out_specs=[local] * len(out_shape),
        scratch_shapes=[
            pltpu.VMEM((slots * rows, HDIM), jnp.bfloat16),
            pltpu.VMEM((slots * rows, HDIM), jnp.bfloat16),
            pltpu.VMEM((slots * rows, rows), jnp.float32),
            pltpu.VMEM((slots * rows, GROUP * rows), jnp.bfloat16),
            pltpu.VMEM((slots * rows, GROUP * rows), jnp.bfloat16),
        ],
        out_shape=out_shape,
        compiler_params=pltpu.CompilerParams(vmem_limit_bytes=VMEM),
        cost_estimate=pl.CostEstimate(
            flops=40 * pairs * HDIM,
            bytes_accessed=per * rows * HDIM * 2 * (3 * GROUP + 6 * slots),
            transcendentals=pairs,
        ),
        name="attend",
    )(*operands)


def shards(queries, keys, values, outputs, grad_out, lse_saved, doc_lengths):
    seq = lax.axis_size("seq")
    me = lax.axis_index("seq").astype(jnp.int32)
    side = lax.rem(me, 2)
    hops = seq // 4
    def onward(hop):
        return [(s, s + 2) for s in range(2 * hop - 2, seq - 2)]

    def back(hop):
        return [(s, s - 2) for s in range(2 * hop, seq)]

    def to_odd(hop):
        return [(s, s + 1) for s in range(2 * hop, seq, 2)]

    def to_even(hop):
        return [(s + 1, s) for s in range(2 * hop, seq, 2)]

    def send(array, pairs):
        return lax.ppermute(array, "seq", pairs)

    def after(array, *others):
        return lax.optimization_barrier((array,) + others)[0]

    delta = delta_rows(outputs, grad_out)
    lse = lse_saved.T
    heads = [sum(CHUNKS[:chunk]) for chunk in range(len(CHUNKS))]
    columns = []
    for head, per in zip(heads, CHUNKS):
        at = slice(head * HDIM, (head + per) * HDIM)
        own = jnp.stack([keys[:, at], values[:, at]])
        columns.append([own, send(own, onward(1))])
        columns[-1][1], delta = lax.optimization_barrier((columns[-1][1], delta))
    for column in columns:
        for hop in range(2, hops + 1):
            column.append(send(column[-1], onward(hop)))
    arrived = []
    for chunk, column in enumerate(columns):
        moved = [(array, None) for array in column]
        if chunk == 0:
            crossed = [send(array, to_odd(1) + to_even(1)) for array in column[1:hops]]
            moved += [(array, None) for array in crossed]
            edge = edge_operand(column[0], [column[hops]])
            edge = send(after(edge, *crossed), to_odd(0) + to_even(hops))
            moved.append((edge, 0))
        else:
            joint = edge_operand(column[0], column[1:])
            crossed = send(joint, to_odd(0) + to_even(1))
            moved += [(crossed, hop) for hop in range(hops)]
            arrived[0][-1] = (after(arrived[0][-1][0], joint), 0)
        arrived.append(moved)

    wide, half = jnp.float32, jnp.bfloat16
    grads_q, sums, outputs_of = [], [], []
    for chunk, (head, per) in enumerate(zip(heads, CHUNKS)):
        joined = chunk < len(CHUNKS) - 1
        grad_q, *parts = attend(
            doc_lengths, queries, grad_out, lse, delta, arrived[chunk], head, per, hops, joined
        )
        grads_q.append(grad_q)
        outputs_of.append((parts[: hops + 1], parts[hops + 1 :], joined))
    before = []
    for column, crossed, joined in outputs_of:
        if joined:
            crossed = send(crossed[0], to_odd(1) + to_even(0))
            crossed = after(crossed, outputs_of[-1][1][-1])
            edge = crossed[hops - 1]
        else:
            edge = send(crossed[-1], to_odd(hops) + to_even(0))
            crossed = [
                send(after(crossed[hop - 1], *before), to_odd(hop) + to_even(hop)) for hop in range(1, hops)
            ]
        edge = edge.astype(wide)
        total = column[hops].astype(wide) + jnp.where(side == 1, edge, 0.0)
        for hop in range(hops - 1, -1, -1):
            total = total.astype(half)
            if hop == hops - 1:
                before = [total]
            far = send(total, back(hop + 1)).astype(wide)
            if hop:
                total = column[hop].astype(wide) + crossed[hop - 1].astype(wide) + far
        total = column[0] + jnp.where(side == 0, edge, 0.0) + far
        sums.append(total.astype(half))
    grads_q[-1] = after(grads_q[-1], edge)
    grad_q = jnp.concatenate(grads_q, axis=1)
    grad_keys = jnp.concatenate([total[0] for total in sums], axis=1)
    grad_values = jnp.concatenate([total[1] for total in sums], axis=1)
    return (grad_q, grad_keys, grad_values)


def solution(mesh):
    rows = P(("packs", "seq"), None)
    return jax.shard_map(
        shards,
        mesh=mesh,
        in_specs=(rows, rows, rows, rows, rows, rows, P("packs")),
        out_specs=(rows, rows, rows),
        check_vma=False,
    )
```

```python
import functools

import jax
import jax.numpy as jnp
from jax import lax
from jax.experimental import pallas as pl
from jax.experimental.pallas import tpu as pltpu
from jax.sharding import PartitionSpec as P

HEADS = 64
KVH = 8
HDIM = 128
GROUP = HEADS // KVH
CHUNKS = (4, 4)
VMEM = 16 * 1024 * 1024


def contract_last(first, second):
    return lax.dot_general(
        first, second, (((1,), (1,)), ((), ())), preferred_element_type=jnp.float32
    )


def contract_first(first, second):
    return lax.dot_general(
        first, second, (((0,), (0,)), ((), ())), preferred_element_type=jnp.float32
    )


def head_rows(block):
    return jnp.concatenate(
        [block[:, h * HDIM : (h + 1) * HDIM] for h in range(GROUP)], axis=0
    )


def delta_kernel(out_ref, gout_ref, q_ref, delta_ref):
    rows = out_ref.shape[0]
    wide = GROUP * HDIM
    first = lax.broadcasted_iota(jnp.int32, (wide, HDIM), 1) * HDIM
    row = lax.broadcasted_iota(jnp.int32, (wide, HDIM), 0)
    ones = jnp.where((row >= first) & (row < first + HDIM), 1.0, 0.0).astype(jnp.bfloat16)
    for group in range(out_ref.shape[1] // wide):
        at = slice(group * wide, (group + 1) * wide)
        product = out_ref[:, at].astype(jnp.float32) * gout_ref[:, at].astype(jnp.float32)
        high = product.astype(jnp.bfloat16)
        low = (product - high.astype(jnp.float32)).astype(jnp.bfloat16)
        total = jnp.dot(high, ones, preferred_element_type=jnp.float32)
        total += jnp.dot(low, ones, preferred_element_type=jnp.float32)
        delta_ref[group * GROUP : (group + 1) * GROUP, :] = total.T[:GROUP]


def delta_rows(outputs, grad_out, queries):
    rows = outputs.shape[0]
    local = pl.BlockSpec(memory_space=pltpu.VMEM)
    return pl.pallas_call(
        delta_kernel,
        in_specs=[local] * 3,
        out_specs=local,
        out_shape=jax.ShapeDtypeStruct((HEADS, rows), jnp.float32),
        compiler_params=pltpu.CompilerParams(vmem_limit_bytes=VMEM),
        cost_estimate=pl.CostEstimate(
            flops=4 * rows * HEADS * HDIM * HDIM,
            bytes_accessed=6 * rows * HEADS * HDIM,
            transcendentals=0,
        ),
        name="delta",
    )(outputs, grad_out, queries)


def slot_shards(me, hops):
    side = lax.rem(me, 2)
    found = [me - 2 * hop for hop in range(hops + 1)]
    found += [me - 2 * hop + 1 - 2 * side for hop in range(1, hops)]
    found.append(jnp.where(side == 1, me - 1, me - 2 * hops + 1))
    return found


def attend_kernel(hops, joined, first, places, docs, q_ref, gout_ref, lse_ref, delta_ref, *refs):
    slots = 2 * hops + 1
    moved, refs = refs[:slots], refs[slots:]
    gq_ref, refs = refs[0], refs[1:]
    if joined:
        parts = refs[: hops + 1] + tuple(refs[hops + 1].at[hop] for hop in range(hops))
    else:
        parts = refs[:slots]
    k_all, v_all, bias, prob, score = refs[-5:]
    rows = q_ref.shape[0]
    scale = 1.0 / HDIM**0.5
    me = lax.axis_index("seq")

    token = lax.broadcasted_iota(jnp.int32, (1, rows), 1) + me * rows
    begin = jnp.zeros((1, rows), jnp.int32)
    bound = jnp.int32(0)
    for doc in range(docs.shape[0]):
        bound = bound + docs[doc]
        begin = jnp.where(token >= bound, bound, begin)
    row = lax.broadcasted_iota(jnp.int32, (rows, rows), 0)
    for slot, shard in enumerate(slot_shards(me, hops)):
        key = row + shard * rows
        visible = (key <= token) & (key >= begin)
        bias[slot * rows : (slot + 1) * rows, :] = jnp.where(visible, 0.0, -1e30)

    @pl.loop(0, moved[0].shape[-1] // HDIM)
    def _(index):
        column = pl.ds(pl.multiple_of(index * HDIM, HDIM), HDIM)
        wide = pl.ds(pl.multiple_of((first + index) * GROUP * HDIM, GROUP * HDIM), GROUP * HDIM)
        stat = pl.ds(pl.multiple_of((first + index) * GROUP, GROUP), GROUP)
        for slot in range(slots):
            here = slice(slot * rows, (slot + 1) * rows)
            pair = moved[slot] if places[slot] is None else moved[slot].at[places[slot]]
            k_all[here, :] = pair[0, :, column]
            v_all[here, :] = pair[1, :, column]
        queries = head_rows(q_ref[:, wide])
        gout = head_rows(gout_ref[:, wide])
        lses = lse_ref[stat, :]
        deltas = delta_ref[stat, :]
        keys = k_all[...]
        values = v_all[...]
        hidden = bias[...]
        hidden = jnp.concatenate([hidden, hidden], axis=1)
        for two in range(GROUP // 2):
            at = slice(2 * two * rows, (2 * two + 2) * rows)
            lse = jnp.concatenate([lses[2 * two : 2 * two + 1], lses[2 * two + 1 : 2 * two + 2]], axis=1)
            delta = jnp.concatenate(
                [deltas[2 * two : 2 * two + 1], deltas[2 * two + 1 : 2 * two + 2]], axis=1
            )
            raw = contract_last(keys, queries[at])
            attn = jnp.exp(raw * scale - lse + hidden)
            grad = contract_last(values, gout[at])
            prob[:, at] = attn.astype(jnp.bfloat16)
            score[:, at] = (attn * (grad - delta)).astype(jnp.bfloat16)
        scores = score[...]
        grad_k = jnp.dot(scores, queries, preferred_element_type=jnp.float32) * scale
        grad_v = jnp.dot(prob[...], gout, preferred_element_type=jnp.float32)
        for slot in range(slots):
            here = slice(slot * rows, (slot + 1) * rows)
            part = parts[slot]
            part[0, :, column] = grad_k[here].astype(part.dtype)
            part[1, :, column] = grad_v[here].astype(part.dtype)
        grad_q = (contract_first(keys, scores) * scale).astype(jnp.bfloat16)
        mine = pl.ds(pl.multiple_of(index * GROUP * HDIM, GROUP * HDIM), GROUP * HDIM)
        gq_ref[:, mine] = jnp.concatenate(
            [grad_q[:, h * rows : (h + 1) * rows].T for h in range(GROUP)], axis=1
        )


def attend(docs, queries, grad_out, lse, delta, moved, head, per, hops, joined):
    rows = queries.shape[0]
    slots = 2 * hops + 1
    local = pl.BlockSpec(memory_space=pltpu.VMEM)
    operands = [docs, queries, grad_out, lse, delta] + [array for array, index in moved]
    out_shape = [jax.ShapeDtypeStruct((rows, per * GROUP * HDIM), jnp.bfloat16)]
    kinds = [jnp.float32] + [jnp.bfloat16] * hops
    out_shape += [jax.ShapeDtypeStruct((2, rows, per * HDIM), kind) for kind in kinds]
    if joined:
        out_shape += [jax.ShapeDtypeStruct((hops, 2, rows, per * HDIM), jnp.bfloat16)]
    else:
        out_shape += [jax.ShapeDtypeStruct((2, rows, per * HDIM), jnp.bfloat16)] * hops
    pairs = slots * rows * rows * GROUP * per
    places = [index for array, index in moved]
    return pl.pallas_call(
        functools.partial(attend_kernel, hops, joined, head, places),
        in_specs=[pl.BlockSpec(memory_space=pltpu.SMEM)] + [local] * (len(operands) - 1),
        out_specs=[local] * len(out_shape),
        scratch_shapes=[
            pltpu.VMEM((slots * rows, HDIM), jnp.bfloat16),
            pltpu.VMEM((slots * rows, HDIM), jnp.bfloat16),
            pltpu.VMEM((slots * rows, rows), jnp.float32),
            pltpu.VMEM((slots * rows, GROUP * rows), jnp.bfloat16),
            pltpu.VMEM((slots * rows, GROUP * rows), jnp.bfloat16),
        ],
        out_shape=out_shape,
        compiler_params=pltpu.CompilerParams(vmem_limit_bytes=VMEM),
        cost_estimate=pl.CostEstimate(
            flops=40 * pairs * HDIM,
            bytes_accessed=per * rows * HDIM * 2 * (3 * GROUP + 6 * slots),
            transcendentals=pairs,
        ),
        name="attend",
    )(*operands)


def finish_kernel(chunks, *refs):
    key_ref, value_ref = refs[-2:]
    refs = refs[:-2]
    keep = jnp.where(lax.rem(lax.axis_index("seq"), 2) == 0, 1.0, 0.0)
    for start, done in chunks:
        if done:
            total, refs = refs[0][...], refs[1:]
        else:
            own, edge, far = (ref[...].astype(jnp.float32) for ref in refs[:3])
            total, refs = (own + edge * keep + far).astype(jnp.bfloat16), refs[3:]
        key_ref[:, start : start + total.shape[2]] = total[0]
        value_ref[:, start : start + total.shape[2]] = total[1]


def finish(sums, shape):
    operands, chunks, start = [], [], 0
    for part in sums:
        chunks.append((start, len(part) == 1))
        start += part[0].shape[2]
        operands += part
    local = pl.BlockSpec(memory_space=pltpu.VMEM)
    return pl.pallas_call(
        functools.partial(finish_kernel, chunks),
        in_specs=[local] * len(operands),
        out_specs=[local] * 2,
        out_shape=[jax.ShapeDtypeStruct(shape, jnp.bfloat16)] * 2,
        compiler_params=pltpu.CompilerParams(vmem_limit_bytes=VMEM),
        cost_estimate=pl.CostEstimate(
            flops=8 * shape[0] * shape[1], bytes_accessed=16 * shape[0] * shape[1], transcendentals=0
        ),
        name="finish",
    )(*operands)


def shards(queries, keys, values, outputs, grad_out, lse_saved, doc_lengths):
    seq = lax.axis_size("seq")
    me = lax.axis_index("seq").astype(jnp.int32)
    side = lax.rem(me, 2)
    hops = seq // 4
    def onward(hop):
        return [(s, s + 2) for s in range(2 * hop - 2, seq - 2)]

    def back(hop):
        return [(s, s - 2) for s in range(2 * hop, seq)]

    def to_odd(hop):
        return [(s, s + 1) for s in range(2 * hop, seq, 2)]

    def to_even(hop):
        return [(s + 1, s) for s in range(2 * hop, seq, 2)]

    def send(array, pairs):
        return lax.ppermute(array, "seq", pairs)

    def after(array, *others):
        return lax.optimization_barrier((array,) + others)[0]

    delta = delta_rows(outputs, grad_out, queries)
    lse = lse_saved.T
    heads = [sum(CHUNKS[:chunk]) for chunk in range(len(CHUNKS))]
    columns = []
    for head, per in zip(heads, CHUNKS):
        at = slice(head * HDIM, (head + per) * HDIM)
        own = lax.optimization_barrier(jnp.stack([keys[:, at], values[:, at]]))
        columns.append([own, send(own, onward(1))])
        columns[-1][1], delta = lax.optimization_barrier((columns[-1][1], delta))
    for column in columns:
        for hop in range(2, hops + 1):
            column.append(send(column[-1], onward(hop)))
    arrived = []
    for chunk, column in enumerate(columns):
        edge = jnp.where(side == 0, column[0], column[hops])
        moved = [(array, None) for array in column]
        if chunk == 0:
            crossed = [send(array, to_odd(1) + to_even(1)) for array in column[1:hops]]
            crossed.append(send(after(edge, *crossed), to_odd(0) + to_even(hops)))
            moved += [(array, None) for array in crossed]
        else:
            joint = jnp.stack(column[1:hops] + [edge])
            crossed = send(joint, to_odd(0) + to_even(1))
            moved += [(crossed, hop) for hop in range(hops)]
            arrived[0][-1] = (after(arrived[0][-1][0], joint), None)
        arrived.append(moved)

    wide, half = jnp.float32, jnp.bfloat16
    grads_q, sums, outputs_of = [], [], []
    for chunk, (head, per) in enumerate(zip(heads, CHUNKS)):
        joined = chunk < len(CHUNKS) - 1
        grad_q, *parts = attend(
            doc_lengths, queries, grad_out, lse, delta, arrived[chunk], head, per, hops, joined
        )
        grads_q.append(grad_q)
        outputs_of.append((parts[: hops + 1], parts[hops + 1 :], joined))
    before = []
    for column, crossed, joined in outputs_of:
        if joined:
            crossed = send(crossed[0], to_odd(1) + to_even(0))
            crossed = after(crossed, outputs_of[-1][1][-1])
            edge = crossed[hops - 1]
        else:
            edge = send(crossed[-1], to_odd(hops) + to_even(0))
            crossed = [
                send(after(crossed[hop - 1], before[0]), to_odd(hop) + to_even(hop)) for hop in range(1, hops)
            ]
        edge = edge.astype(wide)
        total = column[hops].astype(wide) + jnp.where(side == 1, edge, 0.0)
        for hop in range(hops - 1, -1, -1):
            total = total.astype(half)
            if joined:
                before.append(total)
            elif hop == 0:
                total = after(total, *before)
            far = send(total, back(hop + 1)).astype(wide)
            if hop:
                total = column[hop].astype(wide) + crossed[hop - 1].astype(wide) + far
        if joined:
            total = column[0] + jnp.where(side == 0, edge, 0.0) + far
            sums.append([total.astype(half)])
        else:
            sums.append([column[0], edge.astype(half), far.astype(half)])
    grads_q[-1] = after(grads_q[-1], edge)
    grad_q = jnp.concatenate(grads_q, axis=1)
    grad_keys, grad_values = finish(sums, keys.shape)
    return (grad_q, grad_keys, grad_values)


def solution(mesh):
    rows = P(("packs", "seq"), None)
    return jax.shard_map(
        shards,
        mesh=mesh,
        in_specs=(rows, rows, rows, rows, rows, rows, P("packs")),
        out_specs=(rows, rows, rows),
        check_vma=False,
    )
```

```python
import functools

import jax
import jax.numpy as jnp
from jax import lax
from jax.experimental import pallas as pl
from jax.experimental.pallas import tpu as pltpu
from jax.sharding import PartitionSpec as P

HEADS = 64
KVH = 8
HDIM = 128
GROUP = HEADS // KVH
CHUNKS = (4, 4)
VMEM = 16 * 1024 * 1024


def contract_last(first, second):
    return lax.dot_general(
        first, second, (((1,), (1,)), ((), ())), preferred_element_type=jnp.float32
    )


def contract_first(first, second):
    return lax.dot_general(
        first, second, (((0,), (0,)), ((), ())), preferred_element_type=jnp.float32
    )


def head_rows(block):
    return jnp.concatenate(
        [block[:, h * HDIM : (h + 1) * HDIM] for h in range(GROUP)], axis=0
    )


def delta_kernel(out_ref, gout_ref, q_ref, delta_ref):
    rows = out_ref.shape[0]
    wide = GROUP * HDIM
    first = lax.broadcasted_iota(jnp.int32, (wide, HDIM), 1) * HDIM
    row = lax.broadcasted_iota(jnp.int32, (wide, HDIM), 0)
    ones = jnp.where((row >= first) & (row < first + HDIM), 1.0, 0.0).astype(jnp.bfloat16)
    for group in range(out_ref.shape[1] // wide):
        at = slice(group * wide, (group + 1) * wide)
        product = out_ref[:, at].astype(jnp.float32) * gout_ref[:, at].astype(jnp.float32)
        high = product.astype(jnp.bfloat16)
        low = (product - high.astype(jnp.float32)).astype(jnp.bfloat16)
        total = jnp.dot(high, ones, preferred_element_type=jnp.float32)
        total += jnp.dot(low, ones, preferred_element_type=jnp.float32)
        delta_ref[group * GROUP : (group + 1) * GROUP, :] = total.T[:GROUP]


def delta_rows(outputs, grad_out, queries):
    rows = outputs.shape[0]
    local = pl.BlockSpec(memory_space=pltpu.VMEM)
    return pl.pallas_call(
        delta_kernel,
        in_specs=[local] * 3,
        out_specs=local,
        out_shape=jax.ShapeDtypeStruct((HEADS, rows), jnp.float32),
        compiler_params=pltpu.CompilerParams(vmem_limit_bytes=VMEM),
        cost_estimate=pl.CostEstimate(
            flops=4 * rows * HEADS * HDIM * HDIM,
            bytes_accessed=6 * rows * HEADS * HDIM,
            transcendentals=0,
        ),
        name="delta",
    )(outputs, grad_out, queries)


def slot_shards(me, hops):
    side = lax.rem(me, 2)
    found = [me - 2 * hop for hop in range(hops + 1)]
    found += [me - 2 * hop + 1 - 2 * side for hop in range(1, hops)]
    found.append(jnp.where(side == 1, me - 1, me - 2 * hops + 1))
    return found


def attend_kernel(hops, joined, aliased, first, places, docs, q_ref, gout_ref, lse_ref, delta_ref, *refs):
    slots = 2 * hops + 1
    moved, refs = refs[:slots], refs[slots + aliased :]
    grad_queries, refs = refs[0], refs[1:]
    if joined:
        parts = refs[: hops + 1] + tuple(refs[hops + 1].at[hop] for hop in range(hops))
    else:
        parts = refs[:slots]
    k_all, v_all, bias, prob, score, gq_ref, sems = refs[-7:]
    rows = q_ref.shape[0]
    heads = moved[0].shape[-1] // HDIM
    scale = 1.0 / HDIM**0.5
    me = lax.axis_index("seq")

    token = lax.broadcasted_iota(jnp.int32, (1, rows), 1) + me * rows
    begin = jnp.zeros((1, rows), jnp.int32)
    bound = jnp.int32(0)
    for doc in range(docs.shape[0]):
        bound = bound + docs[doc]
        begin = jnp.where(token >= bound, bound, begin)
    row = lax.broadcasted_iota(jnp.int32, (rows, rows), 0)
    for slot, shard in enumerate(slot_shards(me, hops)):
        key = row + shard * rows
        visible = (key <= token) & (key >= begin)
        bias[slot * rows : (slot + 1) * rows, :] = jnp.where(visible, 0.0, -1e30)

    def put(index):
        wide = pl.ds(pl.multiple_of((first + index) * GROUP * HDIM, GROUP * HDIM), GROUP * HDIM)
        return pltpu.make_async_copy(gq_ref.at[index], grad_queries.at[:, wide], sems.at[index])

    @pl.loop(0, heads)
    def _(index):
        column = pl.ds(pl.multiple_of(index * HDIM, HDIM), HDIM)
        wide = pl.ds(pl.multiple_of((first + index) * GROUP * HDIM, GROUP * HDIM), GROUP * HDIM)
        stat = pl.ds(pl.multiple_of((first + index) * GROUP, GROUP), GROUP)
        for slot in range(slots):
            here = slice(slot * rows, (slot + 1) * rows)
            pair = moved[slot] if places[slot] is None else moved[slot].at[places[slot]]
            k_all[here, :] = pair[0, :, column]
            v_all[here, :] = pair[1, :, column]
        queries = head_rows(q_ref[:, wide])
        gout = head_rows(gout_ref[:, wide])
        lses = lse_ref[stat, :]
        deltas = delta_ref[stat, :]
        keys = k_all[...]
        values = v_all[...]
        hidden = bias[...]
        hidden = jnp.concatenate([hidden, hidden], axis=1)
        for two in range(GROUP // 2):
            at = slice(2 * two * rows, (2 * two + 2) * rows)
            lse = jnp.concatenate([lses[2 * two : 2 * two + 1], lses[2 * two + 1 : 2 * two + 2]], axis=1)
            delta = jnp.concatenate(
                [deltas[2 * two : 2 * two + 1], deltas[2 * two + 1 : 2 * two + 2]], axis=1
            )
            raw = contract_last(keys, queries[at])
            attn = jnp.exp(raw * scale - lse + hidden)
            grad = contract_last(values, gout[at])
            prob[:, at] = attn.astype(jnp.bfloat16)
            score[:, at] = (attn * (grad - delta)).astype(jnp.bfloat16)
        scores = score[...]
        grad_k = jnp.dot(scores, queries, preferred_element_type=jnp.float32) * scale
        grad_v = jnp.dot(prob[...], gout, preferred_element_type=jnp.float32)
        for slot in range(slots):
            here = slice(slot * rows, (slot + 1) * rows)
            part = parts[slot]
            part[0, :, column] = grad_k[here].astype(part.dtype)
            part[1, :, column] = grad_v[here].astype(part.dtype)
        grad_q = (contract_first(keys, scores) * scale).astype(jnp.bfloat16)
        gq_ref[index] = jnp.concatenate(
            [grad_q[:, h * rows : (h + 1) * rows].T for h in range(GROUP)], axis=1
        )
        put(index).start()

    for index in range(heads):
        put(index).wait()


def attend(docs, queries, grad_out, lse, delta, moved, grad_q, head, per, hops, joined):
    rows = queries.shape[0]
    slots = 2 * hops + 1
    local = pl.BlockSpec(memory_space=pltpu.VMEM)
    operands = [docs, queries, grad_out, lse, delta] + [array for array, index in moved]
    anywhere = pl.BlockSpec(memory_space=pl.ANY)
    in_specs = [pl.BlockSpec(memory_space=pltpu.SMEM)] + [local] * (len(operands) - 1)
    aliases = {}
    if grad_q is not None:
        operands.append(grad_q)
        in_specs.append(anywhere)
        aliases = {len(operands) - 1: 0}
    out_shape = [jax.ShapeDtypeStruct(queries.shape, jnp.bfloat16)]
    out_shape += [jax.ShapeDtypeStruct((2, rows, per * HDIM), jnp.bfloat16)] * (hops + 1)
    if joined:
        out_shape += [jax.ShapeDtypeStruct((hops, 2, rows, per * HDIM), jnp.bfloat16)]
    else:
        out_shape += [jax.ShapeDtypeStruct((2, rows, per * HDIM), jnp.bfloat16)] * hops
    pairs = slots * rows * rows * GROUP * per
    places = [index for array, index in moved]
    return pl.pallas_call(
        functools.partial(attend_kernel, hops, joined, len(aliases), head, places),
        in_specs=in_specs,
        out_specs=[anywhere] + [local] * (len(out_shape) - 1),
        scratch_shapes=[
            pltpu.VMEM((slots * rows, HDIM), jnp.bfloat16),
            pltpu.VMEM((slots * rows, HDIM), jnp.bfloat16),
            pltpu.VMEM((slots * rows, rows), jnp.float32),
            pltpu.VMEM((slots * rows, GROUP * rows), jnp.bfloat16),
            pltpu.VMEM((slots * rows, GROUP * rows), jnp.bfloat16),
            pltpu.VMEM((per, rows, GROUP * HDIM), jnp.bfloat16),
            pltpu.SemaphoreType.DMA((per,)),
        ],
        out_shape=out_shape,
        input_output_aliases=aliases,
        compiler_params=pltpu.CompilerParams(vmem_limit_bytes=VMEM),
        cost_estimate=pl.CostEstimate(
            flops=40 * pairs * HDIM,
            bytes_accessed=per * rows * HDIM * 2 * (3 * GROUP + 6 * slots),
            transcendentals=pairs,
        ),
        name="attend",
    )(*operands)


def finish_kernel(chunks, *refs):
    key_ref, value_ref = refs[-2:]
    refs = refs[:-2]
    keep = jnp.where(lax.rem(lax.axis_index("seq"), 2) == 0, 1.0, 0.0)
    for start, done in chunks:
        if done:
            total, refs = refs[0][...], refs[1:]
        else:
            own, edge, far = (ref[...].astype(jnp.float32) for ref in refs[:3])
            total, refs = (own + edge * keep + far).astype(jnp.bfloat16), refs[3:]
        key_ref[:, start : start + total.shape[2]] = total[0]
        value_ref[:, start : start + total.shape[2]] = total[1]


def finish(sums, shape):
    operands, chunks, start = [], [], 0
    for part in sums:
        chunks.append((start, len(part) == 1))
        start += part[0].shape[2]
        operands += part
    local = pl.BlockSpec(memory_space=pltpu.VMEM)
    return pl.pallas_call(
        functools.partial(finish_kernel, chunks),
        in_specs=[local] * len(operands),
        out_specs=[local] * 2,
        out_shape=[jax.ShapeDtypeStruct(shape, jnp.bfloat16)] * 2,
        compiler_params=pltpu.CompilerParams(vmem_limit_bytes=VMEM),
        cost_estimate=pl.CostEstimate(
            flops=8 * shape[0] * shape[1], bytes_accessed=16 * shape[0] * shape[1], transcendentals=0
        ),
        name="finish",
    )(*operands)


def shards(queries, keys, values, outputs, grad_out, lse_saved, doc_lengths):
    seq = lax.axis_size("seq")
    me = lax.axis_index("seq").astype(jnp.int32)
    side = lax.rem(me, 2)
    hops = seq // 4
    def onward(hop):
        return [(s, s + 2) for s in range(2 * hop - 2, seq - 2)]

    def back(hop):
        return [(s, s - 2) for s in range(2 * hop, seq)]

    def to_odd(hop):
        return [(s, s + 1) for s in range(2 * hop, seq, 2)]

    def to_even(hop):
        return [(s + 1, s) for s in range(2 * hop, seq, 2)]

    def send(array, pairs):
        return lax.ppermute(array, "seq", pairs)

    def after(array, *others):
        return lax.optimization_barrier((array,) + others)[0]

    delta = delta_rows(outputs, grad_out, queries)
    lse = lse_saved.T
    heads = [sum(CHUNKS[:chunk]) for chunk in range(len(CHUNKS))]
    columns = []
    for head, per in zip(heads, CHUNKS):
        at = slice(head * HDIM, (head + per) * HDIM)
        own = lax.optimization_barrier(jnp.stack([keys[:, at], values[:, at]]))
        columns.append([own, send(own, onward(1))])
        columns[-1][1], delta = lax.optimization_barrier((columns[-1][1], delta))
    for column in columns:
        for hop in range(2, hops + 1):
            column.append(send(column[-1], onward(hop)))
    arrived = []
    for chunk, column in enumerate(columns):
        edge = jnp.where(side == 0, column[0], column[hops])
        moved = [(array, None) for array in column]
        if chunk == 0:
            crossed = [send(array, to_odd(1) + to_even(1)) for array in column[1:hops]]
            crossed.append(send(after(edge, *crossed), to_odd(0) + to_even(hops)))
            moved += [(array, None) for array in crossed]
        else:
            joint = jnp.stack(column[1:hops] + [edge])
            crossed = send(joint, to_odd(0) + to_even(1))
            moved += [(crossed, hop) for hop in range(hops)]
            arrived[0][-1] = (after(arrived[0][-1][0], joint), None)
        arrived.append(moved)

    wide, half = jnp.float32, jnp.bfloat16
    grad_q, sums, outputs_of = None, [], []
    for chunk, (head, per) in enumerate(zip(heads, CHUNKS)):
        joined = chunk < len(CHUNKS) - 1
        grad_q, *parts = attend(
            doc_lengths, queries, grad_out, lse, delta, arrived[chunk], grad_q, head, per, hops, joined
        )
        outputs_of.append((parts[: hops + 1], parts[hops + 1 :], joined))
    swapped = []
    for column, crossed, joined in outputs_of:
        if joined:
            crossed = send(crossed[0], to_odd(1) + to_even(0))
            crossed = after(crossed, outputs_of[-1][1][-1])
            edge = crossed[hops - 1]
        else:
            edge = send(crossed[-1], to_odd(hops) + to_even(0))
            crossed = [
                send(after(crossed[hop - 1], swapped[0][2]), to_odd(hop) + to_even(hop))
                for hop in range(1, hops)
            ]
        edge = edge.astype(wide)
        total = column[hops].astype(wide) + jnp.where(side == 1, edge, 0.0)
        swapped.append((crossed, edge, total.astype(half)))
    before = []
    for (column, _, joined), (crossed, edge, total) in zip(outputs_of, swapped):
        for hop in range(hops - 1, -1, -1):
            if joined:
                if hop == 0 and hops > 1:
                    total = after(total, *swapped[-1][0])
                before.append(total)
            elif hop == 0:
                total = after(total, *before)
            far = send(total, back(hop + 1)).astype(wide)
            if hop:
                total = column[hop].astype(wide) + crossed[hop - 1].astype(wide) + far
                total = total.astype(half)
        if joined:
            total = column[0].astype(wide) + jnp.where(side == 0, edge, 0.0) + far
            sums.append([total.astype(half)])
        else:
            sums.append([column[0], edge.astype(half), far.astype(half)])
    grad_keys, grad_values = finish(sums, keys.shape)
    return (grad_q, grad_keys, grad_values)


def solution(mesh):
    rows = P(("packs", "seq"), None)
    return jax.shard_map(
        shards,
        mesh=mesh,
        in_specs=(rows, rows, rows, rows, rows, rows, P("packs")),
        out_specs=(rows, rows, rows),
        check_vma=False,
    )
```

```python
import functools

import jax
import jax.numpy as jnp
from jax import lax
from jax.experimental import pallas as pl
from jax.experimental.pallas import tpu as pltpu
from jax.sharding import PartitionSpec as P

HEADS = 64
KVH = 8
HDIM = 128
GROUP = HEADS // KVH
CHUNKS = (4, 4)
VMEM = 16 * 1024 * 1024


def contract_last(first, second):
    return lax.dot_general(
        first, second, (((1,), (1,)), ((), ())), preferred_element_type=jnp.float32
    )


def contract_first(first, second):
    return lax.dot_general(
        first, second, (((0,), (0,)), ((), ())), preferred_element_type=jnp.float32
    )


def head_rows(block):
    return jnp.concatenate(
        [block[:, h * HDIM : (h + 1) * HDIM] for h in range(GROUP)], axis=0
    )


def delta_kernel(out_ref, gout_ref, q_ref, delta_ref):
    rows = out_ref.shape[0]
    wide = GROUP * HDIM
    first = lax.broadcasted_iota(jnp.int32, (wide, HDIM), 1) * HDIM
    row = lax.broadcasted_iota(jnp.int32, (wide, HDIM), 0)
    ones = jnp.where((row >= first) & (row < first + HDIM), 1.0, 0.0).astype(jnp.bfloat16)
    for group in range(out_ref.shape[1] // wide):
        at = slice(group * wide, (group + 1) * wide)
        product = out_ref[:, at].astype(jnp.float32) * gout_ref[:, at].astype(jnp.float32)
        high = product.astype(jnp.bfloat16)
        low = (product - high.astype(jnp.float32)).astype(jnp.bfloat16)
        total = jnp.dot(high, ones, preferred_element_type=jnp.float32)
        total += jnp.dot(low, ones, preferred_element_type=jnp.float32)
        delta_ref[group * GROUP : (group + 1) * GROUP, :] = total.T[:GROUP]


def delta_rows(outputs, grad_out, queries):
    rows = outputs.shape[0]
    local = pl.BlockSpec(memory_space=pltpu.VMEM)
    return pl.pallas_call(
        delta_kernel,
        in_specs=[local] * 3,
        out_specs=local,
        out_shape=jax.ShapeDtypeStruct((HEADS, rows), jnp.float32),
        compiler_params=pltpu.CompilerParams(vmem_limit_bytes=VMEM),
        cost_estimate=pl.CostEstimate(
            flops=4 * rows * HEADS * HDIM * HDIM,
            bytes_accessed=6 * rows * HEADS * HDIM,
            transcendentals=0,
        ),
        name="delta",
    )(outputs, grad_out, queries)


def slot_shards(me, hops):
    side = lax.rem(me, 2)
    found = [me - 2 * hop for hop in range(hops + 1)]
    found += [me - 2 * hop + 1 - 2 * side for hop in range(1, hops)]
    found.append(jnp.where(side == 1, me - 1, me - 2 * hops + 1))
    return found


def attend_kernel(hops, joined, aliased, first, places, docs, q_ref, gout_ref, lse_ref, delta_ref, *refs):
    slots = 2 * hops + 1
    moved, refs = refs[:slots], refs[slots + aliased :]
    grad_queries, refs = refs[0], refs[1:]
    if joined:
        parts = refs[: hops + 1] + tuple(refs[hops + 1].at[hop] for hop in range(hops))
    else:
        parts = refs[:slots]
    k_all, v_all, bias, prob, score, gq_ref, sems = refs[-7:]
    rows = q_ref.shape[0]
    heads = moved[0].shape[-1] // HDIM
    scale = 1.0 / HDIM**0.5
    me = lax.axis_index("seq")

    token = lax.broadcasted_iota(jnp.int32, (1, rows), 1) + me * rows
    begin = jnp.zeros((1, rows), jnp.int32)
    bound = jnp.int32(0)
    for doc in range(docs.shape[0]):
        bound = bound + docs[doc]
        begin = jnp.where(token >= bound, bound, begin)
    row = lax.broadcasted_iota(jnp.int32, (rows, rows), 0)
    for slot, shard in enumerate(slot_shards(me, hops)):
        key = row + shard * rows
        visible = (key <= token) & (key >= begin)
        bias[slot * rows : (slot + 1) * rows, :] = jnp.where(visible, 0.0, -1e30)

    def put(index):
        wide = pl.ds(pl.multiple_of((first + index) * GROUP * HDIM, GROUP * HDIM), GROUP * HDIM)
        return pltpu.make_async_copy(gq_ref.at[index], grad_queries.at[:, wide], sems.at[index])

    @pl.loop(0, heads)
    def _(index):
        column = pl.ds(pl.multiple_of(index * HDIM, HDIM), HDIM)
        wide = pl.ds(pl.multiple_of((first + index) * GROUP * HDIM, GROUP * HDIM), GROUP * HDIM)
        stat = pl.ds(pl.multiple_of((first + index) * GROUP, GROUP), GROUP)
        for slot in range(slots):
            here = slice(slot * rows, (slot + 1) * rows)
            pair = moved[slot] if places[slot] is None else moved[slot].at[places[slot]]
            k_all[here, :] = pair[0, :, column]
            v_all[here, :] = pair[1, :, column]
        queries = head_rows(q_ref[:, wide])
        gout = head_rows(gout_ref[:, wide])
        lses = lse_ref[stat, :]
        deltas = delta_ref[stat, :]
        keys = k_all[...]
        values = v_all[...]
        hidden = bias[...]
        hidden = jnp.concatenate([hidden, hidden], axis=1)
        for two in range(GROUP // 2):
            at = slice(2 * two * rows, (2 * two + 2) * rows)
            lse = jnp.concatenate([lses[2 * two : 2 * two + 1], lses[2 * two + 1 : 2 * two + 2]], axis=1)
            delta = jnp.concatenate(
                [deltas[2 * two : 2 * two + 1], deltas[2 * two + 1 : 2 * two + 2]], axis=1
            )
            raw = contract_last(keys, queries[at])
            attn = jnp.exp(raw * scale - lse + hidden)
            grad = contract_last(values, gout[at])
            prob[:, at] = attn.astype(jnp.bfloat16)
            score[:, at] = (attn * (grad - delta)).astype(jnp.bfloat16)
        scores = score[...]
        grad_k = jnp.dot(scores, queries, preferred_element_type=jnp.float32) * scale
        grad_v = jnp.dot(prob[...], gout, preferred_element_type=jnp.float32)
        for slot in range(slots):
            here = slice(slot * rows, (slot + 1) * rows)
            part = parts[slot]
            part[0, :, column] = grad_k[here].astype(part.dtype)
            part[1, :, column] = grad_v[here].astype(part.dtype)
        grad_q = (contract_first(keys, scores) * scale).astype(jnp.bfloat16)
        gq_ref[index] = jnp.concatenate(
            [grad_q[:, h * rows : (h + 1) * rows].T for h in range(GROUP)], axis=1
        )
        put(index).start()

    for index in range(heads):
        put(index).wait()


def attend(docs, queries, grad_out, lse, delta, moved, grad_q, head, per, hops, joined):
    rows = queries.shape[0]
    slots = 2 * hops + 1
    local = pl.BlockSpec(memory_space=pltpu.VMEM)
    operands = [docs, queries, grad_out, lse, delta] + [array for array, index in moved]
    anywhere = pl.BlockSpec(memory_space=pl.ANY)
    in_specs = [pl.BlockSpec(memory_space=pltpu.SMEM)] + [local] * (len(operands) - 1)
    aliases = {}
    if grad_q is not None:
        operands.append(grad_q)
        in_specs.append(anywhere)
        aliases = {len(operands) - 1: 0}
    out_shape = [jax.ShapeDtypeStruct(queries.shape, jnp.bfloat16)]
    out_shape += [jax.ShapeDtypeStruct((2, rows, per * HDIM), jnp.bfloat16)] * (hops + 1)
    if joined:
        out_shape += [jax.ShapeDtypeStruct((hops, 2, rows, per * HDIM), jnp.bfloat16)]
    else:
        out_shape += [jax.ShapeDtypeStruct((2, rows, per * HDIM), jnp.bfloat16)] * hops
    pairs = slots * rows * rows * GROUP * per
    places = [index for array, index in moved]
    return pl.pallas_call(
        functools.partial(attend_kernel, hops, joined, len(aliases), head, places),
        in_specs=in_specs,
        out_specs=[anywhere] + [local] * (len(out_shape) - 1),
        scratch_shapes=[
            pltpu.VMEM((slots * rows, HDIM), jnp.bfloat16),
            pltpu.VMEM((slots * rows, HDIM), jnp.bfloat16),
            pltpu.VMEM((slots * rows, rows), jnp.float32),
            pltpu.VMEM((slots * rows, GROUP * rows), jnp.bfloat16),
            pltpu.VMEM((slots * rows, GROUP * rows), jnp.bfloat16),
            pltpu.VMEM((per, rows, GROUP * HDIM), jnp.bfloat16),
            pltpu.SemaphoreType.DMA((per,)),
        ],
        out_shape=out_shape,
        input_output_aliases=aliases,
        compiler_params=pltpu.CompilerParams(vmem_limit_bytes=VMEM),
        cost_estimate=pl.CostEstimate(
            flops=40 * pairs * HDIM,
            bytes_accessed=per * rows * HDIM * 2 * (3 * GROUP + 6 * slots),
            transcendentals=pairs,
        ),
        name="attend",
    )(*operands)


def finish_kernel(chunks, *refs):
    key_ref, value_ref = refs[-2:]
    refs = refs[:-2]
    keep = jnp.where(lax.rem(lax.axis_index("seq"), 2) == 0, 1.0, 0.0)
    for start, done in chunks:
        if done:
            total, refs = refs[0][...], refs[1:]
        else:
            own, edge, far = (ref[...].astype(jnp.float32) for ref in refs[:3])
            total, refs = (own + edge * keep + far).astype(jnp.bfloat16), refs[3:]
        key_ref[:, start : start + total.shape[2]] = total[0]
        value_ref[:, start : start + total.shape[2]] = total[1]


def finish(sums, shape):
    operands, chunks, start = [], [], 0
    for part in sums:
        chunks.append((start, len(part) == 1))
        start += part[0].shape[2]
        operands += part
    local = pl.BlockSpec(memory_space=pltpu.VMEM)
    return pl.pallas_call(
        functools.partial(finish_kernel, chunks),
        in_specs=[local] * len(operands),
        out_specs=[local] * 2,
        out_shape=[jax.ShapeDtypeStruct(shape, jnp.bfloat16)] * 2,
        compiler_params=pltpu.CompilerParams(vmem_limit_bytes=VMEM),
        cost_estimate=pl.CostEstimate(
            flops=8 * shape[0] * shape[1], bytes_accessed=16 * shape[0] * shape[1], transcendentals=0
        ),
        name="finish",
    )(*operands)


def shards(queries, keys, values, outputs, grad_out, lse_saved, doc_lengths):
    seq = lax.axis_size("seq")
    me = lax.axis_index("seq").astype(jnp.int32)
    side = lax.rem(me, 2)
    even, odd = side == 0, side == 1
    hops = seq // 4
    def onward(hop):
        return [(s, s + 2) for s in range(2 * hop - 2, seq - 2)]

    def back(hop):
        return [(s, s - 2) for s in range(2 * hop, seq)]

    def to_odd(hop):
        return [(s, s + 1) for s in range(2 * hop, seq, 2)]

    def to_even(hop):
        return [(s + 1, s) for s in range(2 * hop, seq, 2)]

    def send(array, pairs):
        return lax.ppermute(array, "seq", pairs)

    def after(array, *others):
        return lax.optimization_barrier((array,) + others)[0]

    delta = delta_rows(outputs, grad_out, queries)
    lse = lse_saved.T
    heads = [sum(CHUNKS[:chunk]) for chunk in range(len(CHUNKS))]
    columns = []
    for head, per in zip(heads, CHUNKS):
        at = slice(head * HDIM, (head + per) * HDIM)
        own = jnp.stack([keys[:, at], values[:, at]])
        own, even, odd = lax.optimization_barrier((own, even, odd))
        columns.append([own, send(own, onward(1))])
        columns[-1][1], delta = lax.optimization_barrier((columns[-1][1], delta))
    for column in columns:
        for hop in range(2, hops + 1):
            column.append(send(column[-1], onward(hop)))
    arrived = []
    for chunk, column in enumerate(columns):
        edge = jnp.where(even, column[0], column[hops])
        moved = [(array, None) for array in column]
        if chunk == 0:
            crossed = [send(array, to_odd(1) + to_even(1)) for array in column[1:hops]]
            crossed.append(send(after(edge, *crossed), to_odd(0) + to_even(hops)))
            moved += [(array, None) for array in crossed]
        else:
            joint = jnp.stack(column[1:hops] + [edge])
            crossed = send(joint, to_odd(0) + to_even(1))
            moved += [(crossed, hop) for hop in range(hops)]
            arrived[0][-1] = (after(arrived[0][-1][0], joint), None)
        arrived.append(moved)

    wide, half = jnp.float32, jnp.bfloat16
    grad_q, sums, outputs_of = None, [], []
    for chunk, (head, per) in enumerate(zip(heads, CHUNKS)):
        joined = chunk < len(CHUNKS) - 1
        grad_q, *parts = attend(
            doc_lengths, queries, grad_out, lse, delta, arrived[chunk], grad_q, head, per, hops, joined
        )
        outputs_of.append((parts[: hops + 1], parts[hops + 1 :], joined))
    swapped = []
    for column, crossed, joined in outputs_of:
        if joined:
            crossed = send(crossed[0], to_odd(1) + to_even(0))
            crossed = after(crossed, outputs_of[-1][1][-1])
            edge = crossed[hops - 1]
        else:
            edge = send(crossed[-1], to_odd(hops) + to_even(0))
            crossed = [
                send(after(crossed[hop - 1], swapped[0][2]), to_odd(hop) + to_even(hop))
                for hop in range(1, hops)
            ]
        edge = edge.astype(wide)
        total = column[hops].astype(wide) + jnp.where(odd, edge, 0.0)
        swapped.append((crossed, edge, total.astype(half)))
    before = []
    for (column, _, joined), (crossed, edge, total) in zip(outputs_of, swapped):
        for hop in range(hops - 1, -1, -1):
            if joined:
                if hop == 0 and hops > 1:
                    total = after(total, *swapped[-1][0])
                before.append(total)
            elif hop == 0:
                total = after(total, *before)
            far = send(total, back(hop + 1)).astype(wide)
            if hop:
                total = column[hop].astype(wide) + crossed[hop - 1].astype(wide) + far
                total = total.astype(half)
        if joined:
            total = column[0].astype(wide) + jnp.where(even, edge, 0.0) + far
            sums.append([total.astype(half)])
        else:
            sums.append([column[0], edge.astype(half), far.astype(half)])
    grad_keys, grad_values = finish(sums, keys.shape)
    return (grad_q, grad_keys, grad_values)


def solution(mesh):
    rows = P(("packs", "seq"), None)
    return jax.shard_map(
        shards,
        mesh=mesh,
        in_specs=(rows, rows, rows, rows, rows, rows, P("packs")),
        out_specs=(rows, rows, rows),
        check_vma=False,
    )
```

```python
import functools

import jax
import jax.numpy as jnp
from jax import lax
from jax.experimental import pallas as pl
from jax.experimental.pallas import tpu as pltpu
from jax.sharding import PartitionSpec as P

HEADS = 64
KVH = 8
HDIM = 128
GROUP = HEADS // KVH
CHUNKS = (4, 4)
VMEM = 16 * 1024 * 1024


def contract_last(first, second):
    return lax.dot_general(
        first, second, (((1,), (1,)), ((), ())), preferred_element_type=jnp.float32
    )


def contract_first(first, second):
    return lax.dot_general(
        first, second, (((0,), (0,)), ((), ())), preferred_element_type=jnp.float32
    )


def head_rows(block):
    return jnp.concatenate(
        [block[:, h * HDIM : (h + 1) * HDIM] for h in range(GROUP)], axis=0
    )


def delta_kernel(out_ref, gout_ref, q_ref, delta_ref):
    rows = out_ref.shape[0]
    wide = GROUP * HDIM
    first = lax.broadcasted_iota(jnp.int32, (wide, HDIM), 1) * HDIM
    row = lax.broadcasted_iota(jnp.int32, (wide, HDIM), 0)
    ones = jnp.where((row >= first) & (row < first + HDIM), 1.0, 0.0).astype(jnp.bfloat16)
    for group in range(out_ref.shape[1] // wide):
        at = slice(group * wide, (group + 1) * wide)
        product = out_ref[:, at].astype(jnp.float32) * gout_ref[:, at].astype(jnp.float32)
        high = product.astype(jnp.bfloat16)
        low = (product - high.astype(jnp.float32)).astype(jnp.bfloat16)
        total = jnp.dot(high, ones, preferred_element_type=jnp.float32)
        total += jnp.dot(low, ones, preferred_element_type=jnp.float32)
        delta_ref[group * GROUP : (group + 1) * GROUP, :] = total.T[:GROUP]


def delta_rows(outputs, grad_out, queries):
    rows = outputs.shape[0]
    local = pl.BlockSpec(memory_space=pltpu.VMEM)
    return pl.pallas_call(
        delta_kernel,
        in_specs=[local] * 3,
        out_specs=local,
        out_shape=jax.ShapeDtypeStruct((HEADS, rows), jnp.float32),
        compiler_params=pltpu.CompilerParams(vmem_limit_bytes=VMEM),
        cost_estimate=pl.CostEstimate(
            flops=4 * rows * HEADS * HDIM * HDIM,
            bytes_accessed=6 * rows * HEADS * HDIM,
            transcendentals=0,
        ),
        name="delta",
    )(outputs, grad_out, queries)


def slot_shards(me, hops):
    side = lax.rem(me, 2)
    found = [me - 2 * hop for hop in range(hops + 1)]
    found += [me - 2 * hop + 1 - 2 * side for hop in range(1, hops)]
    found.append(jnp.where(side == 1, me - 1, me - 2 * hops + 1))
    return found


def attend_kernel(hops, joined, first, places, docs, q_ref, gout_ref, lse_ref, delta_ref, *refs):
    slots = 2 * hops + 1
    moved, refs = refs[:slots], refs[slots:]
    gq_ref, refs = refs[0], refs[1:]
    if joined:
        parts = refs[: hops + 1] + tuple(refs[hops + 1].at[hop] for hop in range(hops))
    else:
        parts = refs[:slots]
    k_all, v_all, bias, prob, score = refs[-5:]
    rows = q_ref.shape[0]
    heads = moved[0].shape[-1] // HDIM
    scale = 1.0 / HDIM**0.5
    me = lax.axis_index("seq")

    token = lax.broadcasted_iota(jnp.int32, (1, rows), 1) + me * rows
    begin = jnp.zeros((1, rows), jnp.int32)
    bound = jnp.int32(0)
    for doc in range(docs.shape[0]):
        bound = bound + docs[doc]
        begin = jnp.where(token >= bound, bound, begin)
    row = lax.broadcasted_iota(jnp.int32, (rows, rows), 0)
    for slot, shard in enumerate(slot_shards(me, hops)):
        key = row + shard * rows
        visible = (key <= token) & (key >= begin)
        bias[slot * rows : (slot + 1) * rows, :] = jnp.where(visible, 0.0, -1e30)

    @pl.loop(0, heads)
    def _(index):
        column = pl.ds(pl.multiple_of(index * HDIM, HDIM), HDIM)
        wide = pl.ds(pl.multiple_of((first + index) * GROUP * HDIM, GROUP * HDIM), GROUP * HDIM)
        stat = pl.ds(pl.multiple_of((first + index) * GROUP, GROUP), GROUP)
        for slot in range(slots):
            here = slice(slot * rows, (slot + 1) * rows)
            pair = moved[slot] if places[slot] is None else moved[slot].at[places[slot]]
            k_all[here, :] = pair[0, :, column]
            v_all[here, :] = pair[1, :, column]
        queries = head_rows(q_ref[:, wide])
        gout = head_rows(gout_ref[:, wide])
        lses = lse_ref[stat, :]
        deltas = delta_ref[stat, :]
        keys = k_all[...]
        values = v_all[...]
        hidden = bias[...]
        hidden = jnp.concatenate([hidden, hidden], axis=1)
        for two in range(GROUP // 2):
            at = slice(2 * two * rows, (2 * two + 2) * rows)
            lse = jnp.concatenate([lses[2 * two : 2 * two + 1], lses[2 * two + 1 : 2 * two + 2]], axis=1)
            delta = jnp.concatenate(
                [deltas[2 * two : 2 * two + 1], deltas[2 * two + 1 : 2 * two + 2]], axis=1
            )
            raw = contract_last(keys, queries[at])
            attn = jnp.exp(raw * scale - lse + hidden)
            grad = contract_last(values, gout[at])
            prob[:, at] = attn.astype(jnp.bfloat16)
            score[:, at] = (attn * (grad - delta)).astype(jnp.bfloat16)
        scores = score[...]
        grad_k = jnp.dot(scores, queries, preferred_element_type=jnp.float32) * scale
        grad_v = jnp.dot(prob[...], gout, preferred_element_type=jnp.float32)
        for slot in range(slots):
            here = slice(slot * rows, (slot + 1) * rows)
            part = parts[slot]
            part[0, :, column] = grad_k[here].astype(part.dtype)
            part[1, :, column] = grad_v[here].astype(part.dtype)
        grad_q = (contract_first(keys, scores) * scale).astype(jnp.bfloat16)
        mine = pl.ds(pl.multiple_of(index * GROUP * HDIM, GROUP * HDIM), GROUP * HDIM)
        gq_ref[:, mine] = jnp.concatenate(
            [grad_q[:, h * rows : (h + 1) * rows].T for h in range(GROUP)], axis=1
        )


def attend(docs, queries, grad_out, lse, delta, moved, head, per, hops, joined):
    rows = queries.shape[0]
    slots = 2 * hops + 1
    local = pl.BlockSpec(memory_space=pltpu.VMEM)
    operands = [docs, queries, grad_out, lse, delta] + [array for array, index in moved]
    in_specs = [pl.BlockSpec(memory_space=pltpu.SMEM)] + [local] * (len(operands) - 1)
    out_shape = [jax.ShapeDtypeStruct((rows, per * GROUP * HDIM), jnp.bfloat16)]
    out_shape += [jax.ShapeDtypeStruct((2, rows, per * HDIM), jnp.bfloat16)] * (hops + 1)
    if joined:
        out_shape += [jax.ShapeDtypeStruct((hops, 2, rows, per * HDIM), jnp.bfloat16)]
    else:
        out_shape += [jax.ShapeDtypeStruct((2, rows, per * HDIM), jnp.bfloat16)] * hops
    pairs = slots * rows * rows * GROUP * per
    places = [index for array, index in moved]
    return pl.pallas_call(
        functools.partial(attend_kernel, hops, joined, head, places),
        in_specs=in_specs,
        out_specs=[local] * len(out_shape),
        scratch_shapes=[
            pltpu.VMEM((slots * rows, HDIM), jnp.bfloat16),
            pltpu.VMEM((slots * rows, HDIM), jnp.bfloat16),
            pltpu.VMEM((slots * rows, rows), jnp.float32),
            pltpu.VMEM((slots * rows, GROUP * rows), jnp.bfloat16),
            pltpu.VMEM((slots * rows, GROUP * rows), jnp.bfloat16),
        ],
        out_shape=out_shape,
        compiler_params=pltpu.CompilerParams(vmem_limit_bytes=VMEM),
        cost_estimate=pl.CostEstimate(
            flops=40 * pairs * HDIM,
            bytes_accessed=per * rows * HDIM * 2 * (3 * GROUP + 6 * slots),
            transcendentals=pairs,
        ),
        name="attend",
    )(*operands)


def finish_kernel(chunks, *refs):
    key_ref, value_ref = refs[-2:]
    refs = refs[:-2]
    keep = jnp.where(lax.rem(lax.axis_index("seq"), 2) == 0, 1.0, 0.0)
    for start, done in chunks:
        if done:
            total, refs = refs[0][...], refs[1:]
        else:
            own, edge, far = (ref[...].astype(jnp.float32) for ref in refs[:3])
            total, refs = (own + edge * keep + far).astype(jnp.bfloat16), refs[3:]
        key_ref[:, start : start + total.shape[2]] = total[0]
        value_ref[:, start : start + total.shape[2]] = total[1]


def finish(sums, shape):
    operands, chunks, start = [], [], 0
    for part in sums:
        chunks.append((start, len(part) == 1))
        start += part[0].shape[2]
        operands += part
    local = pl.BlockSpec(memory_space=pltpu.VMEM)
    return pl.pallas_call(
        functools.partial(finish_kernel, chunks),
        in_specs=[local] * len(operands),
        out_specs=[local] * 2,
        out_shape=[jax.ShapeDtypeStruct(shape, jnp.bfloat16)] * 2,
        compiler_params=pltpu.CompilerParams(vmem_limit_bytes=VMEM),
        cost_estimate=pl.CostEstimate(
            flops=8 * shape[0] * shape[1], bytes_accessed=16 * shape[0] * shape[1], transcendentals=0
        ),
        name="finish",
    )(*operands)


def shards(queries, keys, values, outputs, grad_out, lse_saved, doc_lengths):
    seq = lax.axis_size("seq")
    me = lax.axis_index("seq").astype(jnp.int32)
    side = lax.rem(me, 2)
    keys, values, even, odd = lax.optimization_barrier((keys, values, side == 0, side == 1))
    hops = seq // 4
    def onward(hop):
        return [(s, s + 2) for s in range(2 * hop - 2, seq - 2)]

    def back(hop):
        return [(s, s - 2) for s in range(2 * hop, seq)]

    def to_odd(hop):
        return [(s, s + 1) for s in range(2 * hop, seq, 2)]

    def to_even(hop):
        return [(s + 1, s) for s in range(2 * hop, seq, 2)]

    def send(array, pairs):
        return lax.ppermute(array, "seq", pairs)

    def after(array, *others):
        return lax.optimization_barrier((array,) + others)[0]

    delta = delta_rows(outputs, grad_out, queries)
    lse = lse_saved.T
    heads = [sum(CHUNKS[:chunk]) for chunk in range(len(CHUNKS))]
    columns = []
    for head, per in zip(heads, CHUNKS):
        at = slice(head * HDIM, (head + per) * HDIM)
        own = jnp.stack([keys[:, at], values[:, at]])
        own = lax.optimization_barrier(own)
        columns.append([own, send(own, onward(1))])
        columns[-1][1], delta = lax.optimization_barrier((columns[-1][1], delta))
    for column in columns:
        for hop in range(2, hops + 1):
            column.append(send(column[-1], onward(hop)))
    arrived = []
    for chunk, column in enumerate(columns):
        edge = jnp.where(even, column[0], column[hops])
        moved = [(array, None) for array in column]
        if chunk == 0:
            crossed = [send(array, to_odd(1) + to_even(1)) for array in column[1:hops]]
            crossed.append(send(after(edge, *crossed), to_odd(0) + to_even(hops)))
            moved += [(array, None) for array in crossed]
        else:
            joint = jnp.stack(column[1:hops] + [edge])
            crossed = send(joint, to_odd(0) + to_even(1))
            moved += [(crossed, hop) for hop in range(hops)]
            arrived[0][-1] = (after(arrived[0][-1][0], joint), None)
        arrived.append(moved)

    wide, half = jnp.float32, jnp.bfloat16
    grads_q, sums, outputs_of = [], [], []
    for chunk, (head, per) in enumerate(zip(heads, CHUNKS)):
        joined = chunk < len(CHUNKS) - 1
        grad_q, *parts = attend(
            doc_lengths, queries, grad_out, lse, delta, arrived[chunk], head, per, hops, joined
        )
        grads_q.append(grad_q)
        outputs_of.append((parts[: hops + 1], parts[hops + 1 :], joined))
    swapped = []
    for column, crossed, joined in outputs_of:
        if joined:
            crossed = send(crossed[0], to_odd(1) + to_even(0))
            crossed = after(crossed, outputs_of[-1][1][-1])
            edge = crossed[hops - 1]
        else:
            edge = send(crossed[-1], to_odd(hops) + to_even(0))
            crossed = [
                send(after(crossed[hop - 1], swapped[0][2]), to_odd(hop) + to_even(hop))
                for hop in range(1, hops)
            ]
        edge = edge.astype(wide)
        total = column[hops].astype(wide) + jnp.where(odd, edge, 0.0)
        swapped.append((crossed, edge, total.astype(half)))
    before = []
    for (column, _, joined), (crossed, edge, total) in zip(outputs_of, swapped):
        for hop in range(hops - 1, -1, -1):
            if joined:
                if hop == 0 and hops > 1:
                    total = after(total, *swapped[-1][0])
                before.append(total)
            elif hop == 0:
                total = after(total, *before)
            far = send(total, back(hop + 1)).astype(wide)
            if hop:
                total = column[hop].astype(wide) + crossed[hop - 1].astype(wide) + far
                total = total.astype(half)
        if joined:
            total = column[0].astype(wide) + jnp.where(even, edge, 0.0) + far
            sums.append([total.astype(half)])
        else:
            sums.append([column[0], edge.astype(half), far.astype(half)])
    grads_q[-1] = after(grads_q[-1], edge)
    grad_q = jnp.concatenate(grads_q, axis=1)
    grad_keys, grad_values = finish(sums, keys.shape)
    return (grad_q, grad_keys, grad_values)


def solution(mesh):
    rows = P(("packs", "seq"), None)
    return jax.shard_map(
        shards,
        mesh=mesh,
        in_specs=(rows, rows, rows, rows, rows, rows, P("packs")),
        out_specs=(rows, rows, rows),
        check_vma=False,
    )
```

```python
import functools

import jax
import jax.numpy as jnp
from jax import lax
from jax.experimental import pallas as pl
from jax.experimental.pallas import tpu as pltpu
from jax.sharding import PartitionSpec as P

HEADS = 64
KVH = 8
HDIM = 128
GROUP = HEADS // KVH
CHUNKS = (4, 4)
STEP = 2
LOG2E = 1.4426950408889634
VMEM = 20 * 1024 * 1024


def contract_last(first, second):
    return lax.dot_general(
        first, second, (((1,), (1,)), ((), ())), preferred_element_type=jnp.float32
    )


def contract_first(first, second):
    return lax.dot_general(
        first, second, (((0,), (0,)), ((), ())), preferred_element_type=jnp.float32
    )


def head_rows(block):
    return jnp.concatenate(
        [block[:, h * HDIM : (h + 1) * HDIM] for h in range(GROUP)], axis=0
    )


def delta_kernel(out_ref, gout_ref, q_ref, delta_ref):
    rows = out_ref.shape[0]
    wide = GROUP * HDIM
    first = lax.broadcasted_iota(jnp.int32, (wide, HDIM), 1) * HDIM
    row = lax.broadcasted_iota(jnp.int32, (wide, HDIM), 0)
    ones = jnp.where((row >= first) & (row < first + HDIM), 1.0, 0.0).astype(jnp.bfloat16)
    for group in range(out_ref.shape[1] // wide):
        at = slice(group * wide, (group + 1) * wide)
        product = out_ref[:, at].astype(jnp.float32) * gout_ref[:, at].astype(jnp.float32)
        high = product.astype(jnp.bfloat16)
        low = (product - high.astype(jnp.float32)).astype(jnp.bfloat16)
        total = jnp.dot(high, ones, preferred_element_type=jnp.float32)
        total += jnp.dot(low, ones, preferred_element_type=jnp.float32)
        delta_ref[group * GROUP : (group + 1) * GROUP, :] = total.T[:GROUP]


def delta_rows(outputs, grad_out, queries):
    rows = outputs.shape[0]
    local = pl.BlockSpec(memory_space=pltpu.VMEM)
    return pl.pallas_call(
        delta_kernel,
        in_specs=[local] * 3,
        out_specs=local,
        out_shape=jax.ShapeDtypeStruct((HEADS, rows), jnp.float32),
        compiler_params=pltpu.CompilerParams(vmem_limit_bytes=VMEM),
        cost_estimate=pl.CostEstimate(
            flops=4 * rows * HEADS * HDIM * HDIM,
            bytes_accessed=6 * rows * HEADS * HDIM,
            transcendentals=0,
        ),
        name="delta",
    )(outputs, grad_out, queries)


def slot_shards(me, hops):
    side = lax.rem(me, 2)
    found = [me - 2 * hop for hop in range(hops + 1)]
    found += [me - 2 * hop + 1 - 2 * side for hop in range(1, hops)]
    found.append(jnp.where(side == 1, me - 1, me - 2 * hops + 1))
    return found


def attend_kernel(hops, joined, first, places, docs, q_ref, gout_ref, lse_ref, delta_ref, *refs):
    slots = 2 * hops + 1
    moved, refs = refs[:slots], refs[slots:]
    gq_ref, refs = refs[0], refs[1:]
    if joined:
        parts = refs[: hops + 1] + tuple(refs[hops + 1].at[hop] for hop in range(hops))
    else:
        parts = refs[:slots]
    k_all, v_all, bias, prob, score = refs[-5:]
    rows = q_ref.shape[0]
    heads = moved[0].shape[-1] // HDIM
    scale = 1.0 / HDIM**0.5
    me = lax.axis_index("seq")

    token = lax.broadcasted_iota(jnp.int32, (1, rows), 1) + me * rows
    begin = jnp.zeros((1, rows), jnp.int32)
    bound = jnp.int32(0)
    for doc in range(docs.shape[0]):
        bound = bound + docs[doc]
        begin = jnp.where(token >= bound, bound, begin)
    row = lax.broadcasted_iota(jnp.int32, (rows, rows), 0)
    for slot, shard in enumerate(slot_shards(me, hops)):
        key = row + shard * rows
        visible = (key <= token) & (key >= begin)
        bias[slot * rows : (slot + 1) * rows, :] = jnp.where(visible, 0.0, -1e30)

    def one_head(index, k_all, v_all, prob, score):
        column = pl.ds(pl.multiple_of(index * HDIM, HDIM), HDIM)
        wide = pl.ds(pl.multiple_of((first + index) * GROUP * HDIM, GROUP * HDIM), GROUP * HDIM)
        stat = pl.ds(pl.multiple_of((first + index) * GROUP, GROUP), GROUP)
        for slot in range(slots):
            here = slice(slot * rows, (slot + 1) * rows)
            pair = moved[slot] if places[slot] is None else moved[slot].at[places[slot]]
            k_all[here, :] = pair[0, :, column]
            v_all[here, :] = pair[1, :, column]
        queries = head_rows(q_ref[:, wide])
        gout = head_rows(gout_ref[:, wide])
        lses = lse_ref[stat, :]
        deltas = delta_ref[stat, :]
        keys = k_all[...]
        values = v_all[...]
        hidden = bias[...]
        hidden = jnp.concatenate([hidden, hidden], axis=1)
        for two in range(GROUP // 2):
            at = slice(2 * two * rows, (2 * two + 2) * rows)
            lse = jnp.concatenate([lses[2 * two : 2 * two + 1], lses[2 * two + 1 : 2 * two + 2]], axis=1)
            delta = jnp.concatenate(
                [deltas[2 * two : 2 * two + 1], deltas[2 * two + 1 : 2 * two + 2]], axis=1
            )
            raw = contract_last(keys, queries[at])
            attn = jnp.exp2(raw * (scale * LOG2E) - lse * LOG2E + hidden)
            grad = contract_last(values, gout[at])
            prob[:, at] = attn.astype(jnp.bfloat16)
            score[:, at] = (attn * (grad - delta)).astype(jnp.bfloat16)
        scores = score[...]
        grad_k = jnp.dot(scores, queries, preferred_element_type=jnp.float32) * scale
        grad_v = jnp.dot(prob[...], gout, preferred_element_type=jnp.float32)
        for slot in range(slots):
            here = slice(slot * rows, (slot + 1) * rows)
            part = parts[slot]
            part[0, :, column] = grad_k[here].astype(part.dtype)
            part[1, :, column] = grad_v[here].astype(part.dtype)
        grad_q = (contract_first(keys, scores) * scale).astype(jnp.bfloat16)
        mine = pl.ds(pl.multiple_of(index * GROUP * HDIM, GROUP * HDIM), GROUP * HDIM)
        gq_ref[:, mine] = jnp.concatenate(
            [grad_q[:, h * rows : (h + 1) * rows].T for h in range(GROUP)], axis=1
        )

    @pl.loop(0, heads // STEP)
    def _(step):
        for sub in range(STEP):
            one_head(step * STEP + sub, k_all.at[sub], v_all.at[sub], prob.at[sub], score.at[sub])


def attend(docs, queries, grad_out, lse, delta, moved, head, per, hops, joined):
    rows = queries.shape[0]
    slots = 2 * hops + 1
    local = pl.BlockSpec(memory_space=pltpu.VMEM)
    operands = [docs, queries, grad_out, lse, delta] + [array for array, index in moved]
    in_specs = [pl.BlockSpec(memory_space=pltpu.SMEM)] + [local] * (len(operands) - 1)
    out_shape = [jax.ShapeDtypeStruct((rows, per * GROUP * HDIM), jnp.bfloat16)]
    out_shape += [jax.ShapeDtypeStruct((2, rows, per * HDIM), jnp.bfloat16)] * (hops + 1)
    if joined:
        out_shape += [jax.ShapeDtypeStruct((hops, 2, rows, per * HDIM), jnp.bfloat16)]
    else:
        out_shape += [jax.ShapeDtypeStruct((2, rows, per * HDIM), jnp.bfloat16)] * hops
    pairs = slots * rows * rows * GROUP * per
    places = [index for array, index in moved]
    return pl.pallas_call(
        functools.partial(attend_kernel, hops, joined, head, places),
        in_specs=in_specs,
        out_specs=[local] * len(out_shape),
        scratch_shapes=[
            pltpu.VMEM((STEP, slots * rows, HDIM), jnp.bfloat16),
            pltpu.VMEM((STEP, slots * rows, HDIM), jnp.bfloat16),
            pltpu.VMEM((slots * rows, rows), jnp.float32),
            pltpu.VMEM((STEP, slots * rows, GROUP * rows), jnp.bfloat16),
            pltpu.VMEM((STEP, slots * rows, GROUP * rows), jnp.bfloat16),
        ],
        out_shape=out_shape,
        compiler_params=pltpu.CompilerParams(vmem_limit_bytes=VMEM),
        cost_estimate=pl.CostEstimate(
            flops=40 * pairs * HDIM,
            bytes_accessed=per * rows * HDIM * 2 * (3 * GROUP + 6 * slots),
            transcendentals=pairs,
        ),
        name="attend",
    )(*operands)


def finish_kernel(chunks, *refs):
    key_ref, value_ref = refs[-2:]
    refs = refs[:-2]
    keep = jnp.where(lax.rem(lax.axis_index("seq"), 2) == 0, 1.0, 0.0)
    for start, done in chunks:
        if done:
            total, refs = refs[0][...], refs[1:]
        else:
            own, edge, far = (ref[...].astype(jnp.float32) for ref in refs[:3])
            total, refs = (own + edge * keep + far).astype(jnp.bfloat16), refs[3:]
        key_ref[:, start : start + total.shape[2]] = total[0]
        value_ref[:, start : start + total.shape[2]] = total[1]


def finish(sums, shape):
    operands, chunks, start = [], [], 0
    for part in sums:
        chunks.append((start, len(part) == 1))
        start += part[0].shape[2]
        operands += part
    local = pl.BlockSpec(memory_space=pltpu.VMEM)
    return pl.pallas_call(
        functools.partial(finish_kernel, chunks),
        in_specs=[local] * len(operands),
        out_specs=[local] * 2,
        out_shape=[jax.ShapeDtypeStruct(shape, jnp.bfloat16)] * 2,
        compiler_params=pltpu.CompilerParams(vmem_limit_bytes=VMEM),
        cost_estimate=pl.CostEstimate(
            flops=8 * shape[0] * shape[1], bytes_accessed=16 * shape[0] * shape[1], transcendentals=0
        ),
        name="finish",
    )(*operands)


def shards(queries, keys, values, outputs, grad_out, lse_saved, doc_lengths):
    seq = lax.axis_size("seq")
    me = lax.axis_index("seq").astype(jnp.int32)
    side = lax.rem(me, 2)
    keys, values, even, odd = lax.optimization_barrier((keys, values, side == 0, side == 1))
    hops = seq // 4
    def onward(hop):
        return [(s, s + 2) for s in range(2 * hop - 2, seq - 2)]

    def back(hop):
        return [(s, s - 2) for s in range(2 * hop, seq)]

    def to_odd(hop):
        return [(s, s + 1) for s in range(2 * hop, seq, 2)]

    def to_even(hop):
        return [(s + 1, s) for s in range(2 * hop, seq, 2)]

    def send(array, pairs):
        return lax.ppermute(array, "seq", pairs)

    def after(array, *others):
        return lax.optimization_barrier((array,) + others)[0]

    delta = delta_rows(outputs, grad_out, queries)
    lse = lse_saved.T
    heads = [sum(CHUNKS[:chunk]) for chunk in range(len(CHUNKS))]
    columns = []
    for head, per in zip(heads, CHUNKS):
        at = slice(head * HDIM, (head + per) * HDIM)
        own = jnp.stack([keys[:, at], values[:, at]])
        own = lax.optimization_barrier(own)
        columns.append([own, send(own, onward(1))])
        columns[-1][1], delta = lax.optimization_barrier((columns[-1][1], delta))
    for column in columns:
        for hop in range(2, hops + 1):
            column.append(send(column[-1], onward(hop)))
    arrived = []
    for chunk, column in enumerate(columns):
        edge = jnp.where(even, column[0], column[hops])
        moved = [(array, None) for array in column]
        if chunk == 0:
            crossed = [send(array, to_odd(1) + to_even(1)) for array in column[1:hops]]
            crossed.append(send(after(edge, *crossed), to_odd(0) + to_even(hops)))
            moved += [(array, None) for array in crossed]
        else:
            joint = jnp.stack(column[1:hops] + [edge])
            crossed = send(joint, to_odd(0) + to_even(1))
            moved += [(crossed, hop) for hop in range(hops)]
            arrived[0][-1] = (after(arrived[0][-1][0], joint), None)
        arrived.append(moved)

    wide, half = jnp.float32, jnp.bfloat16
    grads_q, sums, outputs_of = [], [], []
    for chunk, (head, per) in enumerate(zip(heads, CHUNKS)):
        joined = chunk < len(CHUNKS) - 1
        grad_q, *parts = attend(
            doc_lengths, queries, grad_out, lse, delta, arrived[chunk], head, per, hops, joined
        )
        grads_q.append(grad_q)
        outputs_of.append((parts[: hops + 1], parts[hops + 1 :], joined))
    swapped = []
    for column, crossed, joined in outputs_of:
        if joined:
            crossed = send(crossed[0], to_odd(1) + to_even(0))
            crossed = after(crossed, outputs_of[-1][1][-1])
            edge = crossed[hops - 1]
        else:
            edge = send(crossed[-1], to_odd(hops) + to_even(0))
            crossed = [
                send(after(crossed[hop - 1], swapped[0][2]), to_odd(hop) + to_even(hop))
                for hop in range(1, hops)
            ]
        edge = edge.astype(wide)
        total = column[hops].astype(wide) + jnp.where(odd, edge, 0.0)
        swapped.append((crossed, edge, total.astype(half)))
    before = []
    for (column, _, joined), (crossed, edge, total) in zip(outputs_of, swapped):
        for hop in range(hops - 1, -1, -1):
            if joined:
                if hop == 0 and hops > 1:
                    total = after(total, *swapped[-1][0])
                before.append(total)
            elif hop == 0:
                total = after(total, *before)
            far = send(total, back(hop + 1)).astype(wide)
            if hop:
                total = column[hop].astype(wide) + crossed[hop - 1].astype(wide) + far
                total = total.astype(half)
        if joined:
            total = column[0].astype(wide) + jnp.where(even, edge, 0.0) + far
            sums.append([total.astype(half)])
        else:
            sums.append([column[0], edge.astype(half), far.astype(half)])
    grads_q[-1] = after(grads_q[-1], edge)
    grad_q = jnp.concatenate(grads_q, axis=1)
    grad_keys, grad_values = finish(sums, keys.shape)
    return (grad_q, grad_keys, grad_values)


def solution(mesh):
    rows = P(("packs", "seq"), None)
    return jax.shard_map(
        shards,
        mesh=mesh,
        in_specs=(rows, rows, rows, rows, rows, rows, P("packs")),
        out_specs=(rows, rows, rows),
        check_vma=False,
    )
```

```python
import functools

import jax
import jax.numpy as jnp
from jax import lax
from jax.experimental import pallas as pl
from jax.experimental.pallas import tpu as pltpu
from jax.sharding import PartitionSpec as P

HEADS = 64
KVH = 8
HDIM = 128
GROUP = HEADS // KVH
CHUNKS = (4, 4)
STEP = 2
LOG2E = 1.4426950408889634
VMEM = 20 * 1024 * 1024


def contract_last(first, second):
    return lax.dot_general(
        first, second, (((1,), (1,)), ((), ())), preferred_element_type=jnp.float32
    )


def contract_first(first, second):
    return lax.dot_general(
        first, second, (((0,), (0,)), ((), ())), preferred_element_type=jnp.float32
    )


def head_rows(block):
    return jnp.concatenate(
        [block[:, h * HDIM : (h + 1) * HDIM] for h in range(GROUP)], axis=0
    )


def delta_kernel(out_ref, gout_ref, q_ref, delta_ref):
    rows = out_ref.shape[0]
    wide = GROUP * HDIM
    first = lax.broadcasted_iota(jnp.int32, (wide, HDIM), 1) * HDIM
    row = lax.broadcasted_iota(jnp.int32, (wide, HDIM), 0)
    ones = jnp.where((row >= first) & (row < first + HDIM), 1.0, 0.0).astype(jnp.bfloat16)
    for group in range(out_ref.shape[1] // wide):
        at = slice(group * wide, (group + 1) * wide)
        product = out_ref[:, at].astype(jnp.float32) * gout_ref[:, at].astype(jnp.float32)
        high = product.astype(jnp.bfloat16)
        low = (product - high.astype(jnp.float32)).astype(jnp.bfloat16)
        total = jnp.dot(high, ones, preferred_element_type=jnp.float32)
        total += jnp.dot(low, ones, preferred_element_type=jnp.float32)
        delta_ref[group * GROUP : (group + 1) * GROUP, :] = total.T[:GROUP]


def delta_rows(outputs, grad_out, queries):
    rows = outputs.shape[0]
    local = pl.BlockSpec(memory_space=pltpu.VMEM)
    return pl.pallas_call(
        delta_kernel,
        in_specs=[local] * 3,
        out_specs=local,
        out_shape=jax.ShapeDtypeStruct((HEADS, rows), jnp.float32),
        compiler_params=pltpu.CompilerParams(vmem_limit_bytes=VMEM),
        cost_estimate=pl.CostEstimate(
            flops=4 * rows * HEADS * HDIM * HDIM,
            bytes_accessed=6 * rows * HEADS * HDIM,
            transcendentals=0,
        ),
        name="delta",
    )(outputs, grad_out, queries)


def slot_shards(me, hops):
    side = lax.rem(me, 2)
    found = [me - 2 * hop for hop in range(hops + 1)]
    found += [me - 2 * hop + 1 - 2 * side for hop in range(1, hops)]
    found.append(jnp.where(side == 1, me - 1, me - 2 * hops + 1))
    return found


def attend_kernel(hops, joined, first, places, docs, q_ref, gout_ref, lse_ref, delta_ref, *refs):
    slots = 2 * hops + 1
    moved, refs = refs[:slots], refs[slots:]
    gq_ref, refs = refs[0], refs[1:]
    if joined:
        parts = refs[: hops + 1] + tuple(refs[hops + 1].at[hop] for hop in range(hops))
    else:
        parts = refs[:slots]
    k_all, v_all, bias, prob, score = refs[-5:]
    rows = q_ref.shape[0]
    heads = moved[0].shape[-1] // HDIM
    scale = 1.0 / HDIM**0.5
    me = lax.axis_index("seq")

    token = lax.broadcasted_iota(jnp.int32, (1, rows), 1) + me * rows
    begin = jnp.zeros((1, rows), jnp.int32)
    bound = jnp.int32(0)
    for doc in range(docs.shape[0]):
        bound = bound + docs[doc]
        begin = jnp.where(token >= bound, bound, begin)
    row = lax.broadcasted_iota(jnp.int32, (rows, rows), 0)
    for slot, shard in enumerate(slot_shards(me, hops)):
        key = row + shard * rows
        visible = (key <= token) & (key >= begin)
        bias[slot * rows : (slot + 1) * rows, :] = jnp.where(visible, 0.0, -1e30)

    def one_head(index, k_all, v_all, prob, score):
        column = pl.ds(pl.multiple_of(index * HDIM, HDIM), HDIM)
        wide = pl.ds(pl.multiple_of((first + index) * GROUP * HDIM, GROUP * HDIM), GROUP * HDIM)
        stat = pl.ds(pl.multiple_of((first + index) * GROUP, GROUP), GROUP)
        for slot in range(slots):
            here = slice(slot * rows, (slot + 1) * rows)
            pair = moved[slot] if places[slot] is None else moved[slot].at[places[slot]]
            k_all[here, :] = pair[0, :, column]
            v_all[here, :] = pair[1, :, column]
        queries = head_rows(q_ref[:, wide])
        gout = head_rows(gout_ref[:, wide])
        lses = lse_ref[stat, :]
        deltas = delta_ref[stat, :]
        keys = k_all[...]
        values = v_all[...]
        hidden = bias[...]
        hidden = jnp.concatenate([hidden, hidden], axis=1)
        for two in range(GROUP // 2):
            at = slice(2 * two * rows, (2 * two + 2) * rows)
            lse = jnp.concatenate([lses[2 * two : 2 * two + 1], lses[2 * two + 1 : 2 * two + 2]], axis=1)
            delta = jnp.concatenate(
                [deltas[2 * two : 2 * two + 1], deltas[2 * two + 1 : 2 * two + 2]], axis=1
            )
            raw = contract_last(keys, queries[at])
            attn = jnp.exp2(raw * (scale * LOG2E) - lse * LOG2E + hidden)
            grad = contract_last(values, gout[at])
            prob[:, at] = attn.astype(jnp.bfloat16)
            score[:, at] = (attn * (grad - delta)).astype(jnp.bfloat16)
        scores = score[...]
        grad_k = jnp.dot(scores, queries, preferred_element_type=jnp.float32) * scale
        grad_v = jnp.dot(prob[...], gout, preferred_element_type=jnp.float32)
        for slot in range(slots):
            here = slice(slot * rows, (slot + 1) * rows)
            part = parts[slot]
            part[0, :, column] = grad_k[here].astype(part.dtype)
            part[1, :, column] = grad_v[here].astype(part.dtype)
        grad_q = (contract_first(keys, scores) * scale).astype(jnp.bfloat16)
        mine = pl.ds(pl.multiple_of(index * GROUP * HDIM, GROUP * HDIM), GROUP * HDIM)
        gq_ref[:, mine] = jnp.concatenate(
            [grad_q[:, h * rows : (h + 1) * rows].T for h in range(GROUP)], axis=1
        )

    @pl.loop(0, heads // STEP)
    def _(step):
        for sub in range(STEP):
            one_head(step * STEP + sub, k_all.at[sub], v_all.at[sub], prob.at[sub], score.at[sub])


def attend(docs, queries, grad_out, lse, delta, moved, head, per, hops, joined):
    rows = queries.shape[0]
    slots = 2 * hops + 1
    local = pl.BlockSpec(memory_space=pltpu.VMEM)
    operands = [docs, queries, grad_out, lse, delta] + [array for array, index in moved]
    in_specs = [pl.BlockSpec(memory_space=pltpu.SMEM)] + [local] * (len(operands) - 1)
    out_shape = [jax.ShapeDtypeStruct((rows, per * GROUP * HDIM), jnp.bfloat16)]
    out_shape += [jax.ShapeDtypeStruct((2, rows, per * HDIM), jnp.bfloat16)] * (hops + 1)
    if joined:
        out_shape += [jax.ShapeDtypeStruct((hops, 2, rows, per * HDIM), jnp.bfloat16)]
    else:
        out_shape += [jax.ShapeDtypeStruct((2, rows, per * HDIM), jnp.bfloat16)] * hops
    pairs = slots * rows * rows * GROUP * per
    places = [index for array, index in moved]
    return pl.pallas_call(
        functools.partial(attend_kernel, hops, joined, head, places),
        in_specs=in_specs,
        out_specs=[local] * len(out_shape),
        scratch_shapes=[
            pltpu.VMEM((STEP, slots * rows, HDIM), jnp.bfloat16),
            pltpu.VMEM((STEP, slots * rows, HDIM), jnp.bfloat16),
            pltpu.VMEM((slots * rows, rows), jnp.float32),
            pltpu.VMEM((STEP, slots * rows, GROUP * rows), jnp.bfloat16),
            pltpu.VMEM((STEP, slots * rows, GROUP * rows), jnp.bfloat16),
        ],
        out_shape=out_shape,
        compiler_params=pltpu.CompilerParams(vmem_limit_bytes=VMEM),
        cost_estimate=pl.CostEstimate(
            flops=40 * pairs * HDIM,
            bytes_accessed=per * rows * HDIM * 2 * (3 * GROUP + 6 * slots),
            transcendentals=pairs,
        ),
        name="attend",
    )(*operands)


def finish_kernel(chunks, *refs):
    key_ref, value_ref = refs[-2:]
    refs = refs[:-2]
    keep = jnp.where(lax.rem(lax.axis_index("seq"), 2) == 0, 1.0, 0.0)
    for start, done in chunks:
        if done:
            total, refs = refs[0][...], refs[1:]
        else:
            own, edge, far = (ref[...].astype(jnp.float32) for ref in refs[:3])
            total, refs = (own + edge * keep + far).astype(jnp.bfloat16), refs[3:]
        key_ref[:, start : start + total.shape[2]] = total[0]
        value_ref[:, start : start + total.shape[2]] = total[1]


def finish(sums, shape):
    operands, chunks, start = [], [], 0
    for part in sums:
        chunks.append((start, len(part) == 1))
        start += part[0].shape[2]
        operands += part
    local = pl.BlockSpec(memory_space=pltpu.VMEM)
    return pl.pallas_call(
        functools.partial(finish_kernel, chunks),
        in_specs=[local] * len(operands),
        out_specs=[local] * 2,
        out_shape=[jax.ShapeDtypeStruct(shape, jnp.bfloat16)] * 2,
        compiler_params=pltpu.CompilerParams(vmem_limit_bytes=VMEM),
        cost_estimate=pl.CostEstimate(
            flops=8 * shape[0] * shape[1], bytes_accessed=16 * shape[0] * shape[1], transcendentals=0
        ),
        name="finish",
    )(*operands)


def shards(queries, keys, values, outputs, grad_out, lse_saved, doc_lengths):
    seq = lax.axis_size("seq")
    me = lax.axis_index("seq").astype(jnp.int32)
    side = lax.rem(me, 2)
    keys, values, even, odd = lax.optimization_barrier((keys, values, side == 0, side == 1))
    hops = seq // 4
    def onward(hop):
        return [(s, s + 2) for s in range(2 * hop - 2, seq - 2)]

    def back(hop):
        return [(s, s - 2) for s in range(2 * hop, seq)]

    def to_odd(hop):
        return [(s, s + 1) for s in range(2 * hop, seq, 2)]

    def to_even(hop):
        return [(s + 1, s) for s in range(2 * hop, seq, 2)]

    def send(array, pairs):
        return lax.ppermute(array, "seq", pairs)

    def after(array, *others):
        return lax.optimization_barrier((array,) + others)[0]

    delta = delta_rows(outputs, grad_out, queries)
    lse = lse_saved.T
    heads = [sum(CHUNKS[:chunk]) for chunk in range(len(CHUNKS))]
    columns = []
    for head, per in zip(heads, CHUNKS):
        at = slice(head * HDIM, (head + per) * HDIM)
        own = jnp.stack([keys[:, at], values[:, at]])
        own = after(own, delta) if columns else lax.optimization_barrier(own)
        columns.append([own, send(own, onward(1))])
    columns[0][1] = after(columns[0][1], delta)
    for column in columns:
        for hop in range(2, hops + 1):
            column.append(send(column[-1], onward(hop)))
    arrived = []
    for chunk, column in enumerate(columns):
        edge = jnp.where(even, column[0], column[hops])
        moved = [(array, None) for array in column]
        if chunk == 0:
            crossed = [send(array, to_odd(1) + to_even(1)) for array in column[1:hops]]
            crossed.append(send(after(edge, *crossed), to_odd(0) + to_even(hops)))
            moved += [(array, None) for array in crossed]
        else:
            joint = jnp.stack(column[1:hops] + [edge])
            crossed = send(joint, to_odd(0) + to_even(1))
            moved += [(crossed, hop) for hop in range(hops)]
            arrived[0][-1] = (after(arrived[0][-1][0], joint), None)
        arrived.append(moved)

    wide, half = jnp.float32, jnp.bfloat16
    grads_q, sums, outputs_of = [], [], []
    for chunk, (head, per) in enumerate(zip(heads, CHUNKS)):
        joined = chunk < len(CHUNKS) - 1
        grad_q, *parts = attend(
            doc_lengths, queries, grad_out, lse, delta, arrived[chunk], head, per, hops, joined
        )
        grads_q.append(grad_q)
        outputs_of.append((parts[: hops + 1], parts[hops + 1 :], joined))
    swapped = []
    for column, crossed, joined in outputs_of:
        if joined:
            crossed = send(crossed[0], to_odd(1) + to_even(0))
            crossed = after(crossed, outputs_of[-1][1][-1])
            edge = crossed[hops - 1]
        else:
            edge = send(crossed[-1], to_odd(hops) + to_even(0))
            crossed = [
                send(after(crossed[hop - 1], swapped[0][2]), to_odd(hop) + to_even(hop))
                for hop in range(1, hops)
            ]
        edge = edge.astype(wide)
        total = column[hops].astype(wide) + jnp.where(odd, edge, 0.0)
        swapped.append((crossed, edge, total.astype(half)))
    before = []
    for (column, _, joined), (crossed, edge, total) in zip(outputs_of, swapped):
        for hop in range(hops - 1, -1, -1):
            if joined:
                if hop == 0 and hops > 1:
                    total = after(total, *swapped[-1][0])
                before.append(total)
            elif hop == 0:
                total = after(total, *before)
            far = send(total, back(hop + 1)).astype(wide)
            if hop:
                total = column[hop].astype(wide) + crossed[hop - 1].astype(wide) + far
                total = total.astype(half)
        if joined:
            total = column[0].astype(wide) + jnp.where(even, edge, 0.0) + far
            sums.append([total.astype(half)])
        else:
            sums.append([column[0], edge.astype(half), far.astype(half)])
    grads_q[-1] = after(grads_q[-1], edge)
    grad_q = jnp.concatenate(grads_q, axis=1)
    grad_keys, grad_values = finish(sums, keys.shape)
    return (grad_q, grad_keys, grad_values)


def solution(mesh):
    rows = P(("packs", "seq"), None)
    return jax.shard_map(
        shards,
        mesh=mesh,
        in_specs=(rows, rows, rows, rows, rows, rows, P("packs")),
        out_specs=(rows, rows, rows),
        check_vma=False,
    )
```

```python
import functools

import jax
import jax.numpy as jnp
from jax import lax
from jax.experimental import pallas as pl
from jax.experimental.pallas import tpu as pltpu
from jax.sharding import PartitionSpec as P

HEADS = 64
KVH = 8
HDIM = 128
GROUP = HEADS // KVH
CHUNKS = (4, 4)
STEP = 4
LOG2E = 1.4426950408889634
VMEM = 24 * 1024 * 1024


def contract_last(first, second):
    return lax.dot_general(
        first, second, (((1,), (1,)), ((), ())), preferred_element_type=jnp.float32
    )


def contract_first(first, second):
    return lax.dot_general(
        first, second, (((0,), (0,)), ((), ())), preferred_element_type=jnp.float32
    )


def head_rows(block):
    return jnp.concatenate(
        [block[:, h * HDIM : (h + 1) * HDIM] for h in range(GROUP)], axis=0
    )


def delta_kernel(out_ref, gout_ref, q_ref, delta_ref):
    rows = out_ref.shape[0]
    wide = GROUP * HDIM
    first = lax.broadcasted_iota(jnp.int32, (wide, HDIM), 1) * HDIM
    row = lax.broadcasted_iota(jnp.int32, (wide, HDIM), 0)
    ones = jnp.where((row >= first) & (row < first + HDIM), 1.0, 0.0).astype(jnp.bfloat16)
    for group in range(out_ref.shape[1] // wide):
        at = slice(group * wide, (group + 1) * wide)
        product = out_ref[:, at].astype(jnp.float32) * gout_ref[:, at].astype(jnp.float32)
        high = product.astype(jnp.bfloat16)
        low = (product - high.astype(jnp.float32)).astype(jnp.bfloat16)
        total = jnp.dot(high, ones, preferred_element_type=jnp.float32)
        total += jnp.dot(low, ones, preferred_element_type=jnp.float32)
        delta_ref[group * GROUP : (group + 1) * GROUP, :] = total.T[:GROUP]


def delta_rows(outputs, grad_out, queries):
    rows = outputs.shape[0]
    local = pl.BlockSpec(memory_space=pltpu.VMEM)
    return pl.pallas_call(
        delta_kernel,
        in_specs=[local] * 3,
        out_specs=local,
        out_shape=jax.ShapeDtypeStruct((HEADS, rows), jnp.float32),
        compiler_params=pltpu.CompilerParams(vmem_limit_bytes=VMEM),
        cost_estimate=pl.CostEstimate(
            flops=4 * rows * HEADS * HDIM * HDIM,
            bytes_accessed=6 * rows * HEADS * HDIM,
            transcendentals=0,
        ),
        name="delta",
    )(outputs, grad_out, queries)


def slot_shards(me, hops):
    side = lax.rem(me, 2)
    found = [me - 2 * hop for hop in range(hops + 1)]
    found += [me - 2 * hop + 1 - 2 * side for hop in range(1, hops)]
    found.append(jnp.where(side == 1, me - 1, me - 2 * hops + 1))
    return found


def attend_kernel(hops, joined, first, places, docs, q_ref, gout_ref, lse_ref, delta_ref, *refs):
    slots = 2 * hops + 1
    moved, refs = refs[:slots], refs[slots:]
    gq_ref, refs = refs[0], refs[1:]
    if joined:
        parts = refs[: hops + 1] + tuple(refs[hops + 1].at[hop] for hop in range(hops))
    else:
        parts = refs[:slots]
    k_all, v_all, bias, prob, score = refs[-5:]
    rows = q_ref.shape[0]
    heads = moved[0].shape[-1] // HDIM
    scale = 1.0 / HDIM**0.5
    me = lax.axis_index("seq")

    token = lax.broadcasted_iota(jnp.int32, (1, rows), 1) + me * rows
    begin = jnp.zeros((1, rows), jnp.int32)
    bound = jnp.int32(0)
    for doc in range(docs.shape[0]):
        bound = bound + docs[doc]
        begin = jnp.where(token >= bound, bound, begin)
    row = lax.broadcasted_iota(jnp.int32, (rows, rows), 0)
    for slot, shard in enumerate(slot_shards(me, hops)):
        key = row + shard * rows
        visible = (key <= token) & (key >= begin)
        bias[slot * rows : (slot + 1) * rows, :] = jnp.where(visible, 0.0, -1e30)

    def one_head(index, k_all, v_all, prob, score):
        column = pl.ds(pl.multiple_of(index * HDIM, HDIM), HDIM)
        wide = pl.ds(pl.multiple_of((first + index) * GROUP * HDIM, GROUP * HDIM), GROUP * HDIM)
        stat = pl.ds(pl.multiple_of((first + index) * GROUP, GROUP), GROUP)
        for slot in range(slots):
            here = slice(slot * rows, (slot + 1) * rows)
            pair = moved[slot] if places[slot] is None else moved[slot].at[places[slot]]
            k_all[here, :] = pair[0, :, column]
            v_all[here, :] = pair[1, :, column]
        queries = head_rows(q_ref[:, wide])
        gout = head_rows(gout_ref[:, wide])
        lses = lse_ref[stat, :]
        deltas = delta_ref[stat, :]
        keys = k_all[...]
        values = v_all[...]
        hidden = bias[...]
        hidden = jnp.concatenate([hidden, hidden], axis=1)
        for two in range(GROUP // 2):
            at = slice(2 * two * rows, (2 * two + 2) * rows)
            lse = jnp.concatenate([lses[2 * two : 2 * two + 1], lses[2 * two + 1 : 2 * two + 2]], axis=1)
            delta = jnp.concatenate(
                [deltas[2 * two : 2 * two + 1], deltas[2 * two + 1 : 2 * two + 2]], axis=1
            )
            raw = contract_last(keys, queries[at])
            attn = jnp.exp2(raw * (scale * LOG2E) - lse * LOG2E + hidden)
            grad = contract_last(values, gout[at])
            prob[:, at] = attn.astype(jnp.bfloat16)
            score[:, at] = (attn * (grad - delta)).astype(jnp.bfloat16)
        scores = score[...]
        grad_k = jnp.dot(scores, queries, preferred_element_type=jnp.float32) * scale
        grad_v = jnp.dot(prob[...], gout, preferred_element_type=jnp.float32)
        for slot in range(slots):
            here = slice(slot * rows, (slot + 1) * rows)
            part = parts[slot]
            part[0, :, column] = grad_k[here].astype(part.dtype)
            part[1, :, column] = grad_v[here].astype(part.dtype)
        grad_q = (contract_first(keys, scores) * scale).astype(jnp.bfloat16)
        mine = pl.ds(pl.multiple_of(index * GROUP * HDIM, GROUP * HDIM), GROUP * HDIM)
        gq_ref[:, mine] = jnp.concatenate(
            [grad_q[:, h * rows : (h + 1) * rows].T for h in range(GROUP)], axis=1
        )

    @pl.loop(0, heads // STEP)
    def _(step):
        for sub in range(STEP):
            one_head(step * STEP + sub, k_all.at[sub], v_all.at[sub], prob.at[sub], score.at[sub])


def attend(docs, queries, grad_out, lse, delta, moved, head, per, hops, joined):
    rows = queries.shape[0]
    slots = 2 * hops + 1
    local = pl.BlockSpec(memory_space=pltpu.VMEM)
    operands = [docs, queries, grad_out, lse, delta] + [array for array, index in moved]
    in_specs = [pl.BlockSpec(memory_space=pltpu.SMEM)] + [local] * (len(operands) - 1)
    out_shape = [jax.ShapeDtypeStruct((rows, per * GROUP * HDIM), jnp.bfloat16)]
    out_shape += [jax.ShapeDtypeStruct((2, rows, per * HDIM), jnp.bfloat16)] * (hops + 1)
    if joined:
        out_shape += [jax.ShapeDtypeStruct((hops, 2, rows, per * HDIM), jnp.bfloat16)]
    else:
        out_shape += [jax.ShapeDtypeStruct((2, rows, per * HDIM), jnp.bfloat16)] * hops
    pairs = slots * rows * rows * GROUP * per
    places = [index for array, index in moved]
    return pl.pallas_call(
        functools.partial(attend_kernel, hops, joined, head, places),
        in_specs=in_specs,
        out_specs=[local] * len(out_shape),
        scratch_shapes=[
            pltpu.VMEM((STEP, slots * rows, HDIM), jnp.bfloat16),
            pltpu.VMEM((STEP, slots * rows, HDIM), jnp.bfloat16),
            pltpu.VMEM((slots * rows, rows), jnp.float32),
            pltpu.VMEM((STEP, slots * rows, GROUP * rows), jnp.bfloat16),
            pltpu.VMEM((STEP, slots * rows, GROUP * rows), jnp.bfloat16),
        ],
        out_shape=out_shape,
        compiler_params=pltpu.CompilerParams(vmem_limit_bytes=VMEM),
        cost_estimate=pl.CostEstimate(
            flops=40 * pairs * HDIM,
            bytes_accessed=per * rows * HDIM * 2 * (3 * GROUP + 6 * slots),
            transcendentals=pairs,
        ),
        name="attend",
    )(*operands)


def finish_kernel(chunks, *refs):
    key_ref, value_ref = refs[-2:]
    refs = refs[:-2]
    keep = jnp.where(lax.rem(lax.axis_index("seq"), 2) == 0, 1.0, 0.0)
    for start, done in chunks:
        if done:
            total, refs = refs[0][...], refs[1:]
        else:
            own, edge, far = (ref[...].astype(jnp.float32) for ref in refs[:3])
            total, refs = (own + edge * keep + far).astype(jnp.bfloat16), refs[3:]
        key_ref[:, start : start + total.shape[2]] = total[0]
        value_ref[:, start : start + total.shape[2]] = total[1]


def finish(sums, shape):
    operands, chunks, start = [], [], 0
    for part in sums:
        chunks.append((start, len(part) == 1))
        start += part[0].shape[2]
        operands += part
    local = pl.BlockSpec(memory_space=pltpu.VMEM)
    return pl.pallas_call(
        functools.partial(finish_kernel, chunks),
        in_specs=[local] * len(operands),
        out_specs=[local] * 2,
        out_shape=[jax.ShapeDtypeStruct(shape, jnp.bfloat16)] * 2,
        compiler_params=pltpu.CompilerParams(vmem_limit_bytes=VMEM),
        cost_estimate=pl.CostEstimate(
            flops=8 * shape[0] * shape[1], bytes_accessed=16 * shape[0] * shape[1], transcendentals=0
        ),
        name="finish",
    )(*operands)


def shards(queries, keys, values, outputs, grad_out, lse_saved, doc_lengths):
    seq = lax.axis_size("seq")
    me = lax.axis_index("seq").astype(jnp.int32)
    side = lax.rem(me, 2)
    keys, values, even, odd = lax.optimization_barrier((keys, values, side == 0, side == 1))
    hops = seq // 4
    def onward(hop):
        return [(s, s + 2) for s in range(2 * hop - 2, seq - 2)]

    def back(hop):
        return [(s, s - 2) for s in range(2 * hop, seq)]

    def to_odd(hop):
        return [(s, s + 1) for s in range(2 * hop, seq, 2)]

    def to_even(hop):
        return [(s + 1, s) for s in range(2 * hop, seq, 2)]

    def send(array, pairs):
        return lax.ppermute(array, "seq", pairs)

    def after(array, *others):
        return lax.optimization_barrier((array,) + others)[0]

    delta = delta_rows(outputs, grad_out, queries)
    lse = lse_saved.T
    heads = [sum(CHUNKS[:chunk]) for chunk in range(len(CHUNKS))]
    columns = []
    for head, per in zip(heads, CHUNKS):
        at = slice(head * HDIM, (head + per) * HDIM)
        own = jnp.stack([keys[:, at], values[:, at]])
        own = lax.optimization_barrier(own)
        columns.append([own, send(own, onward(1))])
        columns[-1][1], delta = lax.optimization_barrier((columns[-1][1], delta))
    for column in columns:
        for hop in range(2, hops + 1):
            column.append(send(column[-1], onward(hop)))
    arrived = []
    for chunk, column in enumerate(columns):
        edge = jnp.where(even, column[0], column[hops])
        moved = [(array, None) for array in column]
        if chunk == 0:
            crossed = [send(array, to_odd(1) + to_even(1)) for array in column[1:hops]]
            crossed.append(send(after(edge, *crossed), to_odd(0) + to_even(hops)))
            moved += [(array, None) for array in crossed]
        else:
            joint = jnp.stack(column[1:hops] + [edge])
            crossed = send(joint, to_odd(0) + to_even(1))
            moved += [(crossed, hop) for hop in range(hops)]
            arrived[0][-1] = (after(arrived[0][-1][0], joint), None)
        arrived.append(moved)

    wide, half = jnp.float32, jnp.bfloat16
    grads_q, sums, outputs_of = [], [], []
    for chunk, (head, per) in enumerate(zip(heads, CHUNKS)):
        joined = chunk < len(CHUNKS) - 1
        grad_q, *parts = attend(
            doc_lengths, queries, grad_out, lse, delta, arrived[chunk], head, per, hops, joined
        )
        grads_q.append(grad_q)
        outputs_of.append((parts[: hops + 1], parts[hops + 1 :], joined))
    swapped = []
    for column, crossed, joined in outputs_of:
        if joined:
            crossed = send(crossed[0], to_odd(1) + to_even(0))
            crossed = after(crossed, outputs_of[-1][1][-1])
            edge = crossed[hops - 1]
        else:
            edge = send(crossed[-1], to_odd(hops) + to_even(0))
            crossed = [
                send(after(crossed[hop - 1], swapped[0][2]), to_odd(hop) + to_even(hop))
                for hop in range(1, hops)
            ]
        edge = edge.astype(wide)
        total = column[hops].astype(wide) + jnp.where(odd, edge, 0.0)
        swapped.append((crossed, edge, total.astype(half)))
    before = []
    for (column, _, joined), (crossed, edge, total) in zip(outputs_of, swapped):
        for hop in range(hops - 1, -1, -1):
            if joined:
                if hop == 0 and hops > 1:
                    total = after(total, *swapped[-1][0])
                before.append(total)
            elif hop == 0:
                total = after(total, *before)
            far = send(total, back(hop + 1)).astype(wide)
            if hop:
                total = column[hop].astype(wide) + crossed[hop - 1].astype(wide) + far
                total = total.astype(half)
        if joined:
            total = column[0].astype(wide) + jnp.where(even, edge, 0.0) + far
            sums.append([total.astype(half)])
        else:
            sums.append([column[0], edge.astype(half), far.astype(half)])
    grads_q[-1] = after(grads_q[-1], edge)
    grad_q = jnp.concatenate(grads_q, axis=1)
    grad_keys, grad_values = finish(sums, keys.shape)
    return (grad_q, grad_keys, grad_values)


def solution(mesh):
    rows = P(("packs", "seq"), None)
    return jax.shard_map(
        shards,
        mesh=mesh,
        in_specs=(rows, rows, rows, rows, rows, rows, P("packs")),
        out_specs=(rows, rows, rows),
        check_vma=False,
    )
```

```python
import functools

import jax
import jax.numpy as jnp
from jax import lax
from jax.experimental import pallas as pl
from jax.experimental.pallas import tpu as pltpu
from jax.sharding import PartitionSpec as P

HEADS = 64
KVH = 8
HDIM = 128
GROUP = HEADS // KVH
CHUNKS = (4, 4)
STEP = 2
LOG2E = 1.4426950408889634
VMEM = 20 * 1024 * 1024


def contract_last(first, second):
    return lax.dot_general(
        first, second, (((1,), (1,)), ((), ())), preferred_element_type=jnp.float32
    )


def contract_first(first, second):
    return lax.dot_general(
        first, second, (((0,), (0,)), ((), ())), preferred_element_type=jnp.float32
    )


def head_rows(block):
    return jnp.concatenate(
        [block[:, h * HDIM : (h + 1) * HDIM] for h in range(GROUP)], axis=0
    )


def delta_kernel(out_ref, gout_ref, delta_ref):
    rows = out_ref.shape[0]
    wide = GROUP * HDIM
    first = lax.broadcasted_iota(jnp.int32, (wide, HDIM), 1) * HDIM
    row = lax.broadcasted_iota(jnp.int32, (wide, HDIM), 0)
    ones = jnp.where((row >= first) & (row < first + HDIM), 1.0, 0.0).astype(jnp.bfloat16)
    for group in range(out_ref.shape[1] // wide):
        at = slice(group * wide, (group + 1) * wide)
        product = out_ref[:, at].astype(jnp.float32) * gout_ref[:, at].astype(jnp.float32)
        high = product.astype(jnp.bfloat16)
        low = (product - high.astype(jnp.float32)).astype(jnp.bfloat16)
        total = jnp.dot(high, ones, preferred_element_type=jnp.float32)
        total += jnp.dot(low, ones, preferred_element_type=jnp.float32)
        delta_ref[group * GROUP : (group + 1) * GROUP, :] = total.T[:GROUP]


def delta_rows(outputs, grad_out):
    rows = outputs.shape[0]
    local = pl.BlockSpec(memory_space=pltpu.VMEM)
    return pl.pallas_call(
        delta_kernel,
        in_specs=[local] * 2,
        out_specs=local,
        out_shape=jax.ShapeDtypeStruct((HEADS, rows), jnp.float32),
        compiler_params=pltpu.CompilerParams(vmem_limit_bytes=VMEM),
        cost_estimate=pl.CostEstimate(
            flops=4 * rows * HEADS * HDIM * HDIM,
            bytes_accessed=4 * rows * HEADS * HDIM,
            transcendentals=0,
        ),
        name="delta",
    )(outputs, grad_out)


def slot_shards(me, hops):
    side = lax.rem(me, 2)
    found = [me - 2 * hop for hop in range(hops + 1)]
    found += [me - 2 * hop + 1 - 2 * side for hop in range(1, hops)]
    found.append(jnp.where(side == 1, me - 1, me - 2 * hops + 1))
    return found


def attend_kernel(hops, joined, first, places, docs, q_ref, gout_ref, lse_ref, delta_ref, *refs):
    slots = 2 * hops + 1
    moved, refs = refs[:slots], refs[slots:]
    gq_ref, refs = refs[0], refs[1:]
    if joined:
        parts = refs[: hops + 1] + tuple(refs[hops + 1].at[hop] for hop in range(hops))
    else:
        parts = refs[:slots]
    k_all, v_all, bias, prob, score = refs[-5:]
    rows = q_ref.shape[0]
    heads = moved[0].shape[-1] // HDIM
    scale = 1.0 / HDIM**0.5
    me = lax.axis_index("seq")

    token = lax.broadcasted_iota(jnp.int32, (1, rows), 1) + me * rows
    begin = jnp.zeros((1, rows), jnp.int32)
    bound = jnp.int32(0)
    for doc in range(docs.shape[0]):
        bound = bound + docs[doc]
        begin = jnp.where(token >= bound, bound, begin)
    row = lax.broadcasted_iota(jnp.int32, (rows, rows), 0)
    for slot, shard in enumerate(slot_shards(me, hops)):
        key = row + shard * rows
        visible = (key <= token) & (key >= begin)
        bias[slot * rows : (slot + 1) * rows, :] = jnp.where(visible, 0.0, -1e30)

    def one_head(index, k_all, v_all, prob, score):
        column = pl.ds(pl.multiple_of(index * HDIM, HDIM), HDIM)
        wide = pl.ds(pl.multiple_of((first + index) * GROUP * HDIM, GROUP * HDIM), GROUP * HDIM)
        stat = pl.ds(pl.multiple_of((first + index) * GROUP, GROUP), GROUP)
        for slot in range(slots):
            here = slice(slot * rows, (slot + 1) * rows)
            pair = moved[slot] if places[slot] is None else moved[slot].at[places[slot]]
            k_all[here, :] = pair[0, :, column]
            v_all[here, :] = pair[1, :, column]
        queries = head_rows(q_ref[:, wide])
        gout = head_rows(gout_ref[:, wide])
        lses = lse_ref[stat, :]
        deltas = delta_ref[stat, :]
        keys = k_all[...]
        values = v_all[...]
        hidden = bias[...]
        hidden = jnp.concatenate([hidden, hidden], axis=1)
        for two in range(GROUP // 2):
            at = slice(2 * two * rows, (2 * two + 2) * rows)
            lse = jnp.concatenate([lses[2 * two : 2 * two + 1], lses[2 * two + 1 : 2 * two + 2]], axis=1)
            delta = jnp.concatenate(
                [deltas[2 * two : 2 * two + 1], deltas[2 * two + 1 : 2 * two + 2]], axis=1
            )
            raw = contract_last(keys, queries[at])
            attn = jnp.exp2(raw * (scale * LOG2E) - lse * LOG2E + hidden)
            grad = contract_last(values, gout[at])
            prob[:, at] = attn.astype(jnp.bfloat16)
            score[:, at] = (attn * (grad - delta)).astype(jnp.bfloat16)
        scores = score[...]
        grad_k = jnp.dot(scores, queries, preferred_element_type=jnp.float32) * scale
        grad_v = jnp.dot(prob[...], gout, preferred_element_type=jnp.float32)
        for slot in range(slots):
            here = slice(slot * rows, (slot + 1) * rows)
            part = parts[slot]
            part[0, :, column] = grad_k[here].astype(part.dtype)
            part[1, :, column] = grad_v[here].astype(part.dtype)
        grad_q = (contract_first(keys, scores) * scale).astype(jnp.bfloat16)
        mine = pl.ds(pl.multiple_of(index * GROUP * HDIM, GROUP * HDIM), GROUP * HDIM)
        gq_ref[:, mine] = jnp.concatenate(
            [grad_q[:, h * rows : (h + 1) * rows].T for h in range(GROUP)], axis=1
        )

    @pl.loop(0, heads // STEP)
    def _(step):
        for sub in range(STEP):
            one_head(step * STEP + sub, k_all.at[sub], v_all.at[sub], prob.at[sub], score.at[sub])


def attend(docs, queries, grad_out, lse, delta, moved, head, per, hops, joined):
    rows = queries.shape[0]
    slots = 2 * hops + 1
    local = pl.BlockSpec(memory_space=pltpu.VMEM)
    operands = [docs, queries, grad_out, lse, delta] + [array for array, index in moved]
    in_specs = [pl.BlockSpec(memory_space=pltpu.SMEM)] + [local] * (len(operands) - 1)
    out_shape = [jax.ShapeDtypeStruct((rows, per * GROUP * HDIM), jnp.bfloat16)]
    out_shape += [jax.ShapeDtypeStruct((2, rows, per * HDIM), jnp.bfloat16)] * (hops + 1)
    if joined:
        out_shape += [jax.ShapeDtypeStruct((hops, 2, rows, per * HDIM), jnp.bfloat16)]
    else:
        out_shape += [jax.ShapeDtypeStruct((2, rows, per * HDIM), jnp.bfloat16)] * hops
    pairs = slots * rows * rows * GROUP * per
    places = [index for array, index in moved]
    return pl.pallas_call(
        functools.partial(attend_kernel, hops, joined, head, places),
        in_specs=in_specs,
        out_specs=[local] * len(out_shape),
        scratch_shapes=[
            pltpu.VMEM((STEP, slots * rows, HDIM), jnp.bfloat16),
            pltpu.VMEM((STEP, slots * rows, HDIM), jnp.bfloat16),
            pltpu.VMEM((slots * rows, rows), jnp.float32),
            pltpu.VMEM((STEP, slots * rows, GROUP * rows), jnp.bfloat16),
            pltpu.VMEM((STEP, slots * rows, GROUP * rows), jnp.bfloat16),
        ],
        out_shape=out_shape,
        compiler_params=pltpu.CompilerParams(vmem_limit_bytes=VMEM),
        cost_estimate=pl.CostEstimate(
            flops=40 * pairs * HDIM,
            bytes_accessed=per * rows * HDIM * 2 * (3 * GROUP + 6 * slots),
            transcendentals=pairs,
        ),
        name="attend",
    )(*operands)


def finish_kernel(chunks, *refs):
    key_ref, value_ref = refs[-2:]
    refs = refs[:-2]
    keep = jnp.where(lax.rem(lax.axis_index("seq"), 2) == 0, 1.0, 0.0)
    for start, done in chunks:
        if done:
            total, refs = refs[0][...], refs[1:]
        else:
            own, edge, far = (ref[...].astype(jnp.float32) for ref in refs[:3])
            total, refs = (own + edge * keep + far).astype(jnp.bfloat16), refs[3:]
        key_ref[:, start : start + total.shape[2]] = total[0]
        value_ref[:, start : start + total.shape[2]] = total[1]


def finish(sums, shape):
    operands, chunks, start = [], [], 0
    for part in sums:
        chunks.append((start, len(part) == 1))
        start += part[0].shape[2]
        operands += part
    local = pl.BlockSpec(memory_space=pltpu.VMEM)
    return pl.pallas_call(
        functools.partial(finish_kernel, chunks),
        in_specs=[local] * len(operands),
        out_specs=[local] * 2,
        out_shape=[jax.ShapeDtypeStruct(shape, jnp.bfloat16)] * 2,
        compiler_params=pltpu.CompilerParams(vmem_limit_bytes=VMEM),
        cost_estimate=pl.CostEstimate(
            flops=8 * shape[0] * shape[1], bytes_accessed=16 * shape[0] * shape[1], transcendentals=0
        ),
        name="finish",
    )(*operands)


def shards(queries, keys, values, outputs, grad_out, lse_saved, doc_lengths):
    seq = lax.axis_size("seq")
    me = lax.axis_index("seq").astype(jnp.int32)
    side = lax.rem(me, 2)
    keys, values, even, odd = lax.optimization_barrier((keys, values, side == 0, side == 1))
    hops = seq // 4
    def onward(hop):
        return [(s, s + 2) for s in range(2 * hop - 2, seq - 2)]

    def back(hop):
        return [(s, s - 2) for s in range(2 * hop, seq)]

    def to_odd(hop):
        return [(s, s + 1) for s in range(2 * hop, seq, 2)]

    def to_even(hop):
        return [(s + 1, s) for s in range(2 * hop, seq, 2)]

    def send(array, pairs):
        return lax.ppermute(array, "seq", pairs)

    def after(array, *others):
        return lax.optimization_barrier((array,) + others)[0]

    delta = delta_rows(outputs, grad_out)
    lse = lse_saved.T
    heads = [sum(CHUNKS[:chunk]) for chunk in range(len(CHUNKS))]
    columns = []
    for head, per in zip(heads, CHUNKS):
        at = slice(head * HDIM, (head + per) * HDIM)
        own = jnp.stack([keys[:, at], values[:, at]])
        own = lax.optimization_barrier(own)
        columns.append([own, send(own, onward(1))])
        columns[-1][1], delta = lax.optimization_barrier((columns[-1][1], delta))
    for column in columns:
        for hop in range(2, hops + 1):
            column.append(send(column[-1], onward(hop)))
    arrived = []
    for chunk, column in enumerate(columns):
        edge = jnp.where(even, column[0], column[hops])
        moved = [(array, None) for array in column]
        if chunk == 0:
            crossed = [send(array, to_odd(1) + to_even(1)) for array in column[1:hops]]
            crossed.append(send(after(edge, *crossed), to_odd(0) + to_even(hops)))
            moved += [(array, None) for array in crossed]
        else:
            joint = jnp.stack(column[1:hops] + [edge])
            crossed = send(joint, to_odd(0) + to_even(1))
            moved += [(crossed, hop) for hop in range(hops)]
            arrived[0][-1] = (after(arrived[0][-1][0], joint), None)
        arrived.append(moved)

    wide, half = jnp.float32, jnp.bfloat16
    grads_q, sums, outputs_of = [], [], []
    for chunk, (head, per) in enumerate(zip(heads, CHUNKS)):
        joined = chunk < len(CHUNKS) - 1
        grad_q, *parts = attend(
            doc_lengths, queries, grad_out, lse, delta, arrived[chunk], head, per, hops, joined
        )
        grads_q.append(grad_q)
        outputs_of.append((parts[: hops + 1], parts[hops + 1 :], joined))
    swapped = []
    for column, crossed, joined in outputs_of:
        if joined:
            crossed = send(crossed[0], to_odd(1) + to_even(0))
            crossed = after(crossed, outputs_of[-1][1][-1])
            edge = crossed[hops - 1]
        else:
            edge = send(crossed[-1], to_odd(hops) + to_even(0))
            crossed = [
                send(after(crossed[hop - 1], swapped[0][2]), to_odd(hop) + to_even(hop))
                for hop in range(1, hops)
            ]
        edge = edge.astype(wide)
        total = column[hops].astype(wide) + jnp.where(odd, edge, 0.0)
        swapped.append((crossed, edge, total.astype(half)))
    before = []
    for (column, _, joined), (crossed, edge, total) in zip(outputs_of, swapped):
        for hop in range(hops - 1, -1, -1):
            if joined:
                if hop == 0 and hops > 1:
                    total = after(total, *swapped[-1][0])
                before.append(total)
            elif hop == 0:
                total = after(total, *before)
            far = send(total, back(hop + 1)).astype(wide)
            if hop:
                total = column[hop].astype(wide) + crossed[hop - 1].astype(wide) + far
                total = total.astype(half)
        if joined:
            total = column[0].astype(wide) + jnp.where(even, edge, 0.0) + far
            sums.append([total.astype(half)])
        else:
            sums.append([column[0], edge.astype(half), far.astype(half)])
    grads_q[-1] = after(grads_q[-1], edge)
    grad_q = jnp.concatenate(grads_q, axis=1)
    grad_keys, grad_values = finish(sums, keys.shape)
    return (grad_q, grad_keys, grad_values)


def solution(mesh):
    rows = P(("packs", "seq"), None)
    return jax.shard_map(
        shards,
        mesh=mesh,
        in_specs=(rows, rows, rows, rows, rows, rows, P("packs")),
        out_specs=(rows, rows, rows),
        check_vma=False,
    )
```

```python
import functools

import jax
import jax.numpy as jnp
from jax import lax
from jax.experimental import pallas as pl
from jax.experimental.pallas import tpu as pltpu
from jax.sharding import PartitionSpec as P

HEADS = 64
KVH = 8
HDIM = 128
GROUP = HEADS // KVH
CHUNKS = (4, 4)
STEP = 2
LOG2E = 1.4426950408889634
VMEM = 20 * 1024 * 1024


def contract_last(first, second):
    return lax.dot_general(
        first, second, (((1,), (1,)), ((), ())), preferred_element_type=jnp.float32
    )


def contract_first(first, second):
    return lax.dot_general(
        first, second, (((0,), (0,)), ((), ())), preferred_element_type=jnp.float32
    )


def head_rows(block):
    return jnp.concatenate(
        [block[:, h * HDIM : (h + 1) * HDIM] for h in range(GROUP)], axis=0
    )


def delta_kernel(out_ref, gout_ref, delta_ref):
    rows = out_ref.shape[0]
    wide = GROUP * HDIM
    first = lax.broadcasted_iota(jnp.int32, (wide, HDIM), 1) * HDIM
    row = lax.broadcasted_iota(jnp.int32, (wide, HDIM), 0)
    ones = jnp.where((row >= first) & (row < first + HDIM), 1.0, 0.0).astype(jnp.bfloat16)
    for group in range(out_ref.shape[1] // wide):
        at = slice(group * wide, (group + 1) * wide)
        product = out_ref[:, at].astype(jnp.float32) * gout_ref[:, at].astype(jnp.float32)
        high = product.astype(jnp.bfloat16)
        low = (product - high.astype(jnp.float32)).astype(jnp.bfloat16)
        total = jnp.dot(high, ones, preferred_element_type=jnp.float32)
        total += jnp.dot(low, ones, preferred_element_type=jnp.float32)
        delta_ref[group * GROUP : (group + 1) * GROUP, :] = total.T[:GROUP]


def delta_rows(outputs, grad_out):
    rows = outputs.shape[0]
    local = pl.BlockSpec(memory_space=pltpu.VMEM)
    return pl.pallas_call(
        delta_kernel,
        in_specs=[local] * 2,
        out_specs=local,
        out_shape=jax.ShapeDtypeStruct((HEADS, rows), jnp.float32),
        compiler_params=pltpu.CompilerParams(vmem_limit_bytes=VMEM),
        cost_estimate=pl.CostEstimate(
            flops=4 * rows * HEADS * HDIM * HDIM,
            bytes_accessed=4 * rows * HEADS * HDIM,
            transcendentals=0,
        ),
        name="delta",
    )(outputs, grad_out)


def pair_kernel(key_ref, value_ref, pair_ref):
    pair_ref[0] = key_ref[...]
    pair_ref[1] = value_ref[...]


def own_pair(keys, values, place, width):
    rows = keys.shape[0]
    return pl.pallas_call(
        pair_kernel,
        grid=(1,),
        in_specs=[pl.BlockSpec((rows, width), lambda g: (0, place))] * 2,
        out_specs=pl.BlockSpec((2, rows, width), lambda g: (0, 0, 0)),
        out_shape=jax.ShapeDtypeStruct((2, rows, width), keys.dtype),
        compiler_params=pltpu.CompilerParams(vmem_limit_bytes=VMEM),
        cost_estimate=pl.CostEstimate(
            flops=0, bytes_accessed=8 * rows * width, transcendentals=0
        ),
        name="own_pair",
    )(keys, values)


def slot_shards(me, hops):
    side = lax.rem(me, 2)
    found = [me - 2 * hop for hop in range(hops + 1)]
    found += [me - 2 * hop + 1 - 2 * side for hop in range(1, hops)]
    found.append(jnp.where(side == 1, me - 1, me - 2 * hops + 1))
    return found


def attend_kernel(hops, joined, first, places, docs, q_ref, gout_ref, lse_ref, delta_ref, *refs):
    slots = 2 * hops + 1
    moved, refs = refs[:slots], refs[slots:]
    gq_ref, refs = refs[0], refs[1:]
    if joined:
        parts = refs[: hops + 1] + tuple(refs[hops + 1].at[hop] for hop in range(hops))
    else:
        parts = refs[:slots]
    k_all, v_all, bias, prob, score = refs[-5:]
    rows = q_ref.shape[0]
    heads = moved[0].shape[-1] // HDIM
    scale = 1.0 / HDIM**0.5
    me = lax.axis_index("seq")

    token = lax.broadcasted_iota(jnp.int32, (1, rows), 1) + me * rows
    begin = jnp.zeros((1, rows), jnp.int32)
    bound = jnp.int32(0)
    for doc in range(docs.shape[0]):
        bound = bound + docs[doc]
        begin = jnp.where(token >= bound, bound, begin)
    row = lax.broadcasted_iota(jnp.int32, (rows, rows), 0)
    for slot, shard in enumerate(slot_shards(me, hops)):
        key = row + shard * rows
        visible = (key <= token) & (key >= begin)
        bias[slot * rows : (slot + 1) * rows, :] = jnp.where(visible, 0.0, -1e30)

    def one_head(index, k_all, v_all, prob, score):
        column = pl.ds(pl.multiple_of(index * HDIM, HDIM), HDIM)
        wide = pl.ds(pl.multiple_of((first + index) * GROUP * HDIM, GROUP * HDIM), GROUP * HDIM)
        stat = pl.ds(pl.multiple_of((first + index) * GROUP, GROUP), GROUP)
        for slot in range(slots):
            here = slice(slot * rows, (slot + 1) * rows)
            pair = moved[slot] if places[slot] is None else moved[slot].at[places[slot]]
            k_all[here, :] = pair[0, :, column]
            v_all[here, :] = pair[1, :, column]
        queries = head_rows(q_ref[:, wide])
        gout = head_rows(gout_ref[:, wide])
        lses = lse_ref[stat, :]
        deltas = delta_ref[stat, :]
        keys = k_all[...]
        values = v_all[...]
        hidden = bias[...]
        hidden = jnp.concatenate([hidden, hidden], axis=1)
        for two in range(GROUP // 2):
            at = slice(2 * two * rows, (2 * two + 2) * rows)
            lse = jnp.concatenate([lses[2 * two : 2 * two + 1], lses[2 * two + 1 : 2 * two + 2]], axis=1)
            delta = jnp.concatenate(
                [deltas[2 * two : 2 * two + 1], deltas[2 * two + 1 : 2 * two + 2]], axis=1
            )
            raw = contract_last(keys, queries[at])
            attn = jnp.exp2(raw * (scale * LOG2E) - lse * LOG2E + hidden)
            grad = contract_last(values, gout[at])
            prob[:, at] = attn.astype(jnp.bfloat16)
            score[:, at] = (attn * (grad - delta)).astype(jnp.bfloat16)
        scores = score[...]
        grad_k = jnp.dot(scores, queries, preferred_element_type=jnp.float32) * scale
        grad_v = jnp.dot(prob[...], gout, preferred_element_type=jnp.float32)
        for slot in range(slots):
            here = slice(slot * rows, (slot + 1) * rows)
            part = parts[slot]
            part[0, :, column] = grad_k[here].astype(part.dtype)
            part[1, :, column] = grad_v[here].astype(part.dtype)
        grad_q = (contract_first(keys, scores) * scale).astype(jnp.bfloat16)
        mine = pl.ds(pl.multiple_of(index * GROUP * HDIM, GROUP * HDIM), GROUP * HDIM)
        gq_ref[:, mine] = jnp.concatenate(
            [grad_q[:, h * rows : (h + 1) * rows].T for h in range(GROUP)], axis=1
        )

    @pl.loop(0, heads // STEP)
    def _(step):
        for sub in range(STEP):
            one_head(step * STEP + sub, k_all.at[sub], v_all.at[sub], prob.at[sub], score.at[sub])


def attend(docs, queries, grad_out, lse, delta, moved, head, per, hops, joined):
    rows = queries.shape[0]
    slots = 2 * hops + 1
    local = pl.BlockSpec(memory_space=pltpu.VMEM)
    operands = [docs, queries, grad_out, lse, delta] + [array for array, index in moved]
    in_specs = [pl.BlockSpec(memory_space=pltpu.SMEM)] + [local] * (len(operands) - 1)
    out_shape = [jax.ShapeDtypeStruct((rows, per * GROUP * HDIM), jnp.bfloat16)]
    out_shape += [jax.ShapeDtypeStruct((2, rows, per * HDIM), jnp.bfloat16)] * (hops + 1)
    if joined:
        out_shape += [jax.ShapeDtypeStruct((hops, 2, rows, per * HDIM), jnp.bfloat16)]
    else:
        out_shape += [jax.ShapeDtypeStruct((2, rows, per * HDIM), jnp.bfloat16)] * hops
    pairs = slots * rows * rows * GROUP * per
    places = [index for array, index in moved]
    return pl.pallas_call(
        functools.partial(attend_kernel, hops, joined, head, places),
        in_specs=in_specs,
        out_specs=[local] * len(out_shape),
        scratch_shapes=[
            pltpu.VMEM((STEP, slots * rows, HDIM), jnp.bfloat16),
            pltpu.VMEM((STEP, slots * rows, HDIM), jnp.bfloat16),
            pltpu.VMEM((slots * rows, rows), jnp.float32),
            pltpu.VMEM((STEP, slots * rows, GROUP * rows), jnp.bfloat16),
            pltpu.VMEM((STEP, slots * rows, GROUP * rows), jnp.bfloat16),
        ],
        out_shape=out_shape,
        compiler_params=pltpu.CompilerParams(vmem_limit_bytes=VMEM),
        cost_estimate=pl.CostEstimate(
            flops=40 * pairs * HDIM,
            bytes_accessed=per * rows * HDIM * 2 * (3 * GROUP + 6 * slots),
            transcendentals=pairs,
        ),
        name="attend",
    )(*operands)


def finish_kernel(chunks, *refs):
    key_ref, value_ref = refs[-2:]
    refs = refs[:-2]
    keep = jnp.where(lax.rem(lax.axis_index("seq"), 2) == 0, 1.0, 0.0)
    for start, done in chunks:
        if done:
            total, refs = refs[0][...], refs[1:]
        else:
            own, edge, far = (ref[...].astype(jnp.float32) for ref in refs[:3])
            total, refs = (own + edge * keep + far).astype(jnp.bfloat16), refs[3:]
        key_ref[:, start : start + total.shape[2]] = total[0]
        value_ref[:, start : start + total.shape[2]] = total[1]


def finish(sums, shape):
    operands, chunks, start = [], [], 0
    for part in sums:
        chunks.append((start, len(part) == 1))
        start += part[0].shape[2]
        operands += part
    local = pl.BlockSpec(memory_space=pltpu.VMEM)
    return pl.pallas_call(
        functools.partial(finish_kernel, chunks),
        in_specs=[local] * len(operands),
        out_specs=[local] * 2,
        out_shape=[jax.ShapeDtypeStruct(shape, jnp.bfloat16)] * 2,
        compiler_params=pltpu.CompilerParams(vmem_limit_bytes=VMEM),
        cost_estimate=pl.CostEstimate(
            flops=8 * shape[0] * shape[1], bytes_accessed=16 * shape[0] * shape[1], transcendentals=0
        ),
        name="finish",
    )(*operands)


def shards(queries, keys, values, outputs, grad_out, lse_saved, doc_lengths):
    seq = lax.axis_size("seq")
    me = lax.axis_index("seq").astype(jnp.int32)
    side = lax.rem(me, 2)
    keys, values, even, odd = lax.optimization_barrier((keys, values, side == 0, side == 1))
    hops = seq // 4
    def onward(hop):
        return [(s, s + 2) for s in range(2 * hop - 2, seq - 2)]

    def back(hop):
        return [(s, s - 2) for s in range(2 * hop, seq)]

    def to_odd(hop):
        return [(s, s + 1) for s in range(2 * hop, seq, 2)]

    def to_even(hop):
        return [(s + 1, s) for s in range(2 * hop, seq, 2)]

    def send(array, pairs):
        return lax.ppermute(array, "seq", pairs)

    def after(array, *others):
        return lax.optimization_barrier((array,) + others)[0]

    delta = delta_rows(outputs, grad_out)
    lse = lse_saved.T
    heads = [sum(CHUNKS[:chunk]) for chunk in range(len(CHUNKS))]
    columns = []
    for head, per in zip(heads, CHUNKS):
        at = slice(head * HDIM, (head + per) * HDIM)
        if head and head % per == 0:
            own = own_pair(keys, values, head // per, per * HDIM)
        else:
            own = jnp.stack([keys[:, at], values[:, at]])
        own = lax.optimization_barrier(own)
        columns.append([own, send(own, onward(1))])
        columns[-1][1], delta = lax.optimization_barrier((columns[-1][1], delta))
    for column in columns:
        for hop in range(2, hops + 1):
            column.append(send(column[-1], onward(hop)))
    arrived = []
    for chunk, column in enumerate(columns):
        edge = jnp.where(even, column[0], column[hops])
        moved = [(array, None) for array in column]
        if chunk == 0:
            crossed = [send(array, to_odd(1) + to_even(1)) for array in column[1:hops]]
            crossed.append(send(after(edge, *crossed), to_odd(0) + to_even(hops)))
            moved += [(array, None) for array in crossed]
        else:
            joint = jnp.stack(column[1:hops] + [edge])
            crossed = send(joint, to_odd(0) + to_even(1))
            moved += [(crossed, hop) for hop in range(hops)]
            arrived[0][-1] = (after(arrived[0][-1][0], joint), None)
        arrived.append(moved)

    wide, half = jnp.float32, jnp.bfloat16
    grads_q, sums, outputs_of = [], [], []
    for chunk, (head, per) in enumerate(zip(heads, CHUNKS)):
        joined = chunk < len(CHUNKS) - 1
        grad_q, *parts = attend(
            doc_lengths, queries, grad_out, lse, delta, arrived[chunk], head, per, hops, joined
        )
        grads_q.append(grad_q)
        outputs_of.append((parts[: hops + 1], parts[hops + 1 :], joined))
    swapped = []
    for column, crossed, joined in outputs_of:
        if joined:
            crossed = send(crossed[0], to_odd(1) + to_even(0))
            crossed = after(crossed, outputs_of[-1][1][-1])
            edge = crossed[hops - 1]
        else:
            edge = send(crossed[-1], to_odd(hops) + to_even(0))
            crossed = [
                send(after(crossed[hop - 1], swapped[0][2]), to_odd(hop) + to_even(hop))
                for hop in range(1, hops)
            ]
        edge = edge.astype(wide)
        total = column[hops].astype(wide) + jnp.where(odd, edge, 0.0)
        swapped.append((crossed, edge, total.astype(half)))
    before = []
    for (column, _, joined), (crossed, edge, total) in zip(outputs_of, swapped):
        for hop in range(hops - 1, -1, -1):
            if joined:
                if hop == 0 and hops > 1:
                    total = after(total, *swapped[-1][0])
                before.append(total)
            elif hop == 0:
                total = after(total, *before)
            far = send(total, back(hop + 1)).astype(wide)
            if hop:
                total = column[hop].astype(wide) + crossed[hop - 1].astype(wide) + far
                total = total.astype(half)
        if joined:
            total = column[0].astype(wide) + jnp.where(even, edge, 0.0) + far
            sums.append([total.astype(half)])
        else:
            sums.append([column[0], edge.astype(half), far.astype(half)])
    grads_q[-1] = after(grads_q[-1], edge)
    grad_q = jnp.concatenate(grads_q, axis=1)
    grad_keys, grad_values = finish(sums, keys.shape)
    return (grad_q, grad_keys, grad_values)


def solution(mesh):
    rows = P(("packs", "seq"), None)
    return jax.shard_map(
        shards,
        mesh=mesh,
        in_specs=(rows, rows, rows, rows, rows, rows, P("packs")),
        out_specs=(rows, rows, rows),
        check_vma=False,
    )
```

```python
import functools

import jax
import jax.numpy as jnp
from jax import lax
from jax.experimental import pallas as pl
from jax.experimental.pallas import tpu as pltpu
from jax.sharding import PartitionSpec as P

HEADS = 64
KVH = 8
HDIM = 128
GROUP = HEADS // KVH
CHUNKS = (4, 4)
STEP = 4
LOG2E = 1.4426950408889634
VMEM = 24 * 1024 * 1024


def contract_last(first, second):
    return lax.dot_general(
        first, second, (((1,), (1,)), ((), ())), preferred_element_type=jnp.float32
    )


def contract_first(first, second):
    return lax.dot_general(
        first, second, (((0,), (0,)), ((), ())), preferred_element_type=jnp.float32
    )


def head_rows(block):
    return jnp.concatenate(
        [block[:, h * HDIM : (h + 1) * HDIM] for h in range(GROUP)], axis=0
    )


def delta_kernel(out_ref, gout_ref, delta_ref):
    rows = out_ref.shape[0]
    wide = GROUP * HDIM
    first = lax.broadcasted_iota(jnp.int32, (wide, HDIM), 1) * HDIM
    row = lax.broadcasted_iota(jnp.int32, (wide, HDIM), 0)
    ones = jnp.where((row >= first) & (row < first + HDIM), 1.0, 0.0).astype(jnp.bfloat16)
    for group in range(out_ref.shape[1] // wide):
        at = slice(group * wide, (group + 1) * wide)
        product = out_ref[:, at].astype(jnp.float32) * gout_ref[:, at].astype(jnp.float32)
        high = product.astype(jnp.bfloat16)
        low = (product - high.astype(jnp.float32)).astype(jnp.bfloat16)
        total = jnp.dot(high, ones, preferred_element_type=jnp.float32)
        total += jnp.dot(low, ones, preferred_element_type=jnp.float32)
        delta_ref[group * GROUP : (group + 1) * GROUP, :] = total.T[:GROUP]


def delta_rows(outputs, grad_out):
    rows = outputs.shape[0]
    local = pl.BlockSpec(memory_space=pltpu.VMEM)
    return pl.pallas_call(
        delta_kernel,
        in_specs=[local] * 2,
        out_specs=local,
        out_shape=jax.ShapeDtypeStruct((HEADS, rows), jnp.float32),
        compiler_params=pltpu.CompilerParams(vmem_limit_bytes=VMEM),
        cost_estimate=pl.CostEstimate(
            flops=4 * rows * HEADS * HDIM * HDIM,
            bytes_accessed=4 * rows * HEADS * HDIM,
            transcendentals=0,
        ),
        name="delta",
    )(outputs, grad_out)


def slot_shards(me, hops):
    side = lax.rem(me, 2)
    found = [me - 2 * hop for hop in range(hops + 1)]
    found += [me - 2 * hop + 1 - 2 * side for hop in range(1, hops)]
    found.append(jnp.where(side == 1, me - 1, me - 2 * hops + 1))
    return found


def attend_kernel(hops, joined, first, places, docs, q_ref, gout_ref, lse_ref, delta_ref, *refs):
    slots = 2 * hops + 1
    moved, refs = refs[:slots], refs[slots:]
    gq_ref, refs = refs[0], refs[1:]
    if joined:
        parts = refs[: hops + 1] + tuple(refs[hops + 1].at[hop] for hop in range(hops))
    else:
        parts = refs[:slots]
    k_all, v_all, bias, prob, score = refs[-5:]
    rows = q_ref.shape[0]
    heads = moved[0].shape[-1] // HDIM
    scale = 1.0 / HDIM**0.5
    me = lax.axis_index("seq")

    token = lax.broadcasted_iota(jnp.int32, (1, rows), 1) + me * rows
    begin = jnp.zeros((1, rows), jnp.int32)
    bound = jnp.int32(0)
    for doc in range(docs.shape[0]):
        bound = bound + docs[doc]
        begin = jnp.where(token >= bound, bound, begin)
    row = lax.broadcasted_iota(jnp.int32, (rows, rows), 0)
    for slot, shard in enumerate(slot_shards(me, hops)):
        key = row + shard * rows
        visible = (key <= token) & (key >= begin)
        bias[slot * rows : (slot + 1) * rows, :] = jnp.where(visible, 0.0, -1e30)

    def one_head(index, k_all, v_all, prob, score):
        column = pl.ds(pl.multiple_of(index * HDIM, HDIM), HDIM)
        wide = pl.ds(pl.multiple_of((first + index) * GROUP * HDIM, GROUP * HDIM), GROUP * HDIM)
        stat = pl.ds(pl.multiple_of((first + index) * GROUP, GROUP), GROUP)
        for slot in range(slots):
            here = slice(slot * rows, (slot + 1) * rows)
            pair = moved[slot] if places[slot] is None else moved[slot].at[places[slot]]
            k_all[here, :] = pair[0, :, column]
            v_all[here, :] = pair[1, :, column]
        queries = head_rows(q_ref[:, wide])
        gout = head_rows(gout_ref[:, wide])
        lses = lse_ref[stat, :]
        deltas = delta_ref[stat, :]
        keys = k_all[...]
        values = v_all[...]
        hidden = bias[...]
        hidden = jnp.concatenate([hidden, hidden], axis=1)
        for two in range(GROUP // 2):
            at = slice(2 * two * rows, (2 * two + 2) * rows)
            lse = jnp.concatenate([lses[2 * two : 2 * two + 1], lses[2 * two + 1 : 2 * two + 2]], axis=1)
            delta = jnp.concatenate(
                [deltas[2 * two : 2 * two + 1], deltas[2 * two + 1 : 2 * two + 2]], axis=1
            )
            raw = contract_last(keys, queries[at])
            attn = jnp.exp2(raw * (scale * LOG2E) - lse * LOG2E + hidden)
            grad = contract_last(values, gout[at])
            prob[:, at] = attn.astype(jnp.bfloat16)
            score[:, at] = (attn * (grad - delta)).astype(jnp.bfloat16)
        scores = score[...]
        grad_k = jnp.dot(scores, queries, preferred_element_type=jnp.float32) * scale
        grad_v = jnp.dot(prob[...], gout, preferred_element_type=jnp.float32)
        for slot in range(slots):
            here = slice(slot * rows, (slot + 1) * rows)
            part = parts[slot]
            part[0, :, column] = grad_k[here].astype(part.dtype)
            part[1, :, column] = grad_v[here].astype(part.dtype)
        grad_q = (contract_first(keys, scores) * scale).astype(jnp.bfloat16)
        mine = pl.ds(pl.multiple_of(index * GROUP * HDIM, GROUP * HDIM), GROUP * HDIM)
        gq_ref[:, mine] = jnp.concatenate(
            [grad_q[:, h * rows : (h + 1) * rows].T for h in range(GROUP)], axis=1
        )

    @pl.loop(0, heads // STEP)
    def _(step):
        for sub in range(STEP):
            one_head(step * STEP + sub, k_all.at[sub], v_all.at[sub], prob.at[sub], score.at[sub])


def attend(docs, queries, grad_out, lse, delta, moved, head, per, hops, joined):
    rows = queries.shape[0]
    slots = 2 * hops + 1
    local = pl.BlockSpec(memory_space=pltpu.VMEM)
    operands = [docs, queries, grad_out, lse, delta] + [array for array, index in moved]
    in_specs = [pl.BlockSpec(memory_space=pltpu.SMEM)] + [local] * (len(operands) - 1)
    out_shape = [jax.ShapeDtypeStruct((rows, per * GROUP * HDIM), jnp.bfloat16)]
    out_shape += [jax.ShapeDtypeStruct((2, rows, per * HDIM), jnp.bfloat16)] * (hops + 1)
    if joined:
        out_shape += [jax.ShapeDtypeStruct((hops, 2, rows, per * HDIM), jnp.bfloat16)]
    else:
        out_shape += [jax.ShapeDtypeStruct((2, rows, per * HDIM), jnp.bfloat16)] * hops
    pairs = slots * rows * rows * GROUP * per
    places = [index for array, index in moved]
    return pl.pallas_call(
        functools.partial(attend_kernel, hops, joined, head, places),
        in_specs=in_specs,
        out_specs=[local] * len(out_shape),
        scratch_shapes=[
            pltpu.VMEM((STEP, slots * rows, HDIM), jnp.bfloat16),
            pltpu.VMEM((STEP, slots * rows, HDIM), jnp.bfloat16),
            pltpu.VMEM((slots * rows, rows), jnp.float32),
            pltpu.VMEM((STEP, slots * rows, GROUP * rows), jnp.bfloat16),
            pltpu.VMEM((STEP, slots * rows, GROUP * rows), jnp.bfloat16),
        ],
        out_shape=out_shape,
        compiler_params=pltpu.CompilerParams(vmem_limit_bytes=VMEM),
        cost_estimate=pl.CostEstimate(
            flops=40 * pairs * HDIM,
            bytes_accessed=per * rows * HDIM * 2 * (3 * GROUP + 6 * slots),
            transcendentals=pairs,
        ),
        name="attend",
    )(*operands)


def finish_kernel(chunks, *refs):
    key_ref, value_ref = refs[-2:]
    refs = refs[:-2]
    keep = jnp.where(lax.rem(lax.axis_index("seq"), 2) == 0, 1.0, 0.0)
    for start, done in chunks:
        if done:
            total, refs = refs[0][...], refs[1:]
        else:
            own, edge, far = (ref[...].astype(jnp.float32) for ref in refs[:3])
            total, refs = (own + edge * keep + far).astype(jnp.bfloat16), refs[3:]
        key_ref[:, start : start + total.shape[2]] = total[0]
        value_ref[:, start : start + total.shape[2]] = total[1]


def finish(sums, shape):
    operands, chunks, start = [], [], 0
    for part in sums:
        chunks.append((start, len(part) == 1))
        start += part[0].shape[2]
        operands += part
    local = pl.BlockSpec(memory_space=pltpu.VMEM)
    return pl.pallas_call(
        functools.partial(finish_kernel, chunks),
        in_specs=[local] * len(operands),
        out_specs=[local] * 2,
        out_shape=[jax.ShapeDtypeStruct(shape, jnp.bfloat16)] * 2,
        compiler_params=pltpu.CompilerParams(vmem_limit_bytes=VMEM),
        cost_estimate=pl.CostEstimate(
            flops=8 * shape[0] * shape[1], bytes_accessed=16 * shape[0] * shape[1], transcendentals=0
        ),
        name="finish",
    )(*operands)


def shards(queries, keys, values, outputs, grad_out, lse_saved, doc_lengths):
    seq = lax.axis_size("seq")
    me = lax.axis_index("seq").astype(jnp.int32)
    side = lax.rem(me, 2)
    keys, values, even, odd = lax.optimization_barrier((keys, values, side == 0, side == 1))
    hops = seq // 4
    def onward(hop):
        return [(s, s + 2) for s in range(2 * hop - 2, seq - 2)]

    def back(hop):
        return [(s, s - 2) for s in range(2 * hop, seq)]

    def to_odd(hop):
        return [(s, s + 1) for s in range(2 * hop, seq, 2)]

    def to_even(hop):
        return [(s + 1, s) for s in range(2 * hop, seq, 2)]

    def send(array, pairs):
        return lax.ppermute(array, "seq", pairs)

    def after(array, *others):
        return lax.optimization_barrier((array,) + others)[0]

    delta = delta_rows(outputs, grad_out)
    lse = lse_saved.T
    heads = [sum(CHUNKS[:chunk]) for chunk in range(len(CHUNKS))]
    columns = []
    for head, per in zip(heads, CHUNKS):
        at = slice(head * HDIM, (head + per) * HDIM)
        own = jnp.stack([keys[:, at], values[:, at]])
        own = lax.optimization_barrier(own)
        columns.append([own, send(own, onward(1))])
        columns[-1][1], delta = lax.optimization_barrier((columns[-1][1], delta))
    for column in columns:
        for hop in range(2, hops + 1):
            column.append(send(column[-1], onward(hop)))
    arrived = []
    for chunk, column in enumerate(columns):
        edge = jnp.where(even, column[0], column[hops])
        moved = [(array, None) for array in column]
        if chunk == 0:
            crossed = [send(array, to_odd(1) + to_even(1)) for array in column[1:hops]]
            crossed.append(send(after(edge, *crossed), to_odd(0) + to_even(hops)))
            moved += [(array, None) for array in crossed]
        else:
            joint = jnp.stack(column[1:hops] + [edge])
            crossed = send(joint, to_odd(0) + to_even(1))
            moved += [(crossed, hop) for hop in range(hops)]
            arrived[0][-1] = (after(arrived[0][-1][0], joint), None)
        arrived.append(moved)

    wide, half = jnp.float32, jnp.bfloat16
    grads_q, sums, outputs_of = [], [], []
    for chunk, (head, per) in enumerate(zip(heads, CHUNKS)):
        joined = chunk < len(CHUNKS) - 1
        grad_q, *parts = attend(
            doc_lengths, queries, grad_out, lse, delta, arrived[chunk], head, per, hops, joined
        )
        grads_q.append(grad_q)
        outputs_of.append((parts[: hops + 1], parts[hops + 1 :], joined))
    swapped = []
    for column, crossed, joined in outputs_of:
        if joined:
            crossed = send(crossed[0], to_odd(1) + to_even(0))
            crossed = after(crossed, outputs_of[-1][1][-1])
            edge = crossed[hops - 1]
        else:
            edge = send(crossed[-1], to_odd(hops) + to_even(0))
            crossed = [
                send(after(crossed[hop - 1], swapped[0][2]), to_odd(hop) + to_even(hop))
                for hop in range(1, hops)
            ]
        edge = edge.astype(wide)
        total = column[hops].astype(wide) + jnp.where(odd, edge, 0.0)
        swapped.append((crossed, edge, total.astype(half)))
    before = []
    for (column, _, joined), (crossed, edge, total) in zip(outputs_of, swapped):
        for hop in range(hops - 1, -1, -1):
            if joined:
                if hop == 0 and hops > 1:
                    total = after(total, *swapped[-1][0])
                before.append(total)
            elif hop == 0:
                total = after(total, *before)
            far = send(total, back(hop + 1)).astype(wide)
            if hop:
                total = column[hop].astype(wide) + crossed[hop - 1].astype(wide) + far
                total = total.astype(half)
        if joined:
            total = column[0].astype(wide) + jnp.where(even, edge, 0.0) + far
            sums.append([total.astype(half)])
        else:
            sums.append([column[0], edge.astype(half), far.astype(half)])
    grads_q[-1] = after(grads_q[-1], edge)
    grad_q = jnp.concatenate(grads_q, axis=1)
    grad_keys, grad_values = finish(sums, keys.shape)
    return (grad_q, grad_keys, grad_values)


def solution(mesh):
    rows = P(("packs", "seq"), None)
    return jax.shard_map(
        shards,
        mesh=mesh,
        in_specs=(rows, rows, rows, rows, rows, rows, P("packs")),
        out_specs=(rows, rows, rows),
        check_vma=False,
    )
```
